128 devices in a mesh: dp: 32 (over z, x, core), rep: 4 (over y).
Axes of the slice: x: 4, y: 4, z: 4, core: 2. Of those that a mesh axis runs over, the one named last changes fastest.
Arguments:
- features: bfloat16 [65536, 2048], P(('dp', 'rep'))
- head_weight: bfloat16 [2048, 512], replicated
- slot_of_image: int32 [65536], P(('dp', 'rep')), may hold values from 0 to 65535, as said below
- candidates: int32 [512, 8], replicated, may hold values from 0 to 511, as said below
- positives: int32 [65536], P('dp'), may hold values from 0 to 1023
Outputs:
- anchor_row_loss: float32 [65536], P('dp')
- weight_grad: float32 [2048, 512], P(('dp', 'rep'))
The draws below stay inside these ranges and needn't reach their ends.
Inputs may be any that keep to these rules, and one draw needn't show every extreme that they name: `slot_of_image`: every block row holds exactly one image. The images of one device go to the owners (dp index slot // 2048) as 32 images to each of a quarter of the owners, 16 to each of another quarter and 8 to each of the rest. `candidates`: in the rows of one owner's 16 blocks and one group of 2 consecutive columns (group r is columns r * 2 to r * 2 + 1), the blocks of every owner (block // 16) are named exactly 1 times. Repeats may occur.
All inputs are finite; a program needn't handle non-finite values.
Results may differ from the reference program's by a relative error of at most 0.0035.
Values may be sent and summed in bfloat16 or wider, within the bound.
No kernel may reach another device: no remote copies, remote signals or barrier semaphores. Data moves between devices by JAX's collectives and lax.ppermute only.
A program may use at most 64 MiB of HBM per device.

```python
import math
import jax
import jax.numpy as jnp
from jax import lax

F = 2048
E = 512
BR = 128
PAIRS_REP = 2
BLK_DEV = 16
IMG_DEV = 512
BLOCKS = 512
SLOTS = 65536
PICTURES_OVERALL = 65536
PAIRS = 8
N_REP = 4


def draw_features(key, part):
    key = jax.random.fold_in(key, 11)
    device_count = PICTURES_OVERALL // IMG_DEV
    block_width = F // device_count
    split_keys = jax.random.split(key, 5)
    noise_part = jax.random.normal(split_keys[0], (PICTURES_OVERALL, F), jnp.float32)
    directions = jax.random.normal(split_keys[1], (8, F), jnp.float32)
    loadings = 0.35 * jax.random.normal(split_keys[2], (PICTURES_OVERALL, 8), jnp.float32)
    values = noise_part
    for member in range(8):
        values = values + loadings[:, member:member + 1] * directions[member][None, :]
    row_scale = jnp.exp(jax.random.uniform(split_keys[3], (PICTURES_OVERALL, 1), jnp.float32, math.log(0.5), math.log(5.0)))
    pairing = jax.random.permutation(split_keys[4], device_count)
    row_device = jnp.arange(PICTURES_OVERALL, dtype=jnp.int32) // IMG_DEV
    column_block = jnp.arange(F, dtype=jnp.int32) // block_width
    spike_gain = jnp.where(pairing[row_device][:, None] == column_block[None, :], 6.0, 1.0)
    return (values * row_scale * spike_gain).astype(jnp.bfloat16)


def draw_head_weight(key, part):
    key = jax.random.fold_in(key, 23)
    first_key, second_key = jax.random.split(key)
    matrix = jax.random.normal(first_key, (F, E), jnp.float32)
    column_scale = jnp.exp(jax.random.uniform(second_key, (1, E), jnp.float32, math.log(0.3), math.log(3.0)))
    return (matrix * column_scale / math.sqrt(F)).astype(jnp.bfloat16)


def draw_slot_of_image(key, part):
    key = jax.random.fold_in(key, 37)
    dp_count = BLOCKS // BLK_DEV
    device_count = PICTURES_OVERALL // IMG_DEV
    slot_number_count = BLK_DEV * BR
    mean_count = IMG_DEV // dp_count
    levels = jnp.concatenate([jnp.full((dp_count // 4,), 2 * mean_count, jnp.int32), jnp.full((dp_count // 4,), mean_count, jnp.int32), jnp.full((dp_count - dp_count // 2,), mean_count // 2, jnp.int32)])
    first_key, second_key, third_key, fourth_key = jax.random.split(key, 4)
    owner_shift = jax.random.permutation(first_key, dp_count)
    sender_shift = jax.random.permutation(second_key, device_count) % dp_count
    counts = levels[(owner_shift[None, :] + sender_shift[:, None]) % dp_count]
    bucket_end = jnp.cumsum(counts, axis=1)
    bucket_start = bucket_end - counts
    offsets = jnp.cumsum(counts, axis=0) - counts
    position = jnp.arange(IMG_DEV, dtype=jnp.int32)
    target = jnp.sum((position[None, :, None] >= bucket_end[:, None, :]).astype(jnp.int32), axis=2)
    start_of = jnp.take_along_axis(bucket_start, target, axis=1)
    offset_of = jnp.take_along_axis(offsets, target, axis=1)
    local_slot = offset_of + position[None, :] - start_of
    owner_perm = jax.vmap(lambda single: jax.random.permutation(single, slot_number_count))(jax.random.split(third_key, dp_count))
    shuffled = owner_perm[target, local_slot]
    slot_value = target * slot_number_count + shuffled
    image_perm = jax.vmap(lambda single: jax.random.permutation(single, IMG_DEV))(jax.random.split(fourth_key, device_count))
    image_index = jnp.arange(device_count, dtype=jnp.int32)[:, None] * IMG_DEV + image_perm
    result = jnp.zeros((PICTURES_OVERALL,), jnp.int32).at[image_index.reshape(-1)].set(slot_value.reshape(-1).astype(jnp.int32))
    return result


def draw_candidates(key, part):
    key = jax.random.fold_in(key, 41)
    dp_count = BLOCKS // BLK_DEV
    rep_count = PAIRS // PAIRS_REP
    entries = BLK_DEV * PAIRS_REP
    first_key, second_key = jax.random.split(key)
    orders = jax.vmap(lambda single: jax.random.permutation(single, entries))(jax.random.split(first_key, dp_count * rep_count))
    target = orders % dp_count
    local_block = jax.random.randint(second_key, (dp_count * rep_count, entries), 0, BLK_DEV)
    picked = (target * BLK_DEV + local_block).reshape(dp_count, rep_count, BLK_DEV, PAIRS_REP)
    return jnp.transpose(picked, (0, 2, 1, 3)).reshape(BLOCKS, PAIRS).astype(jnp.int32)


def with_ends(values, stream_key, low, top_value):
    extent = values.shape
    place = [jax.random.randint(jax.random.fold_in(stream_key, axis), (), 0, extent[axis]) for axis in range(len(extent))]
    values = values.at[tuple(place)].set(low)
    longest = extent.index(max(extent))
    place[longest] = (place[longest] + 1) % extent[longest]
    return values.at[tuple(place)].set(top_value)


def setup_inputs(seed: int = 0) -> dict:
    key_of = jax.random.split(jax.random.key(seed), 6)
    features = draw_features(jax.random.fold_in(key_of[5], 71), 0)
    head_weight = draw_head_weight(jax.random.fold_in(key_of[5], 71), 0)
    slot_of_image = draw_slot_of_image(jax.random.fold_in(key_of[5], 71), 0)
    candidates = draw_candidates(jax.random.fold_in(key_of[5], 71), 0)
    positives = with_ends(jax.random.randint(key_of[4], (SLOTS,), 0, PAIRS * BR), jax.random.fold_in(key_of[4], 1), 0, (PAIRS * BR) - 1).astype(jnp.int32)
    return dict(features=features, head_weight=head_weight, slot_of_image=slot_of_image, candidates=candidates, positives=positives)


logit_sharpness = 0.05
objective_factor = 32.0
norm_eps = 1e-06

def reference(features, head_weight, slot_of_image, candidates, positives):
    projected = jnp.dot(features, head_weight, preferred_element_type=jnp.float32)
    row_norms = jnp.sqrt(lax.optimization_barrier(jnp.sum(projected * projected, axis=1, keepdims=True)) + norm_eps)
    unit_rows = projected / row_norms
    descriptor = unit_rows.astype(jnp.bfloat16)
    anchors = jnp.zeros((SLOTS, E), jnp.bfloat16).at[slot_of_image].set(descriptor)
    anchor_blocks = anchors.reshape(BLOCKS, BR, E)
    derivative_factor = objective_factor / (logit_sharpness * math.sqrt(PICTURES_OVERALL))
    share_width = PAIRS_REP * BR
    column_ids = jnp.arange(PAIRS * BR, dtype=jnp.int32)

    def block_terms(inputs_block):
        query_entry, chosen, positive_index = inputs_block
        companion_entries = anchor_blocks[chosen].reshape(PAIRS * BR, E)
        cosine_logits = jnp.dot(query_entry, companion_entries.T, preferred_element_type=jnp.float32) / logit_sharpness
        linear_head_matrix = jnp.exp(cosine_logits - 1.0 / logit_sharpness)
        normalizer_sum = lax.optimization_barrier(jnp.sum(linear_head_matrix, axis=1))
        is_positive = column_ids[None, :] == positive_index[:, None]
        matching_logit = lax.optimization_barrier(jnp.sum(jnp.where(is_positive, cosine_logits, 0.0), axis=1))
        tile_objective = jnp.log(normalizer_sum) + 1.0 / logit_sharpness - matching_logit
        coefficient = (linear_head_matrix / normalizer_sum[:, None] - is_positive.astype(jnp.float32)).astype(jnp.bfloat16)
        block_grad = jnp.zeros((BR, E), jnp.float32)
        for rep_share in range(N_REP):
            first_col = rep_share * share_width
            share_sum = jnp.dot(coefficient[:, first_col:first_col + share_width], companion_entries[first_col:first_col + share_width], preferred_element_type=jnp.float32)
            rounded = lax.optimization_barrier((share_sum * derivative_factor).astype(jnp.bfloat16))
            block_grad = block_grad + rounded.astype(jnp.float32)
        return (tile_objective, block_grad)
    losses, block_grads = lax.map(block_terms, (anchor_blocks, candidates, positives.reshape(BLOCKS, BR)))
    slot_grad = block_grads.reshape(SLOTS, E)
    unit_grad = slot_grad[slot_of_image]
    radial = lax.optimization_barrier(jnp.sum(unit_rows * unit_grad, axis=1, keepdims=True))
    grad_projected = ((unit_grad - unit_rows * radial) / row_norms).astype(jnp.bfloat16)
    weight_grad = jnp.dot(features.T, grad_projected, preferred_element_type=jnp.float32)
    return (losses.reshape(SLOTS), weight_grad)
```

```python
import math

import jax
import jax.numpy as jnp
from jax import lax
from jax.experimental import pallas as pl
from jax.experimental.pallas import tpu as pltpu
from jax.sharding import PartitionSpec as P

BR = 128
PAIRS_REP = 2
REPS = 4

logit_sharpness = 0.05
objective_factor = 32.0
norm_eps = 1e-06

BF = jnp.bfloat16
F32 = jnp.float32
I32 = jnp.int32
VMEM_BYTES = 56 * 1024 * 1024


def params():
    return pltpu.CompilerParams(vmem_limit_bytes=VMEM_BYTES)


def iota(shape, dim):
    return lax.broadcasted_iota(I32, shape, dim)


def hot(mask):
    return jnp.where(mask, 1.0, 0.0).astype(BF)


def dot(a, b, ca=1, cb=0):
    return lax.dot_general(a, b, (((ca,), (cb,)), ((), ())), preferred_element_type=F32)


def sds(shape, dtype):
    return jax.ShapeDtypeStruct(shape, dtype)


def project_kernel(owner_slots, owners, cap, slot, feat, head, send, unit, norm, place):
    n = feat.shape[0]
    e = head.shape[1]
    projected = dot(feat[...], head[...])
    length = jnp.sqrt(jnp.sum(projected * projected, axis=1, keepdims=True) + norm_eps)
    rows = projected / length
    unit[...] = rows
    norm[...] = jnp.broadcast_to(length, norm.shape)
    descriptor = rows.astype(BF)
    s = slot[...]
    owner = s // owner_slots
    local = s - owner * owner_slots
    mine = iota((owners, n), 0) == owner
    before = dot(hot(mine), hot(iota((n, n), 0) < iota((n, n), 1)))
    rank = jnp.sum(jnp.where(mine, before, 0.0), axis=0, keepdims=True).astype(I32)
    p = (owner * REPS + (rank & (REPS - 1))) * cap + rank // REPS
    place[...] = jnp.broadcast_to(p.astype(F32), place.shape)
    count = send.shape[0]
    scatter = hot(iota((count, n), 0) == p)
    send[:, :e] = dot(scatter, descriptor).astype(BF)
    high = local // BR
    low = local - high * BR
    row = iota((BR, n), 0)
    tags = jnp.where(row == 0, high, jnp.where(row == 1, low, jnp.where(row == 2, 1, 0)))
    send[:, e:] = dot(scatter, tags.astype(F32).astype(BF), 1, 1).astype(BF)


def compact_kernel(got, packed, place):
    count = got.shape[0]
    e = packed.shape[1]
    rows = packed.shape[0] - 16
    tags = got[:, e:].astype(F32).T
    valid = tags[2:3, :]
    upper = hot(iota((count, count), 0) < iota((count, count), 1))
    before = dot(jnp.broadcast_to(valid, (16, count)).astype(BF), upper)[0:1, :]
    pos = jnp.where(valid > 0.5, before, -1.0)
    place[...] = jnp.broadcast_to(pos, place.shape)
    pick = hot(iota((rows, count), 0) == pos.astype(I32))
    packed[:rows, :] = dot(pick, got[:, :e]).astype(BF)
    packed[rows:, :] = dot(tags[:16, :].astype(BF), pick, 1, 1).astype(BF)


def anchors_kernel(serve, own, left, right, far_a, far_b, anchors, served, slots, sems):
    rows = own.shape[0] - 16
    half = rows // 2

    def slot_row(ref, base):
        tag = ref[base : base + 16, :].astype(F32)
        return (tag[0:1, :] * BR + tag[1:2, :]).astype(I32)

    ids = (
        slot_row(own, rows),
        slot_row(left, rows),
        slot_row(right, rows),
        slot_row(far_b, half),
    )
    for k in range(4):
        slots[k, :, :] = jnp.broadcast_to(ids[k].astype(F32), slots.shape[1:])
    step = 256

    def body(i, carry):
        base = pl.multiple_of(i * step, step)
        at = iota((step, rows), 0) + base
        total = dot(hot(at == ids[0]), own[:rows, :])
        total += dot(hot(at == ids[1]), left[:rows, :])
        total += dot(hot(at == ids[2]), right[:rows, :])
        far = hot(at == ids[3])
        total += dot(far[:, :half], far_a[...])
        total += dot(far[:, half:], far_b[:half, :])
        anchors[pl.ds(base, step), :] = total.astype(BF)
        return carry

    lax.fori_loop(0, anchors.shape[0] // step, body, 0)
    copies = []
    for d in range(served.shape[0]):
        start = pl.multiple_of(serve[d] * BR, BR)
        copies.append(
            pltpu.make_async_copy(anchors.at[pl.ds(start, BR), :], served.at[d], sems.at[d])
        )
    for c in copies:
        c.start()
    for c in copies:
        c.wait()


def scores_kernel(need, column, anchors, fetched, weights, stats):
    blocks = weights.shape[0]

    def body(i, carry):
        for j in range(4):
            b = i * 4 + j
            q = anchors[pl.ds(pl.multiple_of(b * BR, BR), BR), :]
            total = jnp.zeros((1, BR), F32)
            positive = jnp.zeros((1, BR), F32)
            want = column[pl.ds(b, 1), :]
            for k in range(PAIRS_REP):
                logits = dot(fetched[need[b * PAIRS_REP + k]], q, 1, 1) / logit_sharpness
                w = jnp.exp(logits - 1.0 / logit_sharpness)
                weights[b, k * BR : (k + 1) * BR, :] = w
                total += jnp.sum(w, axis=0, keepdims=True)
                hit = iota((BR, BR), 0) + k * BR == want
                positive += jnp.sum(jnp.where(hit, logits, 0.0), axis=0, keepdims=True)
            stats[pl.ds(b, 1), :] = total
            stats[pl.ds(blocks + b, 1), :] = positive
        return carry

    lax.fori_loop(0, blocks // 4, body, 0)


def grads_kernel(factor, need, column, stats, weights, fetched, slots, y0, y1, y2, y3, share):
    blocks = weights.shape[0]

    def body(i, carry):
        for j in range(4):
            b = i * 4 + j
            want = column[pl.ds(b, 1), :]
            total = stats[pl.ds(b, 1), :]
            grad = jnp.zeros((BR, share.shape[1]), F32)
            for k in range(PAIRS_REP):
                hit = iota((BR, BR), 0) + k * BR == want
                c = weights[b, k * BR : (k + 1) * BR, :] / total - jnp.where(hit, 1.0, 0.0)
                grad += dot(c.astype(BF).T, fetched[need[b * PAIRS_REP + k]])
            share[pl.ds(pl.multiple_of(b * BR, BR), BR), :] = (grad * factor).astype(BF)
        return carry

    lax.fori_loop(0, blocks // 4, body, 0)
    step = 256
    total_slots = share.shape[0]
    for k, out in enumerate((y0, y1, y2, y3)):
        ids = slots[k, :, :].T[:, 0:1].astype(I32)
        for h in range(out.shape[0] // step):
            pick = hot(iota((step, total_slots), 1) == ids[h * step : (h + 1) * step, :])
            out[h * step : (h + 1) * step, :] = dot(pick, share[...]).astype(BF)


def back_kernel(a, b, c, d, place, back):
    total = a[...].astype(F32) + b[...].astype(F32) + c[...].astype(F32) + d[...].astype(F32)
    rows = a.shape[0]
    pos = place[...].T[:, 0:1].astype(I32)
    back[...] = dot(hot(iota((back.shape[0], rows), 1) == pos), total.astype(BF)).astype(BF)


def head_grad_kernel(returned, place, unit, norm, feat, out):
    n = unit.shape[0]
    pos = place[...].T[:, 0:1].astype(I32)
    grad = dot(hot(iota((n, returned.shape[0]), 1) == pos), returned[...])
    rows = unit[...]
    radial = jnp.sum(rows * grad, axis=1, keepdims=True)
    g = ((grad - rows * radial) / norm[:, 0:1]).astype(BF)
    step = 512
    for i in range(feat.shape[1] // step):
        out[i * step : (i + 1) * step, :] = dot(feat[:, i * step : (i + 1) * step], g, 0, 0).astype(BF)


def sum_kernel(parts, out):
    out[...] = jnp.sum(parts[...].astype(F32), axis=0)


def turn(x, k):
    return lax.ppermute(x, "rep", [(i, (i + k) % REPS) for i in range(REPS)])


def shards(features, head_weight, slot_of_image, candidates, positives):
    dp = lax.axis_size("dp")
    me = lax.axis_index("dp")
    rep = lax.axis_index("rep")
    n, width = features.shape
    e = head_weight.shape[1]
    devices = dp * REPS
    owner_slots = n * REPS
    blocks = owner_slots // BR
    cap = 2 * n // devices
    count = devices * cap
    factor = objective_factor / (logit_sharpness * math.sqrt(n * devices))
    both = ("dp", "rep")
    vmem = pl.BlockSpec(memory_space=pltpu.VMEM)
    smem = pl.BlockSpec(memory_space=pltpu.SMEM)

    send, unit, norm, place = pl.pallas_call(
        lambda *r: project_kernel(owner_slots, dp, cap, *r),
        out_shape=(
            sds((count, e + BR), BF),
            sds((n, e), F32),
            sds((n, BR), F32),
            sds((BR, n), F32),
        ),
        compiler_params=params(),
        name="project",
    )(slot_of_image.reshape(1, n), features, head_weight)

    got = lax.all_to_all(send.reshape(devices, cap, e + BR), both, 0, 0, tiled=True)
    packed, back_place = pl.pallas_call(
        compact_kernel,
        out_shape=(sds((n + 16, e), BF), sds((BR, count), F32)),
        compiler_params=params(),
        name="compact",
    )(got.reshape(count, e + BR))

    left, right = turn(packed, 1), turn(packed, 3)
    half = n // 2
    far_a, far_b = turn(left[:half], 1), turn(right[half:], 3)

    table = candidates.reshape(dp, blocks, REPS, PAIRS_REP)
    table = lax.dynamic_index_in_dim(table, rep, axis=2, keepdims=False)
    table = table.reshape(dp, blocks * PAIRS_REP)
    owner = table // blocks
    serve = jnp.sum(jnp.where(owner == me, table - owner * blocks, 0), axis=1)
    need = lax.dynamic_index_in_dim(owner, me, axis=0, keepdims=False)
    column = positives.reshape(blocks, BR) - rep * (PAIRS_REP * BR)

    anchors, served, slots = pl.pallas_call(
        anchors_kernel,
        out_shape=(
            sds((owner_slots, e), BF),
            sds((dp, BR, e), BF),
            sds((4, BR, n), F32),
        ),
        in_specs=[smem] + [vmem] * 5,
        out_specs=(vmem, pl.BlockSpec(memory_space=pl.ANY), vmem),
        scratch_shapes=[pltpu.SemaphoreType.DMA((dp,))],
        compiler_params=params(),
        name="anchors",
    )(serve, packed, left, right, far_a, far_b)

    fetched = lax.all_to_all(served, "dp", 0, 0, tiled=True)

    weights, stats = pl.pallas_call(
        scores_kernel,
        out_shape=(sds((blocks, PAIRS_REP * BR, BR), F32), sds((2 * blocks, BR), F32)),
        in_specs=[smem] + [vmem] * 3,
        compiler_params=params(),
        name="scores",
    )(need, column, anchors, fetched)
    stats = lax.psum(stats, "rep")
    total, matching = stats[:blocks], stats[blocks:]
    anchor_row_loss = (jnp.log(total) + 1.0 / logit_sharpness - matching).reshape(owner_slots)

    y = pl.pallas_call(
        lambda *r: grads_kernel(factor, *r),
        out_shape=(sds((n, e), BF),) * 4,
        in_specs=[smem] + [vmem] * 5,
        scratch_shapes=[pltpu.VMEM((owner_slots, e), BF)],
        compiler_params=params(),
        name="grads",
    )(need, column, stats, weights, fetched, slots)
    shares = (y[0], turn(y[1], 3), turn(y[2], 1), turn(y[3], 2))
    back = pl.pallas_call(
        back_kernel,
        out_shape=sds((count, e), BF),
        compiler_params=params(),
        name="back",
    )(*shares, back_place)
    returned = lax.all_to_all(back.reshape(devices, cap, e), both, 0, 0, tiled=True)
    partial = pl.pallas_call(
        head_grad_kernel,
        out_shape=sds((width, e), BF),
        compiler_params=params(),
        name="head_grad",
    )(returned.reshape(count, e), place, unit, norm, features)
    parts = lax.all_to_all(partial.reshape(devices, width // devices, e), both, 0, 0, tiled=True)
    weight_grad = pl.pallas_call(
        sum_kernel,
        out_shape=sds((width // devices, e), F32),
        compiler_params=params(),
        name="add",
    )(parts)
    return (anchor_row_loss, weight_grad)


def solution(mesh):
    placed = (P(("dp", "rep"), None), P(), P(("dp", "rep")), P(), P("dp"))
    return jax.shard_map(
        shards,
        mesh=mesh,
        in_specs=placed,
        out_specs=(P("dp"), P(("dp", "rep"), None)),
        check_vma=False,
    )
```

```python
import math

import jax
import jax.numpy as jnp
from jax import lax
from jax.experimental import pallas as pl
from jax.experimental.pallas import tpu as pltpu
from jax.sharding import PartitionSpec as P

BR = 128
PAIRS_REP = 2
REPS = 4

logit_sharpness = 0.05
objective_factor = 32.0
norm_eps = 1e-06

BF = jnp.bfloat16
F32 = jnp.float32
I32 = jnp.int32
VMEM_BYTES = 56 * 1024 * 1024


def params():
    return pltpu.CompilerParams(vmem_limit_bytes=VMEM_BYTES)


def iota(shape, dim):
    return lax.broadcasted_iota(I32, shape, dim)


def hot(mask):
    return jnp.where(mask, 1.0, 0.0).astype(BF)


def dot(a, b, ca=1, cb=0):
    return lax.dot_general(a, b, (((ca,), (cb,)), ((), ())), preferred_element_type=F32)


def sds(shape, dtype):
    return jax.ShapeDtypeStruct(shape, dtype)


def column_of(rows):
    wide = jnp.concatenate([rows] * (BR // rows.shape[0]), axis=0)
    return wide.T[:, 0:1].astype(I32)


def project_kernel(owner_slots, owners, cap, slot, feat, head, send0, send1, unit, norm, place):
    n = feat.shape[0]
    h = head.shape[1] // 2
    projected = dot(feat[...], head[...])
    length = jnp.sqrt(jnp.sum(projected * projected, axis=1, keepdims=True) + norm_eps)
    rows = projected / length
    unit[...] = rows
    norm[...] = jnp.broadcast_to(length, norm.shape)
    descriptor = rows.astype(BF)
    s = slot[...]
    owner = s // owner_slots
    local = s - owner * owner_slots
    mine = iota((owners, n), 0) == owner
    before = dot(hot(mine), hot(iota((n, n), 0) < iota((n, n), 1)))
    rank = jnp.sum(jnp.where(mine, before, 0.0), axis=0, keepdims=True).astype(I32)
    p = (owner * REPS + (rank & (REPS - 1))) * cap + rank // REPS
    place[...] = jnp.broadcast_to(p.astype(F32), place.shape)
    scatter = hot(iota((send0.shape[0], n), 0) == p)
    send0[:, :h] = dot(scatter, descriptor[:, :h]).astype(BF)
    send1[...] = dot(scatter, descriptor[:, h:]).astype(BF)
    high = local // BR
    low = local - high * BR
    row = iota((BR, n), 0)
    tags = jnp.where(row == 0, high, jnp.where(row == 1, low, jnp.where(row == 2, 1, 0)))
    send0[:, h:] = dot(scatter, tags.astype(F32).astype(BF), 1, 1).astype(BF)


def stripes_kernel(core, feat, mine, other):
    n = feat.shape[0]
    first = core[0] == 0
    half = BR // 2
    for z in range(feat.shape[1] // BR):
        t = feat[:, z * BR : (z + 1) * BR].astype(F32).T
        a, b = t[:half, :], t[half:, :]
        mine[z * half : (z + 1) * half, :] = jnp.where(first, a, b).astype(BF)
        other[z * half : (z + 1) * half, :] = jnp.where(first, b, a).astype(BF)


def compact0_kernel(got, packed, place):
    count = got.shape[0]
    h = packed.shape[1]
    rows = packed.shape[0] - 32
    tags = got[:, h:].astype(F32).T
    valid = tags[2:3, :]
    upper = hot(iota((count, count), 0) < iota((count, count), 1))
    before = dot(jnp.broadcast_to(valid, (16, count)).astype(BF), upper)[0:1, :]
    pos = jnp.where(valid > 0.5, before, -1.0)
    place[...] = jnp.broadcast_to(pos, place.shape)
    pick = hot(iota((rows, count), 0) == pos.astype(I32))
    packed[:rows, :] = dot(pick, got[:, :h]).astype(BF)
    tag = dot(tags[:16, :].astype(BF), pick, 1, 1).astype(BF)
    packed[rows : rows + 16, :] = tag[:, :h]
    packed[rows + 16 :, :] = tag[:, h:]


def compact1_kernel(got, place, packed):
    rows, count = packed.shape[0], got.shape[0]
    pick = hot(iota((rows, count), 0) == place[0:1, :].astype(I32))
    packed[...] = dot(pick, got[...]).astype(BF)


def near0_kernel(own, left, right, partial, slots):
    n = own.shape[0] - 32
    ids = []
    for k, ref in enumerate((own, left, right)):
        tag = ref[n:, :].astype(F32)
        row = jnp.concatenate(
            [tag[0:1, :] * BR + tag[1:2, :], tag[16:17, :] * BR + tag[17:18, :]], axis=1
        )
        slots[k, :, :] = jnp.broadcast_to(row, slots.shape[1:])
        ids.append(row.astype(I32))
    place_rows(partial, [(ids[k], ref[:n, :]) for k, ref in enumerate((own, left, right))], None)


def near1_kernel(own, left, right, slots, partial):
    ids = [slots[k, 0:1, :].astype(I32) for k in range(3)]
    place_rows(partial, [(ids[k], ref[...]) for k, ref in enumerate((own, left, right))], None)


def place_rows(out, pieces, start):
    step = 256

    def body(i, carry):
        base = pl.multiple_of(i * step, step)
        total = None if start is None else start[pl.ds(base, step), :].astype(F32)
        for ids, rows in pieces:
            at = iota((step, rows.shape[0]), 0) + base
            part = dot(hot(at == ids), rows)
            total = part if total is None else total + part
        out[pl.ds(base, step), :] = total.astype(BF)
        return carry

    lax.fori_loop(0, out.shape[0] // step, body, 0)


def serve_blocks(serve, anchors, served, sems):
    copies = []
    for d in range(served.shape[0]):
        start = pl.multiple_of(serve[d] * BR, BR)
        copies.append(
            pltpu.make_async_copy(anchors.at[pl.ds(start, BR), :], served.at[d], sems.at[d])
        )
    for c in copies:
        c.start()
    for c in copies:
        c.wait()


def far0_kernel(serve, partial, far_a, far_b, anchors, served, slots, sems):
    q = far_a.shape[0]
    tag = far_b[q:, :].astype(F32)
    row = jnp.concatenate(
        [tag[0:1, :] * BR + tag[1:2, :], tag[16:17, :] * BR + tag[17:18, :]], axis=1
    )
    slots[...] = jnp.broadcast_to(row, slots.shape)
    ids = row.astype(I32)
    place_rows(anchors, [(ids[:, :q], far_a[...]), (ids[:, q:], far_b[:q, :])], partial)
    serve_blocks(serve, anchors, served, sems)


def far1_kernel(serve, partial, far_a, far_b, slots, anchors, served, sems):
    q = far_a.shape[0]
    ids = slots[0:1, :].astype(I32)
    place_rows(anchors, [(ids[:, :q], far_a[...]), (ids[:, q:], far_b[...])], partial)
    serve_blocks(serve, anchors, served, sems)


def logits_kernel(need, anchors, fetched, out):
    blocks = out.shape[0]

    def body(i, carry):
        for j in range(4):
            b = i * 4 + j
            q = anchors[pl.ds(pl.multiple_of(b * BR, BR), BR), :]
            for k in range(PAIRS_REP):
                out[b, k * BR : (k + 1) * BR, :] = dot(fetched[need[b * PAIRS_REP + k]], q, 1, 1)
        return carry

    lax.fori_loop(0, blocks // 4, body, 0)


def scores_kernel(need, column, begun, anchors, fetched, weights, stats):
    blocks = weights.shape[0]

    def body(i, carry):
        for j in range(4):
            b = i * 4 + j
            q = anchors[pl.ds(pl.multiple_of(b * BR, BR), BR), :]
            total = jnp.zeros((1, BR), F32)
            positive = jnp.zeros((1, BR), F32)
            want = column[pl.ds(b, 1), :]
            for k in range(PAIRS_REP):
                raw = begun[b, k * BR : (k + 1) * BR, :] + dot(fetched[need[b * PAIRS_REP + k]], q, 1, 1)
                logits = raw / logit_sharpness
                w = jnp.exp(logits - 1.0 / logit_sharpness)
                weights[b, k * BR : (k + 1) * BR, :] = w
                total += jnp.sum(w, axis=0, keepdims=True)
                hit = iota((BR, BR), 0) + k * BR == want
                positive += jnp.sum(jnp.where(hit, logits, 0.0), axis=0, keepdims=True)
            stats[pl.ds(b, 1), :] = total
            stats[pl.ds(blocks + b, 1), :] = positive
        return carry

    lax.fori_loop(0, blocks // 4, body, 0)


def grads_kernel(factor, need, column, stats, weights, fetched, slots, far, y0, y1, y2, y3, share):
    blocks = weights.shape[0]

    def body(i, carry):
        for j in range(4):
            b = i * 4 + j
            want = column[pl.ds(b, 1), :]
            total = stats[pl.ds(b, 1), :]
            grad = jnp.zeros((BR, share.shape[1]), F32)
            for k in range(PAIRS_REP):
                hit = iota((BR, BR), 0) + k * BR == want
                c = weights[b, k * BR : (k + 1) * BR, :] / total - jnp.where(hit, 1.0, 0.0)
                grad += dot(c.astype(BF).T, fetched[need[b * PAIRS_REP + k]])
            share[pl.ds(pl.multiple_of(b * BR, BR), BR), :] = (grad * factor).astype(BF)
        return carry

    lax.fori_loop(0, blocks // 4, body, 0)
    step = 256
    total_slots = share.shape[0]
    ids = [column_of(slots[k, :, :]) for k in range(3)] + [column_of(far[...])]
    for k, out in enumerate((y0, y1, y2, y3)):
        for h in range(out.shape[0] // step):
            pick = hot(iota((step, total_slots), 1) == ids[k][h * step : (h + 1) * step, :])
            out[h * step : (h + 1) * step, :] = dot(pick, share[...]).astype(BF)


def back_kernel(a, b, c, d, place, back):
    total = a[...].astype(F32) + b[...].astype(F32) + c[...].astype(F32) + d[...].astype(F32)
    rows = a.shape[0]
    pos = column_of(place[...])
    back[...] = dot(hot(iota((back.shape[0], rows), 1) == pos), total.astype(BF)).astype(BF)


def unit_grad_kernel(got0, got1, place, unit, norm, out):
    n, e = unit.shape
    h = e // 2
    pick = hot(iota((n, got0.shape[0]), 1) == column_of(place[...]))
    grad0 = dot(pick, got0[...])
    grad1 = dot(pick, got1[...])
    rows0, rows1 = unit[:, :h], unit[:, h:]
    radial = jnp.sum(rows0 * grad0, axis=1, keepdims=True)
    radial += jnp.sum(rows1 * grad1, axis=1, keepdims=True)
    length = norm[:, 0:1]
    out[:, :h] = ((grad0 - rows0 * radial) / length).astype(BF)
    out[:, h:] = ((grad1 - rows1 * radial) / length).astype(BF)


def head_grad_kernel(mine, theirs, grad, partner, out):
    step = 256
    for i in range(out.shape[0] // step):
        at = slice(i * step, (i + 1) * step)
        out[at, :] = (dot(mine[at, :], grad[...]) + dot(theirs[at, :], partner[...])).astype(BF)


def sum_kernel(parts, out):
    out[...] = jnp.sum(parts[...].astype(F32), axis=0)


def turn(x, k):
    return lax.ppermute(x, "rep", [(i, (i + k) % REPS) for i in range(REPS)])


def swap(x):
    return lax.ppermute(x, "core", [(0, 1), (1, 0)])


def gather_rep(x):
    half = x.shape[0] // 2 if x.shape[0] % 64 == 0 else (x.shape[0] - 32) // 2
    left, right = turn(x, 1), turn(x, 3)
    return left, right, turn(left[:half], 1), turn(right[half:], 3)


def exchange(x, axes):
    return lax.all_to_all(x, axes, 0, 0, tiled=True)


def shards(features, head_weight, slot_of_image, candidates, positives):
    owners_axes = ("zx", "core")
    everyone = ("zx", "core", "rep")
    dp = lax.axis_size(owners_axes)
    me = lax.axis_index(owners_axes)
    core = lax.axis_index("core")
    rep = lax.axis_index("rep")
    n, width = features.shape
    e = head_weight.shape[1]
    h = e // 2
    devices = dp * REPS
    owner_slots = n * REPS
    blocks = owner_slots // BR
    cap = 2 * n // devices
    count = devices * cap
    factor = objective_factor / (logit_sharpness * math.sqrt(n * devices))
    vmem = pl.BlockSpec(memory_space=pltpu.VMEM)
    smem = pl.BlockSpec(memory_space=pltpu.SMEM)
    far_away = pl.BlockSpec(memory_space=pl.ANY)

    def call(kernel, name, shapes, args, **more):
        return pl.pallas_call(
            kernel, out_shape=shapes, compiler_params=params(), name=name, **more
        )(*args)

    send0, send1, unit, norm, place = call(
        lambda *r: project_kernel(owner_slots, dp, cap, *r),
        "project",
        (
            sds((count, h + BR), BF),
            sds((count, h), BF),
            sds((n, e), F32),
            sds((n, BR), F32),
            sds((8, n), F32),
        ),
        (slot_of_image.reshape(1, n), features, head_weight),
    )
    got0 = exchange(send0.reshape(devices, cap, h + BR), everyone).reshape(count, h + BR)
    got1 = exchange(send1.reshape(devices, cap, h), everyone).reshape(count, h)

    mine, other = call(
        stripes_kernel,
        "stripes",
        (sds((width // 2, n), BF),) * 2,
        (core.reshape(1), features),
        in_specs=[smem, vmem],
    )
    theirs = swap(other)

    packed0, back_place = call(
        compact0_kernel, "compact0", (sds((n + 32, h), BF), sds((8, count), F32)), (got0,)
    )
    left0, right0, far_a0, far_b0 = gather_rep(packed0)
    packed1 = call(compact1_kernel, "compact1", sds((n, h), BF), (got1, back_place))
    left1, right1, far_a1, far_b1 = gather_rep(packed1)

    table = candidates.reshape(dp, blocks, REPS, PAIRS_REP)
    table = lax.dynamic_index_in_dim(table, rep, axis=2, keepdims=False)
    table = table.reshape(dp, blocks * PAIRS_REP)
    owner = table // blocks
    serve = jnp.sum(jnp.where(owner == me, table - owner * blocks, 0), axis=1)
    need = lax.dynamic_index_in_dim(owner, me, axis=0, keepdims=False)
    column = positives.reshape(blocks, BR) - rep * (PAIRS_REP * BR)

    partial0, slots = call(
        near0_kernel,
        "near0",
        (sds((owner_slots, h), BF), sds((3, 8, n), F32)),
        (packed0, left0, right0),
    )
    served_shape = sds((dp, BR, h), BF)
    sems = [pltpu.SemaphoreType.DMA((dp,))]
    anchors0, served0, far = call(
        far0_kernel,
        "far0",
        (sds((owner_slots, h), BF), served_shape, sds((8, n), F32)),
        (serve, partial0, far_a0, far_b0),
        in_specs=[smem] + [vmem] * 3,
        out_specs=(vmem, far_away, vmem),
        scratch_shapes=sems,
    )
    fetched0 = exchange(served0, owners_axes)
    partial1 = call(
        near1_kernel, "near1", sds((owner_slots, h), BF), (packed1, left1, right1, slots)
    )
    anchors1, served1 = call(
        far1_kernel,
        "far1",
        (sds((owner_slots, h), BF), served_shape),
        (serve, partial1, far_a1, far_b1, far),
        in_specs=[smem] + [vmem] * 4,
        out_specs=(vmem, far_away),
        scratch_shapes=sems,
    )
    fetched1 = exchange(served1, owners_axes)

    begun = call(
        logits_kernel,
        "logits",
        sds((blocks, PAIRS_REP * BR, BR), F32),
        (need, anchors0, fetched0),
        in_specs=[smem] + [vmem] * 2,
    )
    weights, stats = call(
        scores_kernel,
        "scores",
        (sds((blocks, PAIRS_REP * BR, BR), F32), sds((2 * blocks, BR), F32)),
        (need, column, begun, anchors1, fetched1),
        in_specs=[smem] + [vmem] * 4,
    )
    stats = lax.psum(stats, "rep")
    total, matching = stats[:blocks], stats[blocks:]
    anchor_row_loss = (jnp.log(total) + 1.0 / logit_sharpness - matching).reshape(owner_slots)

    returned = []
    for i, fetched in enumerate((fetched0, fetched1)):
        y = call(
            lambda *r: grads_kernel(factor, *r),
            f"grads{i}",
            (sds((n, h), BF),) * 4,
            (need, column, stats, weights, fetched, slots, far),
            in_specs=[smem] + [vmem] * 6,
            scratch_shapes=[pltpu.VMEM((owner_slots, h), BF)],
        )
        shares = (y[0], turn(y[1], 3), turn(y[2], 1), turn(y[3], 2))
        back = call(back_kernel, f"back{i}", sds((count, h), BF), (*shares, back_place))
        returned.append(exchange(back.reshape(devices, cap, h), everyone).reshape(count, h))

    grad = call(
        unit_grad_kernel, "unit_grad", sds((n, e), BF), (*returned, place, unit, norm)
    )
    partner = swap(grad)
    partial = call(
        head_grad_kernel, "head_grad", sds((width // 2, e), BF), (mine, theirs, grad, partner)
    )
    parts = exchange(partial.reshape(devices // 2, width // devices, e), ("zx", "rep"))
    weight_grad = call(sum_kernel, "add", sds((width // devices, e), F32), (parts,))
    return (anchor_row_loss, weight_grad)


def solution(mesh):
    dp, rep = mesh.devices.shape
    split = jax.sharding.Mesh(mesh.devices.reshape(dp // 2, 2, rep), ("zx", "core", "rep"))
    everyone = ("zx", "core", "rep")
    owners = ("zx", "core")
    placed = (P(everyone, None), P(), P(everyone), P(), P(owners))
    return jax.shard_map(
        shards,
        mesh=split,
        in_specs=placed,
        out_specs=(P(owners), P(everyone, None)),
        check_vma=False,
    )
```

```python
import math

import jax
import jax.numpy as jnp
from jax import lax
from jax.experimental import pallas as pl
from jax.experimental.pallas import tpu as pltpu
from jax.sharding import PartitionSpec as P

BR = 128
PAIRS_REP = 2
REPS = 4

logit_sharpness = 0.05
objective_factor = 32.0
norm_eps = 1e-06

BF = jnp.bfloat16
F32 = jnp.float32
I32 = jnp.int32
VMEM_BYTES = 24 * 1024 * 1024


def params():
    return pltpu.CompilerParams(vmem_limit_bytes=VMEM_BYTES)


def iota(shape, dim):
    return lax.broadcasted_iota(I32, shape, dim)


def hot(mask):
    return jnp.where(mask, 1.0, 0.0).astype(BF)


def dot(a, b, ca=1, cb=0):
    return lax.dot_general(a, b, (((ca,), (cb,)), ((), ())), preferred_element_type=F32)


def sds(shape, dtype):
    return jax.ShapeDtypeStruct(shape, dtype)


def column_of(rows):
    wide = jnp.concatenate([rows] * (BR // rows.shape[0]), axis=0)
    return wide.T[:, 0:1].astype(I32)


def project_kernel(owner_slots, owners, cap, slot, feat, head, send, unit, norm, place):
    n = feat.shape[0]
    e = head.shape[1]
    projected = dot(feat[...], head[...])
    length = jnp.sqrt(jnp.sum(projected * projected, axis=1, keepdims=True) + norm_eps)
    rows = projected / length
    unit[...] = rows
    norm[...] = jnp.broadcast_to(length, norm.shape)
    descriptor = rows.astype(BF)
    s = slot[...]
    owner = s // owner_slots
    local = s - owner * owner_slots
    mine = iota((owners, n), 0) == owner
    before = dot(hot(mine), hot(iota((n, n), 0) < iota((n, n), 1)))
    rank = jnp.sum(jnp.where(mine, before, 0.0), axis=0, keepdims=True).astype(I32)
    p = (owner * REPS + (rank & (REPS - 1))) * cap + rank // REPS
    place[...] = jnp.broadcast_to(p.astype(F32), place.shape)
    scatter = hot(iota((send.shape[0], n), 0) == p)
    send[:, :e] = dot(scatter, descriptor).astype(BF)
    high = local // BR
    low = local - high * BR
    row = iota((BR, n), 0)
    tags = jnp.where(row == 0, high, jnp.where(row == 1, low, jnp.where(row == 2, 1, 0)))
    send[:, e:] = dot(scatter, tags.astype(F32).astype(BF), 1, 1).astype(BF)


def stripes_kernel(core, feat, mine, other):
    n = feat.shape[0]
    first = core[0] == 0
    half = BR // 2
    for z in range(feat.shape[1] // BR):
        t = feat[:, z * BR : (z + 1) * BR].astype(F32).T
        a, b = t[:half, :], t[half:, :]
        mine[z * half : (z + 1) * half, :] = jnp.where(first, a, b).astype(BF)
        other[z * half : (z + 1) * half, :] = jnp.where(first, b, a).astype(BF)


def compact_kernel(got, packed, place):
    count = got.shape[0]
    e = packed.shape[1]
    rows = packed.shape[0] - 16
    tags = got[:, e:].astype(F32).T
    valid = tags[2:3, :]
    upper = hot(iota((count, count), 0) < iota((count, count), 1))
    before = dot(jnp.broadcast_to(valid, (16, count)).astype(BF), upper)[0:1, :]
    pos = jnp.where(valid > 0.5, before, -1.0)
    place[...] = jnp.broadcast_to(pos, place.shape)
    pick = hot(iota((rows, count), 0) == pos.astype(I32))
    packed[:rows, :] = dot(pick, got[:, :e]).astype(BF)
    packed[rows:, :] = dot(tags[:16, :].astype(BF), pick, 1, 1).astype(BF)


def slot_row(tag):
    tag = tag.astype(F32)
    return tag[0:1, :] * BR + tag[1:2, :]


def near_kernel(own, left, right, partial, slots):
    n = own.shape[0] - 16
    pieces = []
    for k, ref in enumerate((own, left, right)):
        row = slot_row(ref[n:, :])
        slots[k, :, :] = jnp.broadcast_to(row, slots.shape[1:])
        pieces.append((row.astype(I32), ref[:n, :]))
    place_rows(partial, pieces, None)


def place_rows(out, pieces, start):
    step = 256

    def body(i, carry):
        base = pl.multiple_of(i * step, step)
        total = None if start is None else start[pl.ds(base, step), :].astype(F32)
        for ids, rows in pieces:
            at = iota((step, rows.shape[0]), 0) + base
            part = dot(hot(at == ids), rows)
            total = part if total is None else total + part
        out[pl.ds(base, step), :] = total.astype(BF)
        return carry

    lax.fori_loop(0, out.shape[0] // step, body, 0)


def serve_blocks(serve, anchors, served, sems):
    copies = []
    for d in range(served.shape[0]):
        start = pl.multiple_of(serve[d] * BR, BR)
        copies.append(
            pltpu.make_async_copy(anchors.at[pl.ds(start, BR), :], served.at[d], sems.at[d])
        )
    for c in copies:
        c.start()
    for c in copies:
        c.wait()


def far_kernel(serve, partial, far_a, far_b, anchors, served, slots, sems):
    q = far_a.shape[0]
    row = slot_row(far_b[q:, :])
    slots[...] = jnp.broadcast_to(row, slots.shape)
    ids = row.astype(I32)
    place_rows(anchors, [(ids[:, :q], far_a[...]), (ids[:, q:], far_b[:q, :])], partial)
    serve_blocks(serve, anchors, served, sems)


def scores_kernel(need, column, anchors, fetched, weights, stats):
    blocks = weights.shape[0]

    def body(i, carry):
        for j in range(4):
            b = i * 4 + j
            q = anchors[pl.ds(pl.multiple_of(b * BR, BR), BR), :]
            total = jnp.zeros((1, BR), F32)
            positive = jnp.zeros((1, BR), F32)
            want = column[pl.ds(b, 1), :]
            for k in range(PAIRS_REP):
                logits = dot(fetched[need[b * PAIRS_REP + k]], q, 1, 1) / logit_sharpness
                hit = iota((BR, BR), 0) + k * BR == want
                w = jnp.where(hit, 0.0, jnp.exp(logits - 1.0 / logit_sharpness))
                weights[b, k * BR : (k + 1) * BR, :] = w.astype(BF)
                total += jnp.sum(w, axis=0, keepdims=True)
                positive += jnp.sum(jnp.where(hit, logits, 0.0), axis=0, keepdims=True)
            stats[pl.ds(b, 1), :] = total
            stats[pl.ds(blocks + b, 1), :] = positive
        return carry

    lax.fori_loop(0, blocks // 4, body, 0)


def mix_kernel(need, column, weights, fetched, pulled, partner):
    blocks = weights.shape[0]

    def body(i, carry):
        for j in range(4):
            b = i * 4 + j
            want = column[pl.ds(b, 1), :]
            at = pl.ds(pl.multiple_of(b * BR, BR), BR)
            both = jnp.zeros((2 * BR, pulled.shape[1]), F32)
            for k in range(PAIRS_REP):
                hit = hot(iota((BR, BR), 0) + k * BR == want)
                w = weights[b, k * BR : (k + 1) * BR, :]
                both += dot(
                    jnp.concatenate([w.T, hit.T], axis=0), fetched[need[b * PAIRS_REP + k]]
                )
            pulled[at, :] = both[:BR, :].astype(BF)
            partner[at, :] = both[BR:, :].astype(BF)
        return carry

    lax.fori_loop(0, blocks // 4, body, 0)


def pick_rows(out, rows, ids):
    step = 256
    for h in range(out.shape[0] // step):
        pick = hot(iota((step, rows.shape[0]), 1) == ids[h * step : (h + 1) * step, :])
        out[h * step : (h + 1) * step, :] = dot(pick, rows[...]).astype(BF)


def shares_kernel(factor, s0, s1, s2, s3, pulled, partner, slots, far, share, y1, y2, y3):
    blocks = s0.shape[0] // 2
    stats = (s0[...] + s2[...]) + (s1[...] + s3[...])
    rest, matching = stats[:blocks, :], stats[blocks:, :]
    total = rest + jnp.exp(matching - 1.0 / logit_sharpness)
    scale = jnp.concatenate([factor / total, factor * (rest / total)], axis=0)
    scale = jnp.concatenate([scale] * (BR // (2 * blocks)), axis=0).T
    for b in range(blocks):
        at = slice(b * BR, (b + 1) * BR)
        grad = pulled[at, :].astype(F32) * scale[:, b : b + 1]
        grad -= partner[at, :].astype(F32) * scale[:, blocks + b : blocks + b + 1]
        share[at, :] = grad.astype(BF)
    pick_rows(y3, share, column_of(far[...]))
    pick_rows(y1, share, column_of(slots[1, :, :]))
    pick_rows(y2, share, column_of(slots[2, :, :]))


def own_kernel(share, slots, y0):
    pick_rows(y0, share, column_of(slots[0, :, :]))


def back_kernel(a, b, c, d, place, back):
    total = a[...].astype(F32) + b[...].astype(F32) + c[...].astype(F32) + d[...].astype(F32)
    rows = a.shape[0]
    pos = column_of(place[...])
    back[...] = dot(hot(iota((back.shape[0], rows), 1) == pos), total.astype(BF)).astype(BF)


def unit_grad_kernel(got, place, unit, norm, out):
    n = unit.shape[0]
    grad = dot(hot(iota((n, got.shape[0]), 1) == column_of(place[...])), got[...])
    rows = unit[...]
    radial = jnp.sum(rows * grad, axis=1, keepdims=True)
    out[...] = ((grad - rows * radial) / norm[:, 0:1]).astype(BF)


def head_grad_kernel(mine, theirs, grad, partner, out):
    step = 256
    for i in range(out.shape[0] // step):
        at = slice(i * step, (i + 1) * step)
        out[at, :] = (dot(mine[at, :], grad[...]) + dot(theirs[at, :], partner[...])).astype(BF)


def sum_kernel(parts, out):
    out[...] = jnp.sum(parts[...].astype(F32), axis=0)


def turn(x, k):
    return lax.ppermute(x, "rep", [(i, (i + k) % REPS) for i in range(REPS)])


def swap(x):
    return lax.ppermute(x, "core", [(0, 1), (1, 0)])


def exchange(x, axes):
    return lax.all_to_all(x, axes, 0, 0, tiled=True)


def shards(features, head_weight, slot_of_image, candidates, positives):
    owners_axes = ("zx", "core")
    everyone = ("zx", "core", "rep")
    dp = lax.axis_size(owners_axes)
    me = lax.axis_index(owners_axes)
    core = lax.axis_index("core")
    rep = lax.axis_index("rep")
    n, width = features.shape
    e = head_weight.shape[1]
    devices = dp * REPS
    owner_slots = n * REPS
    blocks = owner_slots // BR
    cap = 2 * n // devices
    count = devices * cap
    factor = objective_factor / (logit_sharpness * math.sqrt(n * devices))
    vmem = pl.BlockSpec(memory_space=pltpu.VMEM)
    smem = pl.BlockSpec(memory_space=pltpu.SMEM)
    far_away = pl.BlockSpec(memory_space=pl.ANY)

    def call(kernel, name, shapes, args, **more):
        return pl.pallas_call(
            kernel, out_shape=shapes, compiler_params=params(), name=name, **more
        )(*args)

    send, unit, norm, place = call(
        lambda *r: project_kernel(owner_slots, dp, cap, *r),
        "project",
        (sds((count, e + BR), BF), sds((n, e), F32), sds((n, BR), F32), sds((8, n), F32)),
        (slot_of_image.reshape(1, n), features, head_weight),
    )
    got = exchange(send.reshape(devices, cap, e + BR), everyone).reshape(count, e + BR)

    mine, other = call(
        stripes_kernel,
        "stripes",
        (sds((width // 2, n), BF),) * 2,
        (core.reshape(1), features),
        in_specs=[smem, vmem],
    )
    theirs = swap(other)

    packed, back_place = call(
        compact_kernel, "compact", (sds((n + 16, e), BF), sds((8, count), F32)), (got,)
    )
    left, right = turn(packed, 1), turn(packed, 3)
    far_a, far_b = turn(left[: n // 2], 1), turn(right[n // 2 :], 3)

    table = candidates.reshape(dp, blocks, REPS, PAIRS_REP)
    table = lax.dynamic_index_in_dim(table, rep, axis=2, keepdims=False)
    table = table.reshape(dp, blocks * PAIRS_REP)
    owner = table // blocks
    serve = jnp.sum(jnp.where(owner == me, table - owner * blocks, 0), axis=1)
    need = lax.dynamic_index_in_dim(owner, me, axis=0, keepdims=False)
    column = positives.reshape(blocks, BR) - rep * (PAIRS_REP * BR)

    partial, slots = call(
        near_kernel,
        "near",
        (sds((owner_slots, e), BF), sds((3, 8, n), F32)),
        (packed, left, right),
    )
    anchors, served, far = call(
        far_kernel,
        "far",
        (sds((owner_slots, e), BF), sds((dp, BR, e), BF), sds((8, n), F32)),
        (serve, partial, far_a, far_b),
        in_specs=[smem] + [vmem] * 3,
        out_specs=(vmem, far_away, vmem),
        scratch_shapes=[pltpu.SemaphoreType.DMA((dp,))],
    )
    fetched = exchange(served, owners_axes)
    weights, stats = call(
        scores_kernel,
        "scores",
        (sds((blocks, PAIRS_REP * BR, BR), BF), sds((2 * blocks, BR), F32)),
        (need, column, anchors, fetched),
        in_specs=[smem] + [vmem] * 3,
    )
    spread = (stats, turn(stats, 1), turn(stats, 2), turn(stats, 3))
    pulled, partner = call(
        mix_kernel,
        "mix",
        (sds((owner_slots, e), BF),) * 2,
        (need, column, weights, fetched),
        in_specs=[smem] + [vmem] * 3,
    )
    share, y1, y2, y3 = call(
        lambda *r: shares_kernel(factor, *r),
        "shares",
        (sds((owner_slots, e), BF),) + (sds((n, e), BF),) * 3,
        (*spread, pulled, partner, slots, far),
    )
    y0 = call(own_kernel, "own", sds((n, e), BF), (share, slots))
    shares = (y0, turn(y1, 3), turn(y2, 1), turn(y3, 2))
    back = call(back_kernel, "back", sds((count, e), BF), (*shares, back_place))
    returned = exchange(back.reshape(devices, cap, e), everyone).reshape(count, e)

    both = (spread[0] + spread[2]) + (spread[1] + spread[3])
    rest, matching = both[:blocks], both[blocks:]
    total = rest + jnp.exp(matching - 1.0 / logit_sharpness)
    anchor_row_loss = (jnp.log(total) + 1.0 / logit_sharpness - matching).reshape(owner_slots)

    grad = call(
        unit_grad_kernel, "unit_grad", sds((n, e), BF), (returned, place, unit, norm)
    )
    partial = call(
        head_grad_kernel, "head_grad", sds((width // 2, e), BF), (mine, theirs, grad, swap(grad))
    )
    parts = exchange(partial.reshape(devices // 2, width // devices, e), ("zx", "rep"))
    weight_grad = call(sum_kernel, "add", sds((width // devices, e), F32), (parts,))
    return (anchor_row_loss, weight_grad)


def solution(mesh):
    dp, rep = mesh.devices.shape
    split = jax.sharding.Mesh(mesh.devices.reshape(dp // 2, 2, rep), ("zx", "core", "rep"))
    everyone = ("zx", "core", "rep")
    owners = ("zx", "core")
    placed = (P(everyone, None), P(), P(everyone), P(), P(owners))
    return jax.shard_map(
        shards,
        mesh=split,
        in_specs=placed,
        out_specs=(P(owners), P(everyone, None)),
        check_vma=False,
    )
```

```python
import math

import jax
import jax.numpy as jnp
from jax import lax
from jax.experimental import pallas as pl
from jax.experimental.pallas import tpu as pltpu
from jax.sharding import PartitionSpec as P

BR = 128
PAIRS_REP = 2
REPS = 4

logit_sharpness = 0.05
objective_factor = 32.0
norm_eps = 1e-06

BF = jnp.bfloat16
F32 = jnp.float32
I32 = jnp.int32
VMEM_BYTES = 24 * 1024 * 1024


def params():
    return pltpu.CompilerParams(vmem_limit_bytes=VMEM_BYTES)


def cost(us):
    return pl.CostEstimate(flops=int(us * 1e9), bytes_accessed=int(us * 1e6), transcendentals=0)


def iota(shape, dim):
    return lax.broadcasted_iota(I32, shape, dim)


def hot(mask):
    return jnp.where(mask, 1.0, 0.0).astype(BF)


def dot(a, b, ca=1, cb=0):
    return lax.dot_general(a, b, (((ca,), (cb,)), ((), ())), preferred_element_type=F32)


def sds(shape, dtype):
    return jax.ShapeDtypeStruct(shape, dtype)


def column_of(rows):
    wide = jnp.concatenate([rows] * (BR // rows.shape[0]), axis=0)
    return wide.T[:, 0:1].astype(I32)


def project_kernel(owner_slots, owners, cap, slot, feat, head, send, unit, norm, place):
    n = feat.shape[0]
    e = head.shape[1]
    projected = dot(feat[...], head[...])
    length = jnp.sqrt(jnp.sum(projected * projected, axis=1, keepdims=True) + norm_eps)
    rows = projected / length
    unit[...] = rows
    norm[...] = jnp.broadcast_to(length, norm.shape)
    descriptor = rows.astype(BF)
    s = slot[...]
    owner = s // owner_slots
    local = s - owner * owner_slots
    mine = iota((owners, n), 0) == owner
    before = dot(hot(mine), hot(iota((n, n), 0) < iota((n, n), 1)))
    rank = jnp.sum(jnp.where(mine, before, 0.0), axis=0, keepdims=True).astype(I32)
    member = rank & (REPS - 1)
    device = (owner // 2) * 8 + (member // 2) * 4 + (owner & 1) * 2 + (member & 1)
    p = device * cap + rank // REPS
    place[...] = jnp.broadcast_to(p.astype(F32), place.shape)
    scatter = hot(iota((send.shape[0], n), 0) == p)
    send[:, :e] = dot(scatter, descriptor).astype(BF)
    high = local // BR
    low = local - high * BR
    row = iota((BR, n), 0)
    tags = jnp.where(row == 0, high, jnp.where(row == 1, low, jnp.where(row == 2, 1, 0)))
    send[:, e:] = dot(scatter, tags.astype(F32).astype(BF), 1, 1).astype(BF)


def stripes_kernel(core, feat, mine, other):
    n = feat.shape[0]
    first = core[0] == 0
    half = BR // 2
    for z in range(feat.shape[1] // BR):
        t = feat[:, z * BR : (z + 1) * BR].astype(F32).T
        a, b = t[:half, :], t[half:, :]
        mine[z * half : (z + 1) * half, :] = jnp.where(first, a, b).astype(BF)
        other[z * half : (z + 1) * half, :] = jnp.where(first, b, a).astype(BF)


def compact_kernel(got, packed, place):
    count = got.shape[0]
    e = packed.shape[1]
    rows = packed.shape[0] - 16
    tags = got[:, e:].astype(F32).T
    valid = tags[2:3, :]
    upper = hot(iota((count, count), 0) < iota((count, count), 1))
    before = dot(jnp.broadcast_to(valid, (16, count)).astype(BF), upper)[0:1, :]
    pos = jnp.where(valid > 0.5, before, -1.0)
    place[...] = jnp.broadcast_to(pos, place.shape)
    pick = hot(iota((rows, count), 0) == pos.astype(I32))
    packed[:rows, :] = dot(pick, got[:, :e]).astype(BF)
    packed[rows:, :] = dot(tags[:16, :].astype(BF), pick, 1, 1).astype(BF)


def slot_row(tag):
    tag = tag.astype(F32)
    return tag[0:1, :] * BR + tag[1:2, :]


def place_rows(out, pieces, start, after=None):
    step = 2 * BR

    def body(i, carry):
        base = pl.multiple_of(i * step, step)
        total = None if start is None else start[pl.ds(base, step), :].astype(F32)
        for ids, rows in pieces:
            at = iota((step, rows.shape[0]), 0) + base
            part = dot(hot(at == ids), rows)
            total = part if total is None else total + part
        out[pl.ds(base, step), :] = total.astype(BF)
        if after is not None:
            after(i)
        return carry

    lax.fori_loop(0, out.shape[0] // step, body, 0)


def near_kernel(own, beside, partial, slots):
    n = own.shape[0] - 16
    pieces = []
    for k, ref in enumerate((own, beside)):
        row = slot_row(ref[n:, :])
        slots[k, :, :] = jnp.broadcast_to(row, slots.shape[1:])
        pieces.append((row.astype(I32), ref[:n, :]))
    place_rows(partial, pieces, None)


def middle_kernel(begun, across, partial, slots):
    n = across.shape[0] - 16
    row = slot_row(across[n:, :])
    slots[...] = jnp.broadcast_to(row, slots.shape)
    place_rows(partial, [(row.astype(I32), across[:n, :])], begun)


def far_kernel(serve, order, ready, begun, corner, anchors, served, slots, sems):
    n = corner.shape[0] - 16
    row = slot_row(corner[n:, :])
    slots[...] = jnp.broadcast_to(row, slots.shape)

    def copy(d):
        start = pl.multiple_of(serve[d] * BR, BR)
        return pltpu.make_async_copy(anchors.at[pl.ds(start, BR), :], served.at[d], sems.at[d])

    def begin(j, carry):
        copy(order[j]).start()
        return carry

    def after(i):
        lax.fori_loop(ready[i], ready[i + 1], begin, 0)

    place_rows(anchors, [(row.astype(I32), corner[:n, :])], begun, after)

    def finish(d, carry):
        copy(d).wait()
        return carry

    lax.fori_loop(0, served.shape[0], finish, 0)


def scores_kernel(need, column, anchors, fetched, weights, stats):
    blocks = weights.shape[0]

    def body(i, carry):
        for j in range(4):
            b = i * 4 + j
            q = anchors[pl.ds(pl.multiple_of(b * BR, BR), BR), :]
            total = jnp.zeros((1, BR), F32)
            positive = jnp.zeros((1, BR), F32)
            want = column[pl.ds(b, 1), :]
            for k in range(PAIRS_REP):
                logits = dot(fetched[need[b * PAIRS_REP + k]], q, 1, 1) / logit_sharpness
                hit = iota((BR, BR), 0) + k * BR == want
                w = jnp.where(hit, 0.0, jnp.exp(logits - 1.0 / logit_sharpness))
                weights[b, k * BR : (k + 1) * BR, :] = w.astype(BF)
                total += jnp.sum(w, axis=0, keepdims=True)
                positive += jnp.sum(jnp.where(hit, logits, 0.0), axis=0, keepdims=True)
            stats[pl.ds(b, 1), :] = total
            stats[pl.ds(blocks + b, 1), :] = positive
        return carry

    lax.fori_loop(0, blocks // 4, body, 0)


def mix_kernel(need, column, weights, fetched, pulled, partner):
    blocks = weights.shape[0]

    def body(i, carry):
        for j in range(4):
            b = i * 4 + j
            want = column[pl.ds(b, 1), :]
            at = pl.ds(pl.multiple_of(b * BR, BR), BR)
            both = jnp.zeros((2 * BR, pulled.shape[1]), F32)
            for k in range(PAIRS_REP):
                hit = hot(iota((BR, BR), 0) + k * BR == want)
                w = weights[b, k * BR : (k + 1) * BR, :]
                both += dot(
                    jnp.concatenate([w.T, hit.T], axis=0), fetched[need[b * PAIRS_REP + k]]
                )
            pulled[at, :] = both[:BR, :].astype(BF)
            partner[at, :] = both[BR:, :].astype(BF)
        return carry

    lax.fori_loop(0, blocks // 4, body, 0)


def pick_rows(out, rows, ids):
    step = 256
    for h in range(out.shape[0] // step):
        pick = hot(iota((step, rows.shape[0]), 1) == ids[h * step : (h + 1) * step, :])
        out[h * step : (h + 1) * step, :] = dot(pick, rows[...]).astype(BF)


def shares_kernel(factor, s0, s1, s2, s3, pulled, partner, slots, share, out):
    blocks = s0.shape[0] // 2
    stats = (s0[...] + s3[...]) + (s1[...] + s2[...])
    rest, matching = stats[:blocks, :], stats[blocks:, :]
    total = rest + jnp.exp(matching - 1.0 / logit_sharpness)
    scale = jnp.concatenate([factor / total, factor * (rest / total)], axis=0)
    scale = jnp.concatenate([scale] * (BR // (2 * blocks)), axis=0).T
    for b in range(blocks):
        at = slice(b * BR, (b + 1) * BR)
        grad = pulled[at, :].astype(F32) * scale[:, b : b + 1]
        grad -= partner[at, :].astype(F32) * scale[:, blocks + b : blocks + b + 1]
        share[at, :] = grad.astype(BF)
    pick_rows(out, share, column_of(slots[...]))


def pick_kernel(share, slots, out):
    pick_rows(out, share, column_of(slots[...]))


def back_kernel(a, b, c, place, back):
    total = a[...].astype(F32) + b[...].astype(F32) + c[...].astype(F32)
    rows = a.shape[0]
    pos = column_of(place[...])
    back[...] = dot(hot(iota((back.shape[0], rows), 1) == pos), total.astype(BF)).astype(BF)


def unit_grad_kernel(got, place, unit, norm, out):
    n = unit.shape[0]
    grad = dot(hot(iota((n, got.shape[0]), 1) == column_of(place[...])), got[...])
    rows = unit[...]
    radial = jnp.sum(rows * grad, axis=1, keepdims=True)
    out[...] = ((grad - rows * radial) / norm[:, 0:1]).astype(BF)


def head_grad_kernel(mine, theirs, grad, partner, out):
    step = 256
    for i in range(out.shape[0] // step):
        at = slice(i * step, (i + 1) * step)
        out[at, :] = (dot(mine[at, :], grad[...]) + dot(theirs[at, :], partner[...])).astype(BF)


def sum_kernel(parts, out):
    out[...] = jnp.sum(parts[...].astype(F32), axis=0)


def swap(x, axes=("core",)):
    size = 2 ** len(axes)
    return lax.ppermute(x, axes, [(i, size - 1 - i) for i in range(size)])


def exchange(x, axes):
    return lax.all_to_all(x, axes, 0, 0, tiled=True)


def shards(features, head_weight, slot_of_image, candidates, positives):
    owners_axes = ("zx", "yhi")
    everyone = ("zx", "core", "yhi", "ylo")
    dp = lax.axis_size(owners_axes)
    me = lax.axis_index(owners_axes)
    core = lax.axis_index("core")
    member = core * 2 + lax.axis_index("ylo")
    home = core == lax.axis_index("yhi")
    n, width = features.shape
    e = head_weight.shape[1]
    devices = dp * REPS
    owner_slots = n * REPS
    blocks = owner_slots // BR
    cap = 2 * n // devices
    count = devices * cap
    factor = objective_factor / (logit_sharpness * math.sqrt(n * devices))
    vmem = pl.BlockSpec(memory_space=pltpu.VMEM)
    smem = pl.BlockSpec(memory_space=pltpu.SMEM)
    far_away = pl.BlockSpec(memory_space=pl.ANY)

    def call(kernel, name, shapes, args, **more):
        return pl.pallas_call(
            kernel, out_shape=shapes, compiler_params=params(), name=name, **more
        )(*args)

    send, unit, norm, place = call(
        lambda *r: project_kernel(owner_slots, dp, cap, *r),
        "project",
        (sds((count, e + BR), BF), sds((n, e), F32), sds((n, BR), F32), sds((8, n), F32)),
        (slot_of_image.reshape(1, n), features, head_weight),
    )
    got = exchange(send.reshape(devices, cap, e + BR), everyone).reshape(count, e + BR)

    mine, other = call(
        stripes_kernel,
        "stripes",
        (sds((width // 2, n), BF),) * 2,
        (core.reshape(1), features),
        in_specs=[smem, vmem],
    )
    theirs = swap(other)

    packed, back_place = call(
        compact_kernel, "compact", (sds((n + 16, e), BF), sds((8, count), F32)), (got,)
    )
    beside = swap(packed)
    across = swap(packed, ("ylo",))

    table = candidates.reshape(dp, blocks, REPS, PAIRS_REP)
    table = lax.dynamic_index_in_dim(table, member, axis=2, keepdims=False)
    table = table.reshape(dp, blocks * PAIRS_REP)
    owner = table // blocks
    serve = jnp.sum(jnp.where(owner == me, table - owner * blocks, 0), axis=1)
    need = lax.dynamic_index_in_dim(owner, me, axis=0, keepdims=False)
    column = jnp.where(home, positives, swap(positives)).reshape(blocks, BR)
    column = column - member * (PAIRS_REP * BR)
    numbers = jnp.arange(dp, dtype=I32)
    keys = serve * dp + numbers
    place_of = jnp.sum((keys[None, :] < keys[:, None]).astype(I32), axis=1)
    order = jnp.sum(jnp.where(place_of[None, :] == numbers[:, None], numbers[None, :], 0), axis=1)
    bounds = 2 * jnp.arange(blocks // 2 + 1, dtype=I32)
    ready = jnp.sum((serve[None, :] < bounds[:, None]).astype(I32), axis=1)

    whole = sds((owner_slots, e), BF)
    ids_shape = sds((8, n), F32)
    partial, slots = call(
        near_kernel,
        "near",
        (whole, sds((2, 8, n), F32)),
        (packed, beside),
        cost_estimate=cost(4),
    )
    partial, across = lax.optimization_barrier((partial, across))
    corner = swap(across)
    partial, slots_across = call(middle_kernel, "middle", (whole, ids_shape), (partial, across))
    anchors, served, slots_corner = call(
        far_kernel,
        "far",
        (whole, pltpu.HBM((dp, BR, e), BF), ids_shape),
        (serve, order, ready, partial, corner),
        in_specs=[smem] * 3 + [vmem] * 2,
        out_specs=(vmem, pl.BlockSpec(memory_space=pltpu.HBM), vmem),
        scratch_shapes=[pltpu.SemaphoreType.DMA((dp,))],
    )
    fetched = exchange(served, owners_axes)
    weights, stats = call(
        scores_kernel,
        "scores",
        (sds((blocks, PAIRS_REP * BR, BR), BF), sds((2 * blocks, BR), F32)),
        (need, column, anchors, fetched),
        in_specs=[smem] + [vmem] * 3,
    )
    spread = (stats, swap(stats), swap(stats, ("ylo",)), swap(stats, ("core", "ylo")))
    pulled, partner = call(
        mix_kernel,
        "mix",
        (sds((owner_slots, e), BF),) * 2,
        (need, column, weights, fetched),
        in_specs=[smem] + [vmem] * 3,
    )
    share, for_corner = call(
        lambda *r: shares_kernel(factor, *r),
        "shares",
        (whole, sds((n, e), BF)),
        (*spread, pulled, partner, slots_corner),
    )

    def pick(name, ids):
        return call(pick_kernel, name, sds((n, e), BF), (share, ids))

    for_across = pick("across", slots_across).astype(F32) + swap(for_corner).astype(F32)
    from_across = swap(for_across.astype(BF), ("ylo",))
    from_beside = swap(pick("beside", slots[1]))
    back = call(
        back_kernel,
        "back",
        pltpu.HBM((count, e), BF),
        (pick("own", slots[0]), from_beside, from_across, back_place),
    )
    returned = exchange(back.reshape(devices, cap, e), everyone).reshape(count, e)

    both = (spread[0] + spread[3]) + (spread[1] + spread[2])
    rest, matching = both[:blocks], both[blocks:]
    total = rest + jnp.exp(matching - 1.0 / logit_sharpness)
    loss = (jnp.log(total) + 1.0 / logit_sharpness - matching).reshape(owner_slots)
    anchor_row_loss = jnp.where(home, loss, swap(loss, ("yhi",)))

    grad = call(
        unit_grad_kernel, "unit_grad", sds((n, e), BF), (returned, place, unit, norm)
    )
    partial = call(
        head_grad_kernel, "head_grad", pltpu.HBM((width // 2, e), BF), (mine, theirs, grad, swap(grad))
    )
    parts = exchange(partial.reshape(devices // 2, width // devices, e), ("zx", "yhi", "ylo"))
    weight_grad = call(sum_kernel, "add", sds((width // devices, e), F32), (parts,))
    return (anchor_row_loss, weight_grad)


def solution(mesh):
    dp, rep = mesh.devices.shape
    split = jax.sharding.Mesh(
        mesh.devices.reshape(dp // 2, 2, rep // 2, 2), ("zx", "core", "yhi", "ylo")
    )
    everyone = ("zx", "core", "yhi", "ylo")
    owners = ("zx", "core")
    placed = (P(everyone, None), P(), P(everyone), P(), P(owners))
    return jax.shard_map(
        shards,
        mesh=split,
        in_specs=placed,
        out_specs=(P(owners), P(everyone, None)),
        check_vma=False,
    )
```

```python
import math

import jax
import jax.numpy as jnp
from jax import lax
from jax.experimental import pallas as pl
from jax.experimental.pallas import tpu as pltpu
from jax.sharding import PartitionSpec as P

BR = 128
PAIRS_REP = 2
REPS = 4

logit_sharpness = 0.05
objective_factor = 32.0
norm_eps = 1e-06

BF = jnp.bfloat16
F32 = jnp.float32
I32 = jnp.int32
VMEM_BYTES = 24 * 1024 * 1024


def params():
    return pltpu.CompilerParams(vmem_limit_bytes=VMEM_BYTES)


def cost(us):
    return pl.CostEstimate(flops=int(us * 1e9), bytes_accessed=int(us * 1e6), transcendentals=0)


def iota(shape, dim):
    return lax.broadcasted_iota(I32, shape, dim)


def hot(mask):
    return jnp.where(mask, 1.0, 0.0).astype(BF)


def dot(a, b, ca=1, cb=0):
    return lax.dot_general(a, b, (((ca,), (cb,)), ((), ())), preferred_element_type=F32)


def sds(shape, dtype):
    return jax.ShapeDtypeStruct(shape, dtype)


def column_of(rows):
    wide = jnp.concatenate([rows] * (BR // rows.shape[0]), axis=0)
    return wide.T[:, 0:1].astype(I32)


def project_kernel(
    owner_slots, owners, cap, slot, feat_in, head_in, send, unit, norm, place, feat, head, sems
):
    n = feat.shape[0]
    width, e = head.shape
    parts = 4
    copies = []
    for k in range(parts):
        at = pl.ds(k * (width // parts), width // parts)
        copies.append(pltpu.make_async_copy(head_in.at[at, :], head.at[at, :], sems.at[k]))
        at = pl.ds(k * (n // parts), n // parts)
        copies.append(pltpu.make_async_copy(feat_in.at[at, :], feat.at[at, :], sems.at[parts + k]))
    for c in copies:
        c.start()
    s = slot[...]
    owner = s // owner_slots
    local = s - owner * owner_slots
    mine = iota((owners, n), 0) == owner
    before = dot(hot(mine), hot(iota((n, n), 0) < iota((n, n), 1)))
    rank = jnp.sum(jnp.where(mine, before, 0.0), axis=0, keepdims=True).astype(I32)
    member = rank & (REPS - 1)
    slab = member & 1
    device = (owner // 2) * 8 + (member // 2) * 4 + slab * 2 + ((owner & 1) ^ slab)
    p = device * cap + rank // REPS
    place[...] = jnp.broadcast_to(p.astype(F32), place.shape)
    scatter = hot(iota((send.shape[0], n), 0) == p)
    high = local // BR
    low = local - high * BR
    row = iota((BR, n), 0)
    tags = jnp.where(row == 0, high, jnp.where(row == 1, low, jnp.where(row == 2, 1, 0)))
    send[:, e:] = dot(scatter, tags.astype(F32).astype(BF), 1, 1).astype(BF)
    for c in copies:
        c.wait()
    projected = dot(feat[...], head[...])
    length = jnp.sqrt(jnp.sum(projected * projected, axis=1, keepdims=True) + norm_eps)
    rows = projected / length
    unit[...] = rows
    norm[...] = jnp.broadcast_to(length, norm.shape)
    send[:, :e] = dot(scatter, rows.astype(BF)).astype(BF)


def stripes_kernel(core, feat, mine, other):
    n = feat.shape[0]
    first = core[0] == 0
    half = BR // 2
    for z in range(feat.shape[1] // BR):
        t = feat[:, z * BR : (z + 1) * BR].astype(F32).T
        a, b = t[:half, :], t[half:, :]
        mine[z * half : (z + 1) * half, :] = jnp.where(first, a, b).astype(BF)
        other[z * half : (z + 1) * half, :] = jnp.where(first, b, a).astype(BF)


def compact_kernel(got, packed, place):
    count = got.shape[0]
    e = packed.shape[1]
    rows = packed.shape[0] - 16
    tags = got[:, e:].astype(F32).T
    valid = tags[2:3, :]
    upper = hot(iota((count, count), 0) < iota((count, count), 1))
    before = dot(jnp.broadcast_to(valid, (16, count)).astype(BF), upper)[0:1, :]
    pos = jnp.where(valid > 0.5, before, -1.0)
    place[...] = jnp.broadcast_to(pos, place.shape)
    pick = hot(iota((rows, count), 0) == pos.astype(I32))
    packed[:rows, :] = dot(pick, got[:, :e]).astype(BF)
    packed[rows:, :] = dot(tags[:16, :].astype(BF), pick, 1, 1).astype(BF)


def slot_row(tag):
    tag = tag.astype(F32)
    return tag[0:1, :] * BR + tag[1:2, :]


def place_rows(out, pieces, start, after=None):
    step = 2 * BR

    def body(i, carry):
        base = pl.multiple_of(i * step, step)
        total = None if start is None else start[pl.ds(base, step), :].astype(F32)
        for ids, rows in pieces:
            at = iota((step, rows.shape[0]), 0) + base
            part = dot(hot(at == ids), rows)
            total = part if total is None else total + part
        out[pl.ds(base, step), :] = total.astype(BF)
        if after is not None:
            after(i)
        return carry

    lax.fori_loop(0, out.shape[0] // step, body, 0)


def near_kernel(own, beside, partial, slots):
    n = own.shape[0] - 16
    pieces = []
    for k, ref in enumerate((own, beside)):
        row = slot_row(ref[n:, :])
        slots[k, :, :] = jnp.broadcast_to(row, slots.shape[1:])
        pieces.append((row.astype(I32), ref[:n, :]))
    place_rows(partial, pieces, None)


def middle_kernel(begun, across, partial, slots):
    n = across.shape[0] - 16
    row = slot_row(across[n:, :])
    slots[...] = jnp.broadcast_to(row, slots.shape)
    place_rows(partial, [(row.astype(I32), across[:n, :])], begun)


def far_kernel(serve, order, ready, begun, corner, anchors, served, slots, sems):
    n = corner.shape[0] - 16
    row = slot_row(corner[n:, :])
    slots[...] = jnp.broadcast_to(row, slots.shape)

    def copy(d):
        start = pl.multiple_of(serve[d] * BR, BR)
        return pltpu.make_async_copy(anchors.at[pl.ds(start, BR), :], served.at[d], sems.at[d])

    def begin(j, carry):
        copy(order[j]).start()
        return carry

    def after(i):
        lax.fori_loop(ready[i], ready[i + 1], begin, 0)

    place_rows(anchors, [(row.astype(I32), corner[:n, :])], begun, after)

    def finish(d, carry):
        copy(d).wait()
        return carry

    lax.fori_loop(0, served.shape[0], finish, 0)


def scores_kernel(need, column, anchors, fetched, weights, stats):
    blocks = weights.shape[0]

    def body(i, carry):
        for j in range(4):
            b = i * 4 + j
            q = anchors[pl.ds(pl.multiple_of(b * BR, BR), BR), :]
            total = jnp.zeros((1, BR), F32)
            positive = jnp.zeros((1, BR), F32)
            want = column[pl.ds(b, 1), :]
            for k in range(PAIRS_REP):
                logits = dot(fetched[need[b * PAIRS_REP + k]], q, 1, 1) / logit_sharpness
                hit = iota((BR, BR), 0) + k * BR == want
                w = jnp.where(hit, 0.0, jnp.exp(logits - 1.0 / logit_sharpness))
                weights[b, k * BR : (k + 1) * BR, :] = w.astype(BF)
                total += jnp.sum(w, axis=0, keepdims=True)
                positive += jnp.sum(jnp.where(hit, logits, 0.0), axis=0, keepdims=True)
            stats[pl.ds(b, 1), :] = total
            stats[pl.ds(blocks + b, 1), :] = positive
        return carry

    lax.fori_loop(0, blocks // 4, body, 0)


def mix_kernel(need, column, weights, fetched, pulled, partner):
    blocks = weights.shape[0]

    def body(i, carry):
        for j in range(4):
            b = i * 4 + j
            want = column[pl.ds(b, 1), :]
            at = pl.ds(pl.multiple_of(b * BR, BR), BR)
            both = jnp.zeros((2 * BR, pulled.shape[1]), F32)
            for k in range(PAIRS_REP):
                hit = hot(iota((BR, BR), 0) + k * BR == want)
                w = weights[b, k * BR : (k + 1) * BR, :]
                both += dot(
                    jnp.concatenate([w.T, hit.T], axis=0), fetched[need[b * PAIRS_REP + k]]
                )
            pulled[at, :] = both[:BR, :].astype(BF)
            partner[at, :] = both[BR:, :].astype(BF)
        return carry

    lax.fori_loop(0, blocks // 4, body, 0)


def pick_rows(out, rows, ids):
    step = 256
    for h in range(out.shape[0] // step):
        pick = hot(iota((step, rows.shape[0]), 1) == ids[h * step : (h + 1) * step, :])
        out[h * step : (h + 1) * step, :] = dot(pick, rows[...]).astype(BF)


def shares_kernel(factor, s0, s1, s2, s3, pulled, partner, slots, share, out):
    blocks = s0.shape[0] // 2
    stats = (s0[...] + s3[...]) + (s1[...] + s2[...])
    rest, matching = stats[:blocks, :], stats[blocks:, :]
    total = rest + jnp.exp(matching - 1.0 / logit_sharpness)
    scale = jnp.concatenate([factor / total, factor * (rest / total)], axis=0)
    scale = jnp.concatenate([scale] * (BR // (2 * blocks)), axis=0).T
    for b in range(blocks):
        at = slice(b * BR, (b + 1) * BR)
        grad = pulled[at, :].astype(F32) * scale[:, b : b + 1]
        grad -= partner[at, :].astype(F32) * scale[:, blocks + b : blocks + b + 1]
        share[at, :] = grad.astype(BF)
    pick_rows(out, share, column_of(slots[...]))


def pick_kernel(share, slots, out):
    pick_rows(out, share, column_of(slots[...]))


def back_kernel(a, b, c, place, back):
    total = a[...].astype(F32) + b[...].astype(F32) + c[...].astype(F32)
    rows = a.shape[0]
    pos = column_of(place[...])
    back[...] = dot(hot(iota((back.shape[0], rows), 1) == pos), total.astype(BF)).astype(BF)


def unit_grad_kernel(got, place, unit, norm, out):
    n = unit.shape[0]
    grad = dot(hot(iota((n, got.shape[0]), 1) == column_of(place[...])), got[...])
    rows = unit[...]
    radial = jnp.sum(rows * grad, axis=1, keepdims=True)
    out[...] = ((grad - rows * radial) / norm[:, 0:1]).astype(BF)


def head_grad_kernel(mine, theirs, grad, partner, out):
    step = 256
    for i in range(out.shape[0] // step):
        at = slice(i * step, (i + 1) * step)
        out[at, :] = (dot(mine[at, :], grad[...]) + dot(theirs[at, :], partner[...])).astype(BF)


def sum_kernel(parts, out):
    out[...] = jnp.sum(parts[...].astype(F32), axis=0)


def swap(x, axes=("core",)):
    size = 2 ** len(axes)
    return lax.ppermute(x, axes, [(i, size - 1 - i) for i in range(size)])


def exchange(x, axes):
    return lax.all_to_all(x, axes, 0, 0, tiled=True)


def shards(features, head_weight, slot_of_image, candidates, positives):
    slab_axes = ("zx", "ylo")
    everyone = ("zx", "core", "yhi", "ylo")
    dp = lax.axis_size(slab_axes)
    slab = lax.axis_index("yhi")
    me = lax.axis_index(slab_axes) ^ slab
    core = lax.axis_index("core")
    member = core * 2 + slab
    home = core == (me & 1)
    n, width = features.shape
    e = head_weight.shape[1]
    devices = dp * REPS
    owner_slots = n * REPS
    blocks = owner_slots // BR
    cap = 2 * n // devices
    count = devices * cap
    factor = objective_factor / (logit_sharpness * math.sqrt(n * devices))
    vmem = pl.BlockSpec(memory_space=pltpu.VMEM)
    smem = pl.BlockSpec(memory_space=pltpu.SMEM)
    far_away = pl.BlockSpec(memory_space=pl.ANY)

    def call(kernel, name, shapes, args, **more):
        return pl.pallas_call(
            kernel, out_shape=shapes, compiler_params=params(), name=name, **more
        )(*args)

    send, unit, norm, place = call(
        lambda *r: project_kernel(owner_slots, dp, cap, *r),
        "project",
        (sds((count, e + BR), BF), sds((n, e), F32), sds((n, BR), F32), sds((8, n), F32)),
        (
            slot_of_image.reshape(1, n),
            pltpu.with_memory_space_constraint(features, pltpu.HBM),
            pltpu.with_memory_space_constraint(head_weight, pltpu.HBM),
        ),
        in_specs=[vmem, far_away, far_away],
        scratch_shapes=[
            pltpu.VMEM((n, width), BF),
            pltpu.VMEM((width, e), BF),
            pltpu.SemaphoreType.DMA((8,)),
        ],
    )
    got = exchange(send.reshape(devices, cap, e + BR), everyone).reshape(count, e + BR)

    mine, other = call(
        stripes_kernel,
        "stripes",
        (sds((width // 2, n), BF),) * 2,
        (core.reshape(1), features),
        in_specs=[smem, vmem],
    )
    theirs = swap(other)

    table = candidates.reshape(dp, blocks, REPS, PAIRS_REP)
    table = lax.dynamic_index_in_dim(table, member, axis=2, keepdims=False)
    table = table.reshape(dp, blocks * PAIRS_REP)
    owner = table // blocks
    numbers = jnp.arange(dp, dtype=I32)
    wanted = jnp.sum(jnp.where(owner == me, table - owner * blocks, 0), axis=1)
    serve = jnp.sum(jnp.where(numbers[None, :] == (numbers ^ slab)[:, None], wanted[None, :], 0), axis=1)
    need = lax.dynamic_index_in_dim(owner, me, axis=0, keepdims=False) ^ slab
    column = jnp.where(home, positives, swap(positives)).reshape(blocks, BR)
    column = column - member * (PAIRS_REP * BR)
    keys = serve * dp + numbers
    place_of = jnp.sum((keys[None, :] < keys[:, None]).astype(I32), axis=1)
    order = jnp.sum(jnp.where(place_of[None, :] == numbers[:, None], numbers[None, :], 0), axis=1)
    bounds = 2 * jnp.arange(blocks // 2 + 1, dtype=I32)
    ready = jnp.sum((serve[None, :] < bounds[:, None]).astype(I32), axis=1)

    got, serve, order, ready, need = lax.optimization_barrier((got, serve, order, ready, need))
    packed, back_place = call(
        compact_kernel, "compact", (sds((n + 16, e), BF), sds((8, count), F32)), (got,)
    )
    beside = swap(packed)
    across = swap(packed, ("yhi", "ylo"))

    whole = sds((owner_slots, e), BF)
    ids_shape = sds((8, n), F32)
    partial, slots = call(
        near_kernel,
        "near",
        (whole, sds((2, 8, n), F32)),
        (packed, beside),
        cost_estimate=cost(4),
    )
    partial, across = lax.optimization_barrier((partial, across))
    corner = swap(across)
    partial, slots_across = call(middle_kernel, "middle", (whole, ids_shape), (partial, across))
    anchors, served, slots_corner = call(
        far_kernel,
        "far",
        (whole, pltpu.HBM((dp, BR, e), BF), ids_shape),
        (serve, order, ready, partial, corner),
        in_specs=[smem] * 3 + [vmem] * 2,
        out_specs=(vmem, pl.BlockSpec(memory_space=pltpu.HBM), vmem),
        scratch_shapes=[pltpu.SemaphoreType.DMA((dp,))],
    )
    fetched = exchange(served, slab_axes)
    weights, stats = call(
        scores_kernel,
        "scores",
        (sds((blocks, PAIRS_REP * BR, BR), BF), sds((2 * blocks, BR), F32)),
        (need, column, anchors, fetched),
        in_specs=[smem] + [vmem] * 3,
    )
    spread = (stats, swap(stats), swap(stats, ("yhi", "ylo")), swap(stats, ("core", "yhi", "ylo")))
    pulled, partner = call(
        mix_kernel,
        "mix",
        (sds((owner_slots, e), BF),) * 2,
        (need, column, weights, fetched),
        in_specs=[smem] + [vmem] * 3,
    )
    share, for_corner = call(
        lambda *r: shares_kernel(factor, *r),
        "shares",
        (whole, sds((n, e), BF)),
        (*spread, pulled, partner, slots_corner),
    )

    def pick(name, ids):
        return call(pick_kernel, name, sds((n, e), BF), (share, ids))

    for_across = pick("across", slots_across).astype(F32) + swap(for_corner).astype(F32)
    from_across = swap(for_across.astype(BF), ("yhi", "ylo"))
    from_beside = swap(pick("beside", slots[1]))
    back = call(
        back_kernel,
        "back",
        pltpu.HBM((count, e), BF),
        (pick("own", slots[0]), from_beside, from_across, back_place),
    )
    returned = exchange(back.reshape(devices, cap, e), everyone).reshape(count, e)

    both = (spread[0] + spread[3]) + (spread[1] + spread[2])
    rest, matching = both[:blocks], both[blocks:]
    total = rest + jnp.exp(matching - 1.0 / logit_sharpness)
    loss = (jnp.log(total) + 1.0 / logit_sharpness - matching).reshape(owner_slots)
    anchor_row_loss = jnp.where(home, loss, swap(loss, ("ylo",)))

    grad = call(
        unit_grad_kernel, "unit_grad", sds((n, e), BF), (returned, place, unit, norm)
    )
    partial = call(
        head_grad_kernel, "head_grad", pltpu.HBM((width // 2, e), BF), (mine, theirs, grad, swap(grad))
    )
    parts = exchange(partial.reshape(devices // 2, width // devices, e), ("zx", "yhi", "ylo"))
    weight_grad = call(sum_kernel, "add", sds((width // devices, e), F32), (parts,))
    return (anchor_row_loss, weight_grad)


def solution(mesh):
    dp, rep = mesh.devices.shape
    split = jax.sharding.Mesh(
        mesh.devices.reshape(dp // 2, 2, rep // 2, 2), ("zx", "core", "yhi", "ylo")
    )
    everyone = ("zx", "core", "yhi", "ylo")
    owners = ("zx", "core")
    placed = (P(everyone, None), P(), P(everyone), P(), P(owners))
    return jax.shard_map(
        shards,
        mesh=split,
        in_specs=placed,
        out_specs=(P(owners), P(everyone, None)),
        check_vma=False,
    )
```

```python
import math

import jax
import jax.numpy as jnp
from jax import lax
from jax.experimental import pallas as pl
from jax.experimental.pallas import tpu as pltpu
from jax.sharding import PartitionSpec as P

BR = 128
PAIRS_REP = 2
REPS = 4

logit_sharpness = 0.05
objective_factor = 32.0
norm_eps = 1e-06

BF = jnp.bfloat16
F32 = jnp.float32
I32 = jnp.int32
VMEM_BYTES = 24 * 1024 * 1024


def params():
    return pltpu.CompilerParams(vmem_limit_bytes=VMEM_BYTES)


def cost(us):
    return pl.CostEstimate(flops=int(us * 1e9), bytes_accessed=int(us * 1e6), transcendentals=0)


def iota(shape, dim):
    return lax.broadcasted_iota(I32, shape, dim)


def hot(mask):
    return jnp.where(mask, 1.0, 0.0).astype(BF)


def dot(a, b, ca=1, cb=0):
    return lax.dot_general(a, b, (((ca,), (cb,)), ((), ())), preferred_element_type=F32)


def sds(shape, dtype):
    return jax.ShapeDtypeStruct(shape, dtype)


def column_of(rows):
    wide = jnp.concatenate([rows] * (BR // rows.shape[0]), axis=0)
    return wide.T[:, 0:1].astype(I32)


def project_kernel(
    owner_slots, owners, cap, slot, feat_in, head_in, send, unit, norm, place, feat, head, kept, sems
):
    n = feat.shape[0]
    width, e = head.shape
    parts = 4
    depth = width // parts
    copies = []
    for k in range(parts):
        at = pl.ds(k * depth, depth)
        copies.append(pltpu.make_async_copy(head_in.at[at, :], head.at[at, :], sems.at[k]))
        copies.append(pltpu.make_async_copy(feat_in.at[:, at], feat.at[:, at], sems.at[parts + k]))
    for c in copies:
        c.start()
    s = slot[...]
    owner = s // owner_slots
    local = s - owner * owner_slots
    mine = iota((owners, n), 0) == owner
    before = dot(hot(mine), hot(iota((n, n), 0) < iota((n, n), 1)))
    rank = jnp.sum(jnp.where(mine, before, 0.0), axis=0, keepdims=True).astype(I32)
    member = rank & (REPS - 1)
    slab = member & 1
    device = (owner // 2) * 8 + (member // 2) * 4 + slab * 2 + ((owner & 1) ^ slab)
    p = device * cap + rank // REPS
    place[...] = jnp.broadcast_to(p.astype(F32), place.shape)
    scatter = hot(iota((send.shape[0], n), 0) == p)
    high = local // BR
    low = local - high * BR
    row = iota((BR, n), 0)
    tags = jnp.where(row == 0, high, jnp.where(row == 1, low, jnp.where(row == 2, 1, 0)))
    send[:, e:] = dot(scatter, tags.astype(F32).astype(BF), 1, 1).astype(BF)
    projected = jnp.zeros((n, e), F32)
    for k in range(parts):
        copies[2 * k].wait()
        copies[2 * k + 1].wait()
        at = slice(k * depth, (k + 1) * depth)
        projected += dot(feat[:, at], head[at, :])
    length = jnp.sqrt(jnp.sum(projected * projected, axis=1, keepdims=True) + norm_eps)
    rows = projected / length
    kept[...] = rows
    keep = pltpu.make_async_copy(kept, unit, sems.at[2 * parts])
    keep.start()
    norm[...] = jnp.broadcast_to(length, norm.shape)
    send[:, :e] = dot(scatter, rows.astype(BF)).astype(BF)
    keep.wait()


def stripes_kernel(core, feat, mine, other):
    n = feat.shape[0]
    first = core[0] == 0
    half = BR // 2
    for z in range(feat.shape[1] // BR):
        t = feat[:, z * BR : (z + 1) * BR].astype(F32).T
        a, b = t[:half, :], t[half:, :]
        mine[z * half : (z + 1) * half, :] = jnp.where(first, a, b).astype(BF)
        other[z * half : (z + 1) * half, :] = jnp.where(first, b, a).astype(BF)


def compact_kernel(got, packed, place):
    count = got.shape[0]
    e = packed.shape[1]
    rows = packed.shape[0] - 16
    tags = got[:, e:].astype(F32).T
    valid = tags[2:3, :]
    upper = hot(iota((count, count), 0) < iota((count, count), 1))
    before = dot(jnp.broadcast_to(valid, (16, count)).astype(BF), upper)[0:1, :]
    pos = jnp.where(valid > 0.5, before, -1.0)
    place[...] = jnp.broadcast_to(pos, place.shape)
    pick = hot(iota((rows, count), 0) == pos.astype(I32))
    packed[:rows, :] = dot(pick, got[:, :e]).astype(BF)
    packed[rows:, :] = dot(tags[:16, :].astype(BF), pick, 1, 1).astype(BF)


def slot_row(tag):
    tag = tag.astype(F32)
    return tag[0:1, :] * BR + tag[1:2, :]


def place_rows(out, pieces, start, after=None):
    step = 2 * BR

    def body(i, carry):
        base = pl.multiple_of(i * step, step)
        total = None if start is None else start[pl.ds(base, step), :].astype(F32)
        for ids, rows in pieces:
            at = iota((step, rows.shape[0]), 0) + base
            part = dot(hot(at == ids), rows)
            total = part if total is None else total + part
        out[pl.ds(base, step), :] = total.astype(BF)
        if after is not None:
            after(i)
        return carry

    lax.fori_loop(0, out.shape[0] // step, body, 0)


def near_kernel(own, beside, partial, slots):
    n = own.shape[0] - 16
    pieces = []
    for k, ref in enumerate((own, beside)):
        row = slot_row(ref[n:, :])
        slots[k, :, :] = jnp.broadcast_to(row, slots.shape[1:])
        pieces.append((row.astype(I32), ref[:n, :]))
    place_rows(partial, pieces, None)


def middle_kernel(begun, across, partial, slots):
    n = across.shape[0] - 16
    row = slot_row(across[n:, :])
    slots[...] = jnp.broadcast_to(row, slots.shape)
    place_rows(partial, [(row.astype(I32), across[:n, :])], begun)


def far_kernel(serve, order, ready, begun, corner, anchors, served, slots, sems):
    n = corner.shape[0] - 16
    row = slot_row(corner[n:, :])
    slots[...] = jnp.broadcast_to(row, slots.shape)

    def copy(d):
        start = pl.multiple_of(serve[d] * BR, BR)
        return pltpu.make_async_copy(anchors.at[pl.ds(start, BR), :], served.at[d], sems.at[d])

    def begin(j, carry):
        copy(order[j]).start()
        return carry

    def after(i):
        lax.fori_loop(ready[i], ready[i + 1], begin, 0)

    place_rows(anchors, [(row.astype(I32), corner[:n, :])], begun, after)

    def finish(d, carry):
        copy(d).wait()
        return carry

    lax.fori_loop(0, served.shape[0], finish, 0)


def scores_kernel(need, column, anchors, fetched, weights, stats, partners, sems):
    blocks = weights.shape[0]

    def copy(b, k):
        return pltpu.make_async_copy(
            fetched.at[need[b * PAIRS_REP + k]],
            partners.at[b, pl.ds(k * BR, BR), :],
            sems.at[b * PAIRS_REP + k],
        )

    for b in range(blocks):
        for k in range(PAIRS_REP):
            copy(b, k).start()

    def body(i, carry):
        for j in range(4):
            b = i * 4 + j
            for k in range(PAIRS_REP):
                copy(b, k).wait()
            q = anchors[pl.ds(pl.multiple_of(b * BR, BR), BR), :]
            logits = dot(partners[b], q, 1, 1) / logit_sharpness
            hit = iota(logits.shape, 0) == column[pl.ds(b, 1), :]
            w = jnp.where(hit, 0.0, jnp.exp(logits - 1.0 / logit_sharpness))
            weights[b, :, :] = w.astype(BF)
            stats[pl.ds(b, 1), :] = jnp.sum(w, axis=0, keepdims=True)
            positive = jnp.sum(jnp.where(hit, logits, 0.0), axis=0, keepdims=True)
            stats[pl.ds(blocks + b, 1), :] = positive
        return carry

    lax.fori_loop(0, blocks // 4, body, 0)


def mix_kernel(column, weights, partners, pulled, partner):
    blocks = weights.shape[0]

    def body(i, carry):
        for j in range(4):
            b = i * 4 + j
            w = weights[b]
            hit = hot(iota(w.shape, 0) == column[pl.ds(b, 1), :])
            both = dot(jnp.concatenate([w, hit], axis=1), partners[b], 0, 0)
            at = pl.ds(pl.multiple_of(b * BR, BR), BR)
            pulled[at, :] = both[:BR, :].astype(BF)
            partner[at, :] = both[BR:, :].astype(BF)
        return carry

    lax.fori_loop(0, blocks // 4, body, 0)


def pick_rows(out, rows, ids):
    step = 256
    for h in range(out.shape[0] // step):
        pick = hot(iota((step, rows.shape[0]), 1) == ids[h * step : (h + 1) * step, :])
        out[h * step : (h + 1) * step, :] = dot(pick, rows[...]).astype(BF)


def shares_kernel(factor, s0, s1, s2, s3, pulled, partner, slots, share, out):
    blocks = s0.shape[0] // 2
    stats = (s0[...] + s3[...]) + (s1[...] + s2[...])
    rest, matching = stats[:blocks, :], stats[blocks:, :]
    total = rest + jnp.exp(matching - 1.0 / logit_sharpness)
    scale = jnp.concatenate([factor / total, factor * (rest / total)], axis=0)
    scale = jnp.concatenate([scale] * (BR // (2 * blocks)), axis=0).T
    for b in range(blocks):
        at = slice(b * BR, (b + 1) * BR)
        grad = pulled[at, :].astype(F32) * scale[:, b : b + 1]
        grad -= partner[at, :].astype(F32) * scale[:, blocks + b : blocks + b + 1]
        share[at, :] = grad.astype(BF)
    pick_rows(out, share, column_of(slots[...]))


def pick_kernel(share, slots, out):
    pick_rows(out, share, column_of(slots[...]))


def back_kernel(a, b, c, place, back):
    total = a[...].astype(F32) + b[...].astype(F32) + c[...].astype(F32)
    rows = a.shape[0]
    pos = column_of(place[...])
    back[...] = dot(hot(iota((back.shape[0], rows), 1) == pos), total.astype(BF)).astype(BF)


def unit_grad_kernel(got, place, unit, norm, out, kept, sem):
    fetch = pltpu.make_async_copy(unit, kept, sem)
    fetch.start()
    n = norm.shape[0]
    grad = dot(hot(iota((n, got.shape[0]), 1) == column_of(place[...])), got[...])
    fetch.wait()
    rows = kept[...]
    radial = jnp.sum(rows * grad, axis=1, keepdims=True)
    out[...] = ((grad - rows * radial) / norm[:, 0:1]).astype(BF)


def head_begun_kernel(mine, grad, out):
    step = 256
    for i in range(out.shape[0] // step):
        at = slice(i * step, (i + 1) * step)
        out[at, :] = dot(mine[at, :], grad[...])


def head_grad_kernel(begun, theirs, partner, out):
    step = 256
    for i in range(out.shape[0] // step):
        at = slice(i * step, (i + 1) * step)
        out[at, :] = (begun[at, :] + dot(theirs[at, :], partner[...])).astype(BF)


def sum_kernel(parts, out):
    out[...] = jnp.sum(parts[...].astype(F32), axis=0)


def swap(x, axes=("core",)):
    size = 2 ** len(axes)
    return lax.ppermute(x, axes, [(i, size - 1 - i) for i in range(size)])


def exchange(x, axes):
    return lax.all_to_all(x, axes, 0, 0, tiled=True)


def shards(features, head_weight, slot_of_image, candidates, positives):
    slab_axes = ("zx", "ylo")
    everyone = ("zx", "core", "yhi", "ylo")
    dp = lax.axis_size(slab_axes)
    slab = lax.axis_index("yhi")
    me = lax.axis_index(slab_axes) ^ slab
    core = lax.axis_index("core")
    member = core * 2 + slab
    home = core == (me & 1)
    n, width = features.shape
    e = head_weight.shape[1]
    devices = dp * REPS
    owner_slots = n * REPS
    blocks = owner_slots // BR
    cap = 2 * n // devices
    count = devices * cap
    factor = objective_factor / (logit_sharpness * math.sqrt(n * devices))
    vmem = pl.BlockSpec(memory_space=pltpu.VMEM)
    smem = pl.BlockSpec(memory_space=pltpu.SMEM)
    far_away = pl.BlockSpec(memory_space=pl.ANY)

    def call(kernel, name, shapes, args, **more):
        return pl.pallas_call(
            kernel, out_shape=shapes, compiler_params=params(), name=name, **more
        )(*args)

    send, unit, norm, place = call(
        lambda *r: project_kernel(owner_slots, dp, cap, *r),
        "project",
        (sds((count, e + BR), BF), pltpu.HBM((n, e), F32), sds((n, BR), F32), sds((8, n), F32)),
        (
            slot_of_image.reshape(1, n),
            pltpu.with_memory_space_constraint(features, pltpu.HBM),
            pltpu.with_memory_space_constraint(head_weight, pltpu.HBM),
        ),
        in_specs=[vmem, far_away, far_away],
        out_specs=(vmem, far_away, vmem, vmem),
        scratch_shapes=[
            pltpu.VMEM((n, width), BF),
            pltpu.VMEM((width, e), BF),
            pltpu.VMEM((n, e), F32),
            pltpu.SemaphoreType.DMA((9,)),
        ],
    )
    got = exchange(send.reshape(devices, cap, e + BR), everyone).reshape(count, e + BR)

    mine, other = call(
        stripes_kernel,
        "stripes",
        (sds((width // 2, n), BF),) * 2,
        (core.reshape(1), features),
        in_specs=[smem, vmem],
    )
    theirs = swap(other)

    table = candidates.reshape(dp, blocks, REPS, PAIRS_REP)
    table = lax.dynamic_index_in_dim(table, member, axis=2, keepdims=False)
    table = table.reshape(dp, blocks * PAIRS_REP)
    owner = table // blocks
    numbers = jnp.arange(dp, dtype=I32)
    wanted = jnp.sum(jnp.where(owner == me, table - owner * blocks, 0), axis=1)
    serve = jnp.sum(jnp.where(numbers[None, :] == (numbers ^ slab)[:, None], wanted[None, :], 0), axis=1)
    need = lax.dynamic_index_in_dim(owner, me, axis=0, keepdims=False) ^ slab
    column = jnp.where(home, positives, swap(positives)).reshape(blocks, BR)
    column = column - member * (PAIRS_REP * BR)
    keys = serve * dp + numbers
    place_of = jnp.sum((keys[None, :] < keys[:, None]).astype(I32), axis=1)
    order = jnp.sum(jnp.where(place_of[None, :] == numbers[:, None], numbers[None, :], 0), axis=1)
    bounds = 2 * jnp.arange(blocks // 2 + 1, dtype=I32)
    ready = jnp.sum((serve[None, :] < bounds[:, None]).astype(I32), axis=1)

    got, serve, order, ready, need = lax.optimization_barrier((got, serve, order, ready, need))
    packed, back_place = call(
        compact_kernel, "compact", (sds((n + 16, e), BF), sds((8, count), F32)), (got,)
    )
    beside = swap(packed)
    across = swap(packed, ("yhi", "ylo"))

    whole = sds((owner_slots, e), BF)
    ids_shape = sds((8, n), F32)
    partial, slots = call(
        near_kernel,
        "near",
        (whole, sds((2, 8, n), F32)),
        (packed, beside),
        cost_estimate=cost(4),
    )
    partial, across = lax.optimization_barrier((partial, across))
    corner = swap(across)
    partial, slots_across = call(middle_kernel, "middle", (whole, ids_shape), (partial, across))
    anchors, served, slots_corner = call(
        far_kernel,
        "far",
        (whole, pltpu.HBM((dp, BR, e), BF), ids_shape),
        (serve, order, ready, partial, corner),
        in_specs=[smem] * 3 + [vmem] * 2,
        out_specs=(vmem, pl.BlockSpec(memory_space=pltpu.HBM), vmem),
        scratch_shapes=[pltpu.SemaphoreType.DMA((dp,))],
    )
    fetched = exchange(served, slab_axes)
    weights, stats, partners = call(
        scores_kernel,
        "scores",
        (
            sds((blocks, PAIRS_REP * BR, BR), BF),
            sds((2 * blocks, BR), F32),
            sds((blocks, PAIRS_REP * BR, e), BF),
        ),
        (need, column, anchors, fetched),
        in_specs=[smem, vmem, vmem, far_away],
        scratch_shapes=[pltpu.SemaphoreType.DMA((blocks * PAIRS_REP,))],
    )
    spread = (stats, swap(stats), swap(stats, ("yhi", "ylo")), swap(stats, ("core", "yhi", "ylo")))
    pulled, partner = call(
        mix_kernel,
        "mix",
        (sds((owner_slots, e), BF),) * 2,
        (column, weights, partners),
    )
    share, for_corner = call(
        lambda *r: shares_kernel(factor, *r),
        "shares",
        (whole, sds((n, e), BF)),
        (*spread, pulled, partner, slots_corner),
    )

    def pick(name, rows, ids):
        return call(
            pick_kernel, name, sds((n, e), BF), (rows, ids), cost_estimate=cost(0.01)
        )

    for_across = pick("across", share, slots_across).astype(F32) + swap(for_corner).astype(F32)
    from_across = swap(for_across.astype(BF), ("yhi", "ylo"))
    from_beside = swap(pick("beside", share, slots[1]))
    back = call(
        back_kernel,
        "back",
        pltpu.HBM((count, e), BF),
        (pick("own", share, slots[0]), from_beside, from_across, back_place),
    )
    returned = exchange(back.reshape(devices, cap, e), everyone).reshape(count, e)

    both = (spread[0] + spread[3]) + (spread[1] + spread[2])
    rest, matching = both[:blocks], both[blocks:]
    total = rest + jnp.exp(matching - 1.0 / logit_sharpness)
    loss = (jnp.log(total) + 1.0 / logit_sharpness - matching).reshape(owner_slots)
    anchor_row_loss = jnp.where(home, loss, swap(loss, ("ylo",)))

    grad = call(
        unit_grad_kernel,
        "unit_grad",
        sds((n, e), BF),
        (returned, place, pltpu.with_memory_space_constraint(unit, pltpu.HBM), norm),
        in_specs=[vmem, vmem, far_away, vmem],
        scratch_shapes=[pltpu.VMEM((n, e), F32), pltpu.SemaphoreType.DMA],
    )
    begun = call(head_begun_kernel, "head_begun", sds((width // 2, e), F32), (mine, grad))
    partial = call(
        head_grad_kernel,
        "head_grad",
        pltpu.HBM((width // 2, e), BF),
        (begun, theirs, swap(grad)),
    )
    parts = exchange(partial.reshape(devices // 2, width // devices, e), ("zx", "yhi", "ylo"))
    weight_grad = call(sum_kernel, "add", sds((width // devices, e), F32), (parts,))
    return (anchor_row_loss, weight_grad)


def solution(mesh):
    dp, rep = mesh.devices.shape
    split = jax.sharding.Mesh(
        mesh.devices.reshape(dp // 2, 2, rep // 2, 2), ("zx", "core", "yhi", "ylo")
    )
    everyone = ("zx", "core", "yhi", "ylo")
    owners = ("zx", "core")
    placed = (P(everyone, None), P(), P(everyone), P(), P(owners))
    return jax.shard_map(
        shards,
        mesh=split,
        in_specs=placed,
        out_specs=(P(owners), P(everyone, None)),
        check_vma=False,
    )
```

```python
import math

import jax
import jax.numpy as jnp
from jax import lax
from jax.experimental import pallas as pl
from jax.experimental.pallas import tpu as pltpu
from jax.sharding import PartitionSpec as P

BR = 128
PAIRS_REP = 2
REPS = 4

logit_sharpness = 0.05
objective_factor = 32.0
norm_eps = 1e-06

BF = jnp.bfloat16
F32 = jnp.float32
I32 = jnp.int32
VMEM_BYTES = 24 * 1024 * 1024


AXES = ("z", "x", "core", "yhi", "ylo")
DISPATCH = ("core", "x", "yhi", "ylo", "z")
FETCH = ("ylo", "x", "z")
REDUCE = ("x", "yhi", "ylo", "z")


def position(order, sizes, place):
    at = 0
    for axis in order:
        at = at * sizes[axis] + place[axis]
    return at


def params():
    return pltpu.CompilerParams(vmem_limit_bytes=VMEM_BYTES)


def cost(us):
    return pl.CostEstimate(flops=int(us * 1e9), bytes_accessed=int(us * 1e6), transcendentals=0)


def iota(shape, dim):
    return lax.broadcasted_iota(I32, shape, dim)


def hot(mask):
    return jnp.where(mask, 1.0, 0.0).astype(BF)


def dot(a, b, ca=1, cb=0):
    return lax.dot_general(a, b, (((ca,), (cb,)), ((), ())), preferred_element_type=F32)


def sds(shape, dtype):
    return jax.ShapeDtypeStruct(shape, dtype)


def column_of(rows):
    wide = jnp.concatenate([rows] * (BR // rows.shape[0]), axis=0)
    return wide.T[:, 0:1].astype(I32)


def project_kernel(
    owner_slots, sizes, cap, slot, feat_in, head_in, send, unit, norm, place, feat, head, kept, sems
):
    n = feat.shape[0]
    width, e = head.shape
    parts = 4
    depth = width // parts
    copies = []
    for k in range(parts):
        at = pl.ds(k * depth, depth)
        copies.append(pltpu.make_async_copy(head_in.at[at, :], head.at[at, :], sems.at[k]))
        copies.append(pltpu.make_async_copy(feat_in.at[:, at], feat.at[:, at], sems.at[parts + k]))
    for c in copies:
        c.start()
    s = slot[...]
    owner = s // owner_slots
    local = s - owner * owner_slots
    owners = sizes["z"] * sizes["x"] * 2
    mine = iota((owners, n), 0) == owner
    before = dot(hot(mine), hot(iota((n, n), 0) < iota((n, n), 1)))
    rank = jnp.sum(jnp.where(mine, before, 0.0), axis=0, keepdims=True).astype(I32)
    member = rank & (REPS - 1)
    slab = member & 1
    column = owner // 2
    z = column // sizes["x"]
    place_of = dict(
        z=z, x=column - z * sizes["x"], core=member // 2, yhi=slab, ylo=(owner & 1) ^ slab
    )
    device = position(DISPATCH, sizes, place_of)
    p = device * cap + rank // REPS
    place[...] = jnp.broadcast_to(p.astype(F32), place.shape)
    scatter = hot(iota((send.shape[0], n), 0) == p)
    high = local // BR
    low = local - high * BR
    row = iota((BR, n), 0)
    tags = jnp.where(row == 0, high, jnp.where(row == 1, low, jnp.where(row == 2, 1, 0)))
    send[:, e:] = dot(scatter, tags.astype(F32).astype(BF), 1, 1).astype(BF)
    projected = jnp.zeros((n, e), F32)
    for k in range(parts):
        copies[2 * k].wait()
        copies[2 * k + 1].wait()
        at = slice(k * depth, (k + 1) * depth)
        projected += dot(feat[:, at], head[at, :])
    length = jnp.sqrt(jnp.sum(projected * projected, axis=1, keepdims=True) + norm_eps)
    rows = projected / length
    kept[...] = rows
    keep = pltpu.make_async_copy(kept, unit, sems.at[2 * parts])
    keep.start()
    norm[...] = jnp.broadcast_to(length, norm.shape)
    send[:, :e] = dot(scatter, rows.astype(BF)).astype(BF)
    keep.wait()


def stripes_kernel(sizes, core, feat, mine, other):
    first = core[0] == 0
    half = BR // 2
    rows = half // REPS
    for column in range(feat.shape[1] // BR):
        t = feat[:, column * BR : (column + 1) * BR].astype(F32).T
        a, b = t[:half, :], t[half:, :]
        here, there = jnp.where(first, a, b).astype(BF), jnp.where(first, b, a).astype(BF)
        z, x = divmod(column, sizes["x"])
        for y in range(REPS):
            at = position(REDUCE, sizes, dict(z=z, x=x, yhi=y // 2, ylo=y % 2)) * rows
            mine[at : at + rows, :] = here[y * rows : (y + 1) * rows, :]
            other[at : at + rows, :] = there[y * rows : (y + 1) * rows, :]


def compact_kernel(got, packed, place):
    count = got.shape[0]
    e = packed.shape[1]
    rows = packed.shape[0] - 16
    tags = got[:, e:].astype(F32).T
    valid = tags[2:3, :]
    upper = hot(iota((count, count), 0) < iota((count, count), 1))
    before = dot(jnp.broadcast_to(valid, (16, count)).astype(BF), upper)[0:1, :]
    pos = jnp.where(valid > 0.5, before, -1.0)
    place[...] = jnp.broadcast_to(pos, place.shape)
    pick = hot(iota((rows, count), 0) == pos.astype(I32))
    packed[:rows, :] = dot(pick, got[:, :e]).astype(BF)
    packed[rows:, :] = dot(tags[:16, :].astype(BF), pick, 1, 1).astype(BF)


def slot_row(tag):
    tag = tag.astype(F32)
    return tag[0:1, :] * BR + tag[1:2, :]


def place_rows(out, pieces, start, after=None):
    step = 2 * BR

    def body(i, carry):
        base = pl.multiple_of(i * step, step)
        total = None if start is None else start[pl.ds(base, step), :].astype(F32)
        for ids, rows in pieces:
            at = iota((step, rows.shape[0]), 0) + base
            part = dot(hot(at == ids), rows)
            total = part if total is None else total + part
        out[pl.ds(base, step), :] = total.astype(BF)
        if after is not None:
            after(i)
        return carry

    lax.fori_loop(0, out.shape[0] // step, body, 0)


def near_kernel(own, beside, partial, slots):
    n = own.shape[0] - 16
    pieces = []
    for k, ref in enumerate((own, beside)):
        row = slot_row(ref[n:, :])
        slots[k, :, :] = jnp.broadcast_to(row, slots.shape[1:])
        pieces.append((row.astype(I32), ref[:n, :]))
    place_rows(partial, pieces, None)


def middle_kernel(begun, across, partial, slots):
    n = across.shape[0] - 16
    row = slot_row(across[n:, :])
    slots[...] = jnp.broadcast_to(row, slots.shape)
    place_rows(partial, [(row.astype(I32), across[:n, :])], begun)


def far_kernel(serve, order, ready, begun, corner, anchors, served, slots, sems):
    n = corner.shape[0] - 16
    row = slot_row(corner[n:, :])
    slots[...] = jnp.broadcast_to(row, slots.shape)

    def copy(d):
        start = pl.multiple_of(serve[d] * BR, BR)
        return pltpu.make_async_copy(anchors.at[pl.ds(start, BR), :], served.at[d], sems.at[d])

    def begin(j, carry):
        copy(order[j]).start()
        return carry

    def after(i):
        lax.fori_loop(ready[i], ready[i + 1], begin, 0)

    place_rows(anchors, [(row.astype(I32), corner[:n, :])], begun, after)

    def finish(d, carry):
        copy(d).wait()
        return carry

    lax.fori_loop(0, served.shape[0], finish, 0)


def scores_kernel(need, column, anchors, fetched, weights, stats, partners, sem):
    load = pltpu.make_async_copy(fetched, partners, sem)
    load.start()
    blocks = weights.shape[0]
    load.wait()

    def body(i, carry):
        for j in range(4):
            b = i * 4 + j
            q = anchors[pl.ds(pl.multiple_of(b * BR, BR), BR), :]
            total = jnp.zeros((1, BR), F32)
            positive = jnp.zeros((1, BR), F32)
            want = column[pl.ds(b, 1), :]
            for k in range(PAIRS_REP):
                logits = dot(partners[need[b * PAIRS_REP + k]], q, 1, 1) / logit_sharpness
                hit = iota((BR, BR), 0) + k * BR == want
                w = jnp.where(hit, 0.0, jnp.exp(logits - 1.0 / logit_sharpness))
                weights[b, k * BR : (k + 1) * BR, :] = w.astype(BF)
                total += jnp.sum(w, axis=0, keepdims=True)
                positive += jnp.sum(jnp.where(hit, logits, 0.0), axis=0, keepdims=True)
            stats[pl.ds(b, 1), :] = total
            stats[pl.ds(blocks + b, 1), :] = positive
        return carry

    lax.fori_loop(0, blocks // 4, body, 0)


def mix_kernel(need, column, weights, partners, pulled, partner):
    blocks = weights.shape[0]

    def body(i, carry):
        for j in range(4):
            b = i * 4 + j
            w = weights[b]
            hit = hot(iota(w.shape, 0) == column[pl.ds(b, 1), :])
            pair = [partners[need[b * PAIRS_REP + k]] for k in range(PAIRS_REP)]
            both = dot(jnp.concatenate([w, hit], axis=1), jnp.concatenate(pair, axis=0), 0, 0)
            at = pl.ds(pl.multiple_of(b * BR, BR), BR)
            pulled[at, :] = both[:BR, :].astype(BF)
            partner[at, :] = both[BR:, :].astype(BF)
        return carry

    lax.fori_loop(0, blocks // 4, body, 0)


def pick_rows(out, rows, ids):
    step = 256
    for h in range(out.shape[0] // step):
        pick = hot(iota((step, rows.shape[0]), 1) == ids[h * step : (h + 1) * step, :])
        out[h * step : (h + 1) * step, :] = dot(pick, rows[...]).astype(BF)


def shares_kernel(factor, s0, s1, s2, s3, pulled, partner, slots, share, out):
    blocks = s0.shape[0] // 2
    stats = (s0[...] + s3[...]) + (s1[...] + s2[...])
    rest, matching = stats[:blocks, :], stats[blocks:, :]
    total = rest + jnp.exp(matching - 1.0 / logit_sharpness)
    scale = jnp.concatenate([factor / total, factor * (rest / total)], axis=0)
    scale = jnp.concatenate([scale] * (BR // (2 * blocks)), axis=0).T
    for b in range(blocks):
        at = slice(b * BR, (b + 1) * BR)
        grad = pulled[at, :].astype(F32) * scale[:, b : b + 1]
        grad -= partner[at, :].astype(F32) * scale[:, blocks + b : blocks + b + 1]
        share[at, :] = grad.astype(BF)
    pick_rows(out, share, column_of(slots[...]))


def pick_kernel(share, slots, out):
    pick_rows(out, share, column_of(slots[...]))


def back_kernel(a, b, c, place, back):
    total = a[...].astype(F32) + b[...].astype(F32) + c[...].astype(F32)
    rows = a.shape[0]
    pos = column_of(place[...])
    back[...] = dot(hot(iota((back.shape[0], rows), 1) == pos), total.astype(BF)).astype(BF)


def unit_grad_kernel(got, place, unit, norm, out, kept, sem):
    fetch = pltpu.make_async_copy(unit, kept, sem)
    fetch.start()
    n = norm.shape[0]
    grad = dot(hot(iota((n, got.shape[0]), 1) == column_of(place[...])), got[...])
    fetch.wait()
    rows = kept[...]
    radial = jnp.sum(rows * grad, axis=1, keepdims=True)
    out[...] = ((grad - rows * radial) / norm[:, 0:1]).astype(BF)


def head_begun_kernel(mine, grad, out):
    step = 256
    for i in range(out.shape[0] // step):
        at = slice(i * step, (i + 1) * step)
        out[at, :] = dot(mine[at, :], grad[...])


def head_grad_kernel(begun, theirs, partner, out):
    step = 256
    for i in range(out.shape[0] // step):
        at = slice(i * step, (i + 1) * step)
        out[at, :] = (begun[at, :] + dot(theirs[at, :], partner[...])).astype(BF)


def sum_kernel(parts, out):
    out[...] = jnp.sum(parts[...].astype(F32), axis=0)


def swap(x, axes=("core",)):
    size = 2 ** len(axes)
    return lax.ppermute(x, axes, [(i, size - 1 - i) for i in range(size)])


def exchange(x, axes):
    return lax.all_to_all(x, axes, 0, 0, tiled=True)


def shards(features, head_weight, slot_of_image, candidates, positives):
    sizes = {axis: lax.axis_size(axis) for axis in AXES}
    dp = sizes["z"] * sizes["x"] * 2
    slab = lax.axis_index("yhi")
    me = (lax.axis_index("z") * sizes["x"] + lax.axis_index("x")) * 2
    me = me + (lax.axis_index("ylo") ^ slab)
    core = lax.axis_index("core")
    member = core * 2 + slab
    home = core == (me & 1)
    n, width = features.shape
    e = head_weight.shape[1]
    devices = dp * REPS
    owner_slots = n * REPS
    blocks = owner_slots // BR
    cap = 2 * n // devices
    count = devices * cap
    factor = objective_factor / (logit_sharpness * math.sqrt(n * devices))
    vmem = pl.BlockSpec(memory_space=pltpu.VMEM)
    smem = pl.BlockSpec(memory_space=pltpu.SMEM)
    far_away = pl.BlockSpec(memory_space=pl.ANY)

    def call(kernel, name, shapes, args, **more):
        return pl.pallas_call(
            kernel, out_shape=shapes, compiler_params=params(), name=name, **more
        )(*args)

    send, unit, norm, place = call(
        lambda *r: project_kernel(owner_slots, sizes, cap, *r),
        "project",
        (sds((count, e + BR), BF), pltpu.HBM((n, e), F32), sds((n, BR), F32), sds((8, n), F32)),
        (
            slot_of_image.reshape(1, n),
            pltpu.with_memory_space_constraint(features, pltpu.HBM),
            pltpu.with_memory_space_constraint(head_weight, pltpu.HBM),
        ),
        in_specs=[vmem, far_away, far_away],
        out_specs=(vmem, far_away, vmem, vmem),
        scratch_shapes=[
            pltpu.VMEM((n, width), BF),
            pltpu.VMEM((width, e), BF),
            pltpu.VMEM((n, e), F32),
            pltpu.SemaphoreType.DMA((9,)),
        ],
    )
    got = exchange(send.reshape(devices, cap, e + BR), DISPATCH).reshape(count, e + BR)

    mine, other = call(
        lambda *r: stripes_kernel(sizes, *r),
        "stripes",
        (sds((width // 2, n), BF),) * 2,
        (core.reshape(1), features),
        in_specs=[smem, vmem],
    )
    theirs = swap(other)

    table = candidates.reshape(dp, blocks, REPS, PAIRS_REP)
    table = lax.dynamic_index_in_dim(table, member, axis=2, keepdims=False)
    table = table.reshape(dp, blocks * PAIRS_REP)
    owner = table // blocks
    numbers = jnp.arange(dp, dtype=I32)
    wanted = jnp.sum(jnp.where(owner == me, table - owner * blocks, 0), axis=1)

    def fetch_place(number):
        column = number // 2
        z = column // sizes["x"]
        x = column - z * sizes["x"]
        return position(FETCH, sizes, dict(z=z, x=x, ylo=(number & 1) ^ slab))

    serve = jnp.sum(
        jnp.where(fetch_place(numbers)[None, :] == numbers[:, None], wanted[None, :], 0), axis=1
    )
    need = fetch_place(lax.dynamic_index_in_dim(owner, me, axis=0, keepdims=False))
    column = jnp.where(home, positives, swap(positives)).reshape(blocks, BR)
    column = column - member * (PAIRS_REP * BR)
    keys = serve * dp + numbers
    place_of = jnp.sum((keys[None, :] < keys[:, None]).astype(I32), axis=1)
    order = jnp.sum(jnp.where(place_of[None, :] == numbers[:, None], numbers[None, :], 0), axis=1)
    bounds = 2 * jnp.arange(blocks // 2 + 1, dtype=I32)
    ready = jnp.sum((serve[None, :] < bounds[:, None]).astype(I32), axis=1)

    got, serve, order, ready, need = lax.optimization_barrier((got, serve, order, ready, need))
    packed, back_place = call(
        compact_kernel, "compact", (sds((n + 16, e), BF), sds((8, count), F32)), (got,)
    )
    beside = swap(packed)
    across = swap(packed, ("yhi", "ylo"))

    whole = sds((owner_slots, e), BF)
    ids_shape = sds((8, n), F32)
    partial, slots = call(
        near_kernel,
        "near",
        (whole, sds((2, 8, n), F32)),
        (packed, beside),
        cost_estimate=cost(4),
    )
    partial, across = lax.optimization_barrier((partial, across))
    corner = swap(across)
    partial, slots_across = call(middle_kernel, "middle", (whole, ids_shape), (partial, across))
    anchors, served, slots_corner = call(
        far_kernel,
        "far",
        (whole, pltpu.HBM((dp, BR, e), BF), ids_shape),
        (serve, order, ready, partial, corner),
        in_specs=[smem] * 3 + [vmem] * 2,
        out_specs=(vmem, pl.BlockSpec(memory_space=pltpu.HBM), vmem),
        scratch_shapes=[pltpu.SemaphoreType.DMA((dp,))],
    )
    fetched = exchange(served, FETCH)
    weights, stats, partners = call(
        scores_kernel,
        "scores",
        (
            sds((blocks, PAIRS_REP * BR, BR), BF),
            sds((2 * blocks, BR), F32),
            sds((dp, BR, e), BF),
        ),
        (need, column, anchors, fetched),
        in_specs=[smem, vmem, vmem, far_away],
        scratch_shapes=[pltpu.SemaphoreType.DMA],
    )
    spread = (stats, swap(stats), swap(stats, ("yhi", "ylo")), swap(stats, ("core", "yhi", "ylo")))
    pulled, partner = call(
        mix_kernel,
        "mix",
        (sds((owner_slots, e), BF),) * 2,
        (need, column, weights, partners),
        in_specs=[smem] + [vmem] * 3,
    )
    share, for_corner = call(
        lambda *r: shares_kernel(factor, *r),
        "shares",
        (whole, sds((n, e), BF)),
        (*spread, pulled, partner, slots_corner),
    )

    def pick(name, rows, ids):
        return call(
            pick_kernel, name, sds((n, e), BF), (rows, ids), cost_estimate=cost(0.01)
        )

    for_across = pick("across", share, slots_across).astype(F32) + swap(for_corner).astype(F32)
    from_across = swap(for_across.astype(BF), ("yhi", "ylo"))
    from_beside = swap(pick("beside", share, slots[1]))
    back = call(
        back_kernel,
        "back",
        pltpu.HBM((count, e), BF),
        (pick("own", share, slots[0]), from_beside, from_across, back_place),
    )
    returned = exchange(back.reshape(devices, cap, e), DISPATCH).reshape(count, e)

    both = (spread[0] + spread[3]) + (spread[1] + spread[2])
    rest, matching = both[:blocks], both[blocks:]
    total = rest + jnp.exp(matching - 1.0 / logit_sharpness)
    loss = (jnp.log(total) + 1.0 / logit_sharpness - matching).reshape(owner_slots)
    anchor_row_loss = jnp.where(home, loss, swap(loss, ("ylo",)))

    grad = call(
        unit_grad_kernel,
        "unit_grad",
        sds((n, e), BF),
        (returned, place, pltpu.with_memory_space_constraint(unit, pltpu.HBM), norm),
        in_specs=[vmem, vmem, far_away, vmem],
        scratch_shapes=[pltpu.VMEM((n, e), F32), pltpu.SemaphoreType.DMA],
    )
    begun = call(head_begun_kernel, "head_begun", sds((width // 2, e), F32), (mine, grad))
    partial = call(
        head_grad_kernel,
        "head_grad",
        pltpu.HBM((width // 2, e), BF),
        (begun, theirs, swap(grad)),
    )
    parts = exchange(partial.reshape(devices // 2, width // devices, e), REDUCE)
    weight_grad = call(sum_kernel, "add", sds((width // devices, e), F32), (parts,))
    return (anchor_row_loss, weight_grad)


def solution(mesh):
    dp, rep = mesh.devices.shape
    z = x = math.isqrt(dp // 2)
    split = jax.sharding.Mesh(mesh.devices.reshape(z, x, 2, rep // 2, 2), AXES)
    owners = ("z", "x", "core")
    placed = (P(AXES, None), P(), P(AXES), P(), P(owners))
    return jax.shard_map(
        shards,
        mesh=split,
        in_specs=placed,
        out_specs=(P(owners), P(AXES, None)),
        check_vma=False,
    )
```

```python
import math

import jax
import jax.numpy as jnp
from jax import lax
from jax.experimental import pallas as pl
from jax.experimental.pallas import tpu as pltpu
from jax.sharding import PartitionSpec as P

BR = 128
PAIRS_REP = 2
REPS = 4

logit_sharpness = 0.05
objective_factor = 32.0
norm_eps = 1e-06

BF = jnp.bfloat16
F32 = jnp.float32
I32 = jnp.int32
VMEM_BYTES = 24 * 1024 * 1024


AXES = ("z", "x", "core", "yhi", "ylo")
DISPATCH = ("core", "x", "yhi", "ylo", "z")
FETCH = ("ylo", "x", "z")
REDUCE = ("x", "yhi", "ylo", "z")


def position(order, sizes, place):
    at = 0
    for axis in order:
        at = at * sizes[axis] + place[axis]
    return at


def params():
    return pltpu.CompilerParams(vmem_limit_bytes=VMEM_BYTES)


def cost(us):
    return pl.CostEstimate(flops=int(us * 1e9), bytes_accessed=int(us * 1e6), transcendentals=0)


def iota(shape, dim):
    return lax.broadcasted_iota(I32, shape, dim)


def hot(mask):
    return jnp.where(mask, 1.0, 0.0).astype(BF)


def dot(a, b, ca=1, cb=0):
    return lax.dot_general(a, b, (((ca,), (cb,)), ((), ())), preferred_element_type=F32)


def sds(shape, dtype):
    return jax.ShapeDtypeStruct(shape, dtype)


def column_of(rows):
    wide = jnp.concatenate([rows] * (BR // rows.shape[0]), axis=0)
    return wide.T[:, 0:1].astype(I32)


def project_kernel(
    owner_slots, sizes, cap, slot, feat_in, head_in, send, unit, norm, place, feat, head, kept, sems
):
    n = feat.shape[0]
    width, e = head.shape
    parts = 4
    depth = width // parts
    copies = []
    for k in range(parts):
        at = pl.ds(k * depth, depth)
        copies.append(pltpu.make_async_copy(head_in.at[at, :], head.at[at, :], sems.at[k]))
        copies.append(pltpu.make_async_copy(feat_in.at[:, at], feat.at[:, at], sems.at[parts + k]))
    for c in copies:
        c.start()
    s = slot[...]
    owner = s // owner_slots
    local = s - owner * owner_slots
    owners = sizes["z"] * sizes["x"] * 2
    mine = iota((owners, n), 0) == owner
    before = dot(hot(mine), hot(iota((n, n), 0) < iota((n, n), 1)))
    rank = jnp.sum(jnp.where(mine, before, 0.0), axis=0, keepdims=True).astype(I32)
    member = rank & (REPS - 1)
    slab = member & 1
    column = owner // 2
    z = column // sizes["x"]
    place_of = dict(
        z=z, x=column - z * sizes["x"], core=member // 2, yhi=slab, ylo=(owner & 1) ^ slab
    )
    device = position(DISPATCH, sizes, place_of)
    p = device * cap + rank // REPS
    place[...] = jnp.broadcast_to(p.astype(F32), place.shape)
    scatter = hot(iota((send.shape[0], n), 0) == p)
    high = local // BR
    low = local - high * BR
    row = iota((BR, n), 0)
    tags = jnp.where(row == 0, high, jnp.where(row == 1, low, jnp.where(row == 2, 1, 0)))
    send[:, e:] = dot(scatter, tags.astype(F32).astype(BF), 1, 1).astype(BF)
    projected = jnp.zeros((n, e), F32)
    for k in range(parts):
        copies[2 * k].wait()
        copies[2 * k + 1].wait()
        at = slice(k * depth, (k + 1) * depth)
        projected += dot(feat[:, at], head[at, :])
    length = jnp.sqrt(jnp.sum(projected * projected, axis=1, keepdims=True) + norm_eps)
    rows = projected / length
    kept[...] = rows
    keep = pltpu.make_async_copy(kept, unit, sems.at[2 * parts])
    keep.start()
    norm[...] = jnp.broadcast_to(length, norm.shape)
    send[:, :e] = dot(scatter, rows.astype(BF)).astype(BF)
    keep.wait()


def stripes_kernel(sizes, core, feat, mine, other):
    first = core[0] == 0
    half = BR // 2
    rows = half // REPS
    for column in range(feat.shape[1] // BR):
        t = feat[:, column * BR : (column + 1) * BR].astype(F32).T
        a, b = t[:half, :], t[half:, :]
        here, there = jnp.where(first, a, b).astype(BF), jnp.where(first, b, a).astype(BF)
        z, x = divmod(column, sizes["x"])
        for y in range(REPS):
            at = position(REDUCE, sizes, dict(z=z, x=x, yhi=y // 2, ylo=y % 2)) * rows
            mine[at : at + rows, :] = here[y * rows : (y + 1) * rows, :]
            other[at : at + rows, :] = there[y * rows : (y + 1) * rows, :]


def compact_kernel(got, positives, packed, place):
    count = got.shape[0]
    e = packed.shape[1]
    rows = packed.shape[0] - 16
    tags = got[:, e:].astype(F32).T
    valid = tags[2:3, :]
    upper = hot(iota((count, count), 0) < iota((count, count), 1))
    before = dot(jnp.broadcast_to(valid, (16, count)).astype(BF), upper)[0:1, :]
    pos = jnp.where(valid > 0.5, before, -1.0)
    place[...] = jnp.broadcast_to(pos, place.shape)
    pick = hot(iota((rows, count), 0) == pos.astype(I32))
    packed[:rows, :] = dot(pick, got[:, :e]).astype(BF)
    slot = dot(tags[:16, :].astype(BF), pick, 1, 1)
    high = positives[...] // BR
    low = positives[...] - high * BR
    spare = [slot[:4, :], high.astype(F32), low.astype(F32), jnp.zeros((4, e), F32)]
    packed[rows:, :] = jnp.concatenate(spare, axis=0).astype(BF)


def slot_row(tag):
    tag = tag.astype(F32)
    return tag[0:1, :] * BR + tag[1:2, :]


def place_rows(out, pieces, start, after=None):
    step = 2 * BR

    def body(i, carry):
        base = pl.multiple_of(i * step, step)
        total = None if start is None else start[pl.ds(base, step), :].astype(F32)
        for ids, rows in pieces:
            at = iota((step, rows.shape[0]), 0) + base
            part = dot(hot(at == ids), rows)
            total = part if total is None else total + part
        out[pl.ds(base, step), :] = total.astype(BF)
        if after is not None:
            after(i)
        return carry

    lax.fori_loop(0, out.shape[0] // step, body, 0)


def near_kernel(own, beside, partial, slots, positives):
    n = own.shape[0] - 16
    pieces = []
    for k, ref in enumerate((own, beside)):
        row = slot_row(ref[n:, :])
        slots[k, :, :] = jnp.broadcast_to(row, slots.shape[1:])
        pieces.append((row.astype(I32), ref[:n, :]))
    place_rows(partial, pieces, None)
    spare = beside[n:, :].astype(F32)
    digits = (spare[4:8, :] * BR + spare[8:12, :]).astype(I32)
    lanes = digits.shape[1] // BR
    for i in range(positives.shape[0]):
        at = slice((i % lanes) * BR, (i % lanes + 1) * BR)
        positives[i : i + 1, :] = digits[i // lanes : i // lanes + 1, at]


def middle_kernel(begun, across, partial, slots):
    n = across.shape[0] - 16
    row = slot_row(across[n:, :])
    slots[...] = jnp.broadcast_to(row, slots.shape)
    place_rows(partial, [(row.astype(I32), across[:n, :])], begun)


def far_kernel(serve, order, ready, begun, corner, anchors, served, slots, sems):
    n = corner.shape[0] - 16
    row = slot_row(corner[n:, :])
    slots[...] = jnp.broadcast_to(row, slots.shape)

    def copy(d):
        start = pl.multiple_of(serve[d] * BR, BR)
        return pltpu.make_async_copy(anchors.at[pl.ds(start, BR), :], served.at[d], sems.at[d])

    def begin(j, carry):
        copy(order[j]).start()
        return carry

    def after(i):
        lax.fori_loop(ready[i], ready[i + 1], begin, 0)

    place_rows(anchors, [(row.astype(I32), corner[:n, :])], begun, after)

    def finish(d, carry):
        copy(d).wait()
        return carry

    lax.fori_loop(0, served.shape[0], finish, 0)


def scores_kernel(need, column, anchors, fetched, weights, stats, partners, sem):
    load = pltpu.make_async_copy(fetched, partners, sem)
    load.start()
    blocks = weights.shape[0]
    load.wait()

    def body(i, carry):
        for j in range(4):
            b = i * 4 + j
            q = anchors[pl.ds(pl.multiple_of(b * BR, BR), BR), :]
            total = jnp.zeros((1, BR), F32)
            positive = jnp.zeros((1, BR), F32)
            want = column[pl.ds(b, 1), :]
            for k in range(PAIRS_REP):
                logits = dot(partners[need[b * PAIRS_REP + k]], q, 1, 1) / logit_sharpness
                hit = iota((BR, BR), 0) + k * BR == want
                w = jnp.where(hit, 0.0, jnp.exp(logits - 1.0 / logit_sharpness))
                weights[b, k * BR : (k + 1) * BR, :] = w.astype(BF)
                total += jnp.sum(w, axis=0, keepdims=True)
                positive += jnp.sum(jnp.where(hit, logits, 0.0), axis=0, keepdims=True)
            stats[pl.ds(b, 1), :] = total
            stats[pl.ds(blocks + b, 1), :] = positive
        return carry

    lax.fori_loop(0, blocks // 4, body, 0)


def mix_kernel(need, column, weights, partners, pulled, partner):
    blocks = weights.shape[0]

    def body(i, carry):
        for j in range(4):
            b = i * 4 + j
            w = weights[b]
            hit = hot(iota(w.shape, 0) == column[pl.ds(b, 1), :])
            pair = [partners[need[b * PAIRS_REP + k]] for k in range(PAIRS_REP)]
            both = dot(jnp.concatenate([w, hit], axis=1), jnp.concatenate(pair, axis=0), 0, 0)
            at = pl.ds(pl.multiple_of(b * BR, BR), BR)
            pulled[at, :] = both[:BR, :].astype(BF)
            partner[at, :] = both[BR:, :].astype(BF)
        return carry

    lax.fori_loop(0, blocks // 4, body, 0)


def pick_rows(out, rows, ids):
    step = 256
    for h in range(out.shape[0] // step):
        pick = hot(iota((step, rows.shape[0]), 1) == ids[h * step : (h + 1) * step, :])
        out[h * step : (h + 1) * step, :] = dot(pick, rows[...]).astype(BF)


def shares_kernel(factor, s0, s1, s2, s3, pulled, partner, slots, share, out):
    blocks = s0.shape[0] // 2
    stats = (s0[...] + s3[...]) + (s1[...] + s2[...])
    rest, matching = stats[:blocks, :], stats[blocks:, :]
    total = rest + jnp.exp(matching - 1.0 / logit_sharpness)
    scale = jnp.concatenate([factor / total, factor * (rest / total)], axis=0)
    scale = jnp.concatenate([scale] * (BR // (2 * blocks)), axis=0).T
    for b in range(blocks):
        at = slice(b * BR, (b + 1) * BR)
        grad = pulled[at, :].astype(F32) * scale[:, b : b + 1]
        grad -= partner[at, :].astype(F32) * scale[:, blocks + b : blocks + b + 1]
        share[at, :] = grad.astype(BF)
    pick_rows(out, share, column_of(slots[...]))


def pick_kernel(share, slots, out):
    pick_rows(out, share, column_of(slots[...]))


def back_kernel(a, b, c, place, back):
    total = a[...].astype(F32) + b[...].astype(F32) + c[...].astype(F32)
    rows = a.shape[0]
    pos = column_of(place[...])
    back[...] = dot(hot(iota((back.shape[0], rows), 1) == pos), total.astype(BF)).astype(BF)


def unit_grad_kernel(got, place, unit, norm, out, kept, sem):
    fetch = pltpu.make_async_copy(unit, kept, sem)
    fetch.start()
    n = norm.shape[0]
    grad = dot(hot(iota((n, got.shape[0]), 1) == column_of(place[...])), got[...])
    fetch.wait()
    rows = kept[...]
    radial = jnp.sum(rows * grad, axis=1, keepdims=True)
    out[...] = ((grad - rows * radial) / norm[:, 0:1]).astype(BF)


def head_begun_kernel(mine, grad, out):
    step = 256
    for i in range(out.shape[0] // step):
        at = slice(i * step, (i + 1) * step)
        out[at, :] = dot(mine[at, :], grad[...])


def head_grad_kernel(begun, theirs, partner, out):
    step = 256
    for i in range(out.shape[0] // step):
        at = slice(i * step, (i + 1) * step)
        out[at, :] = (begun[at, :] + dot(theirs[at, :], partner[...])).astype(BF)


def sum_kernel(parts, out):
    out[...] = jnp.sum(parts[...].astype(F32), axis=0)


def swap(x, axes=("core",)):
    size = 2 ** len(axes)
    return lax.ppermute(x, axes, [(i, size - 1 - i) for i in range(size)])


def exchange(x, axes):
    return lax.all_to_all(x, axes, 0, 0, tiled=True)


def shards(features, head_weight, slot_of_image, candidates, positives):
    sizes = {axis: lax.axis_size(axis) for axis in AXES}
    dp = sizes["z"] * sizes["x"] * 2
    slab = lax.axis_index("yhi")
    me = (lax.axis_index("z") * sizes["x"] + lax.axis_index("x")) * 2
    me = me + (lax.axis_index("ylo") ^ slab)
    core = lax.axis_index("core")
    member = core * 2 + slab
    home = core == (me & 1)
    n, width = features.shape
    e = head_weight.shape[1]
    devices = dp * REPS
    owner_slots = n * REPS
    blocks = owner_slots // BR
    cap = 2 * n // devices
    count = devices * cap
    factor = objective_factor / (logit_sharpness * math.sqrt(n * devices))
    vmem = pl.BlockSpec(memory_space=pltpu.VMEM)
    smem = pl.BlockSpec(memory_space=pltpu.SMEM)
    far_away = pl.BlockSpec(memory_space=pl.ANY)

    def call(kernel, name, shapes, args, **more):
        return pl.pallas_call(
            kernel, out_shape=shapes, compiler_params=params(), name=name, **more
        )(*args)

    send, unit, norm, place = call(
        lambda *r: project_kernel(owner_slots, sizes, cap, *r),
        "project",
        (sds((count, e + BR), BF), pltpu.HBM((n, e), F32), sds((n, BR), F32), sds((8, n), F32)),
        (
            slot_of_image.reshape(1, n),
            pltpu.with_memory_space_constraint(features, pltpu.HBM),
            pltpu.with_memory_space_constraint(head_weight, pltpu.HBM),
        ),
        in_specs=[vmem, far_away, far_away],
        out_specs=(vmem, far_away, vmem, vmem),
        scratch_shapes=[
            pltpu.VMEM((n, width), BF),
            pltpu.VMEM((width, e), BF),
            pltpu.VMEM((n, e), F32),
            pltpu.SemaphoreType.DMA((9,)),
        ],
    )
    got = exchange(send.reshape(devices, cap, e + BR), DISPATCH).reshape(count, e + BR)

    mine, other = call(
        lambda *r: stripes_kernel(sizes, *r),
        "stripes",
        (sds((width // 2, n), BF),) * 2,
        (core.reshape(1), features),
        in_specs=[smem, vmem],
    )
    theirs = swap(other)

    table = candidates.reshape(dp, blocks, REPS, PAIRS_REP)
    table = lax.dynamic_index_in_dim(table, member, axis=2, keepdims=False)
    table = table.reshape(dp, blocks * PAIRS_REP)
    owner = table // blocks
    numbers = jnp.arange(dp, dtype=I32)
    wanted = jnp.sum(jnp.where(owner == me, table - owner * blocks, 0), axis=1)

    def fetch_place(number):
        column = number // 2
        z = column // sizes["x"]
        x = column - z * sizes["x"]
        return position(FETCH, sizes, dict(z=z, x=x, ylo=(number & 1) ^ slab))

    serve = jnp.sum(
        jnp.where(fetch_place(numbers)[None, :] == numbers[:, None], wanted[None, :], 0), axis=1
    )
    need = fetch_place(lax.dynamic_index_in_dim(owner, me, axis=0, keepdims=False))
    keys = serve * dp + numbers
    place_of = jnp.sum((keys[None, :] < keys[:, None]).astype(I32), axis=1)
    order = jnp.sum(jnp.where(place_of[None, :] == numbers[:, None], numbers[None, :], 0), axis=1)
    bounds = 2 * jnp.arange(blocks // 2 + 1, dtype=I32)
    ready = jnp.sum((serve[None, :] < bounds[:, None]).astype(I32), axis=1)

    got, serve, order, ready, need = lax.optimization_barrier((got, serve, order, ready, need))
    packed, back_place = call(
        compact_kernel, "compact", (sds((n + 16, e), BF), sds((8, count), F32)), (got, positives.reshape(4, e))
    )
    beside = swap(packed)
    across = swap(packed, ("yhi", "ylo"))

    whole = sds((owner_slots, e), BF)
    ids_shape = sds((8, n), F32)
    partial, slots, other_positives = call(
        near_kernel,
        "near",
        (whole, sds((2, 8, n), F32), sds((blocks, BR), I32)),
        (packed, beside),
        cost_estimate=cost(4),
    )
    partial, across = lax.optimization_barrier((partial, across))
    column = jnp.where(home, positives.reshape(blocks, BR), other_positives)
    column = column - member * (PAIRS_REP * BR)
    corner = swap(across)
    partial, slots_across = call(middle_kernel, "middle", (whole, ids_shape), (partial, across))
    anchors, served, slots_corner = call(
        far_kernel,
        "far",
        (whole, pltpu.HBM((dp, BR, e), BF), ids_shape),
        (serve, order, ready, partial, corner),
        in_specs=[smem] * 3 + [vmem] * 2,
        out_specs=(vmem, pl.BlockSpec(memory_space=pltpu.HBM), vmem),
        scratch_shapes=[pltpu.SemaphoreType.DMA((dp,))],
    )
    fetched = exchange(served, FETCH)
    weights, stats, partners = call(
        scores_kernel,
        "scores",
        (
            sds((blocks, PAIRS_REP * BR, BR), BF),
            sds((2 * blocks, BR), F32),
            sds((dp, BR, e), BF),
        ),
        (need, column, anchors, fetched),
        in_specs=[smem, vmem, vmem, far_away],
        scratch_shapes=[pltpu.SemaphoreType.DMA],
    )
    spread = (stats, swap(stats), swap(stats, ("yhi", "ylo")), swap(stats, ("core", "yhi", "ylo")))
    pulled, partner = call(
        mix_kernel,
        "mix",
        (sds((owner_slots, e), BF),) * 2,
        (need, column, weights, partners),
        in_specs=[smem] + [vmem] * 3,
    )
    share, for_corner = call(
        lambda *r: shares_kernel(factor, *r),
        "shares",
        (whole, sds((n, e), BF)),
        (*spread, pulled, partner, slots_corner),
    )

    def pick(name, rows, ids):
        return call(
            pick_kernel, name, sds((n, e), BF), (rows, ids), cost_estimate=cost(0.01)
        )

    for_across = pick("across", share, slots_across).astype(F32) + swap(for_corner).astype(F32)
    from_across = swap(for_across.astype(BF), ("yhi", "ylo"))
    from_beside = swap(pick("beside", share, slots[1]))
    back = call(
        back_kernel,
        "back",
        pltpu.HBM((count, e), BF),
        (pick("own", share, slots[0]), from_beside, from_across, back_place),
    )
    returned = exchange(back.reshape(devices, cap, e), DISPATCH).reshape(count, e)

    both = (spread[0] + spread[3]) + (spread[1] + spread[2])
    rest, matching = both[:blocks], both[blocks:]
    total = rest + jnp.exp(matching - 1.0 / logit_sharpness)
    loss = (jnp.log(total) + 1.0 / logit_sharpness - matching).reshape(owner_slots)
    anchor_row_loss = jnp.where(home, loss, swap(loss, ("ylo",)))

    grad = call(
        unit_grad_kernel,
        "unit_grad",
        sds((n, e), BF),
        (returned, place, pltpu.with_memory_space_constraint(unit, pltpu.HBM), norm),
        in_specs=[vmem, vmem, far_away, vmem],
        scratch_shapes=[pltpu.VMEM((n, e), F32), pltpu.SemaphoreType.DMA],
    )
    begun = call(head_begun_kernel, "head_begun", sds((width // 2, e), F32), (mine, grad))
    partial = call(
        head_grad_kernel,
        "head_grad",
        pltpu.HBM((width // 2, e), BF),
        (begun, theirs, swap(grad)),
    )
    parts = exchange(partial.reshape(devices // 2, width // devices, e), REDUCE)
    weight_grad = call(sum_kernel, "add", sds((width // devices, e), F32), (parts,))
    return (anchor_row_loss, weight_grad)


def solution(mesh):
    dp, rep = mesh.devices.shape
    z = x = math.isqrt(dp // 2)
    split = jax.sharding.Mesh(mesh.devices.reshape(z, x, 2, rep // 2, 2), AXES)
    owners = ("z", "x", "core")
    placed = (P(AXES, None), P(), P(AXES), P(), P(owners))
    return jax.shard_map(
        shards,
        mesh=split,
        in_specs=placed,
        out_specs=(P(owners), P(AXES, None)),
        check_vma=False,
    )
```

```python
import math

import jax
import jax.numpy as jnp
from jax import lax
from jax.experimental import pallas as pl
from jax.experimental.pallas import tpu as pltpu
from jax.sharding import PartitionSpec as P

BR = 128
PAIRS_REP = 2
REPS = 4

logit_sharpness = 0.05
objective_factor = 32.0
norm_eps = 1e-06

BF = jnp.bfloat16
F32 = jnp.float32
I32 = jnp.int32
VMEM_BYTES = 24 * 1024 * 1024


AXES = ("z", "x", "core", "yhi", "ylo")
DISPATCH = ("core", "x", "yhi", "ylo", "z")
FETCH = ("ylo", "x", "z")
REDUCE = ("x", "yhi", "ylo", "z")


def position(order, sizes, place):
    at = 0
    for axis in order:
        at = at * sizes[axis] + place[axis]
    return at


def params():
    return pltpu.CompilerParams(vmem_limit_bytes=VMEM_BYTES)


def cost(us):
    return pl.CostEstimate(flops=int(us * 1e9), bytes_accessed=int(us * 1e6), transcendentals=0)


def iota(shape, dim):
    return lax.broadcasted_iota(I32, shape, dim)


def hot(mask):
    return jnp.where(mask, 1.0, 0.0).astype(BF)


def dot(a, b, ca=1, cb=0):
    return lax.dot_general(a, b, (((ca,), (cb,)), ((), ())), preferred_element_type=F32)


def sds(shape, dtype):
    return jax.ShapeDtypeStruct(shape, dtype)


def column_of(rows):
    wide = jnp.concatenate([rows] * (BR // rows.shape[0]), axis=0)
    return wide.T[:, 0:1].astype(I32)


def project_kernel(
    owner_slots, sizes, cap, slot, feat_in, head_in, send, unit, norm, place, feat, head, kept, sems
):
    n = feat.shape[0]
    width, e = head.shape
    parts = 4
    depth = width // parts
    copies = []
    for k in range(parts):
        at = pl.ds(k * depth, depth)
        copies.append(pltpu.make_async_copy(head_in.at[at, :], head.at[at, :], sems.at[k]))
        copies.append(pltpu.make_async_copy(feat_in.at[:, at], feat.at[:, at], sems.at[parts + k]))
    for c in copies:
        c.start()
    s = slot[...]
    owner = s // owner_slots
    local = s - owner * owner_slots
    owners = sizes["z"] * sizes["x"] * 2
    mine = iota((owners, n), 0) == owner
    before = dot(hot(mine), hot(iota((n, n), 0) < iota((n, n), 1)))
    rank = jnp.sum(jnp.where(mine, before, 0.0), axis=0, keepdims=True).astype(I32)
    member = rank & (REPS - 1)
    slab = member & 1
    column = owner // 2
    z = column // sizes["x"]
    place_of = dict(
        z=z, x=column - z * sizes["x"], core=member // 2, yhi=slab, ylo=(owner & 1) ^ slab
    )
    device = position(DISPATCH, sizes, place_of)
    p = device * cap + rank // REPS
    place[...] = jnp.broadcast_to(p.astype(F32), place.shape)
    scatter = hot(iota((send.shape[0], n), 0) == p)
    high = local // BR
    low = local - high * BR
    row = iota((BR, n), 0)
    tags = jnp.where(row == 0, high, jnp.where(row == 1, low, jnp.where(row == 2, 1, 0)))
    send[:, e:] = dot(scatter, tags.astype(F32).astype(BF), 1, 1).astype(BF)
    projected = jnp.zeros((n, e), F32)
    for k in range(parts):
        copies[2 * k].wait()
        copies[2 * k + 1].wait()
        at = slice(k * depth, (k + 1) * depth)
        projected += dot(feat[:, at], head[at, :])
    length = jnp.sqrt(jnp.sum(projected * projected, axis=1, keepdims=True) + norm_eps)
    rows = projected / length
    kept[...] = rows
    keep = pltpu.make_async_copy(kept, unit, sems.at[2 * parts])
    keep.start()
    norm[...] = jnp.broadcast_to(length, norm.shape)
    send[:, :e] = dot(scatter, rows.astype(BF)).astype(BF)
    keep.wait()


def stripes_kernel(sizes, core, feat, mine, other):
    first = core[0] == 0
    half = BR // 2
    rows = half // REPS
    for column in range(feat.shape[1] // BR):
        t = feat[:, column * BR : (column + 1) * BR].astype(F32).T
        a, b = t[:half, :], t[half:, :]
        here, there = jnp.where(first, a, b).astype(BF), jnp.where(first, b, a).astype(BF)
        z, x = divmod(column, sizes["x"])
        for y in range(REPS):
            at = position(REDUCE, sizes, dict(z=z, x=x, yhi=y // 2, ylo=y % 2)) * rows
            mine[at : at + rows, :] = here[y * rows : (y + 1) * rows, :]
            other[at : at + rows, :] = there[y * rows : (y + 1) * rows, :]


def compact_kernel(got, positives, packed, place):
    count = got.shape[0]
    e = packed.shape[1]
    rows = packed.shape[0] - 16
    tags = got[:, e:].astype(F32).T
    valid = tags[2:3, :]
    upper = hot(iota((count, count), 0) < iota((count, count), 1))
    before = dot(jnp.broadcast_to(valid, (16, count)).astype(BF), upper)[0:1, :]
    pos = jnp.where(valid > 0.5, before, -1.0)
    place[...] = jnp.broadcast_to(pos, place.shape)
    pick = hot(iota((rows, count), 0) == pos.astype(I32))
    packed[:rows, :] = dot(pick, got[:, :e]).astype(BF)
    slot = dot(tags[:16, :].astype(BF), pick, 1, 1)
    high = positives[...] // BR
    low = positives[...] - high * BR
    spare = [slot[:4, :], high.astype(F32), low.astype(F32), jnp.zeros((4, e), F32)]
    packed[rows:, :] = jnp.concatenate(spare, axis=0).astype(BF)


def slot_row(tag):
    tag = tag.astype(F32)
    return tag[0:1, :] * BR + tag[1:2, :]


def place_rows(out, pieces, start, after=None):
    step = 2 * BR

    def body(i, carry):
        base = pl.multiple_of(i * step, step)
        total = None if start is None else start[pl.ds(base, step), :].astype(F32)
        for ids, rows in pieces:
            at = iota((step, rows.shape[0]), 0) + base
            part = dot(hot(at == ids), rows)
            total = part if total is None else total + part
        out[pl.ds(base, step), :] = total.astype(BF)
        if after is not None:
            after(i)
        return carry

    lax.fori_loop(0, out.shape[0] // step, body, 0)


def near_kernel(own, beside, partial, slots, positives):
    n = own.shape[0] - 16
    pieces = []
    for k, ref in enumerate((own, beside)):
        row = slot_row(ref[n:, :])
        slots[k, :, :] = jnp.broadcast_to(row, slots.shape[1:])
        pieces.append((row.astype(I32), ref[:n, :]))
    place_rows(partial, pieces, None)
    spare = beside[n:, :].astype(F32)
    digits = (spare[4:8, :] * BR + spare[8:12, :]).astype(I32)
    lanes = digits.shape[1] // BR
    for i in range(positives.shape[0]):
        at = slice((i % lanes) * BR, (i % lanes + 1) * BR)
        positives[i : i + 1, :] = digits[i // lanes : i // lanes + 1, at]


def middle_kernel(begun, across, partial, slots):
    n = across.shape[0] - 16
    row = slot_row(across[n:, :])
    slots[...] = jnp.broadcast_to(row, slots.shape)
    place_rows(partial, [(row.astype(I32), across[:n, :])], begun)


def far_kernel(serve, order, ready, begun, corner, anchors, served, slots, sems):
    n = corner.shape[0] - 16
    row = slot_row(corner[n:, :])
    slots[...] = jnp.broadcast_to(row, slots.shape)

    def copy(d):
        start = pl.multiple_of(serve[d] * BR, BR)
        return pltpu.make_async_copy(anchors.at[pl.ds(start, BR), :], served.at[d], sems.at[d])

    def begin(j, carry):
        copy(order[j]).start()
        return carry

    def after(i):
        lax.fori_loop(ready[i], ready[i + 1], begin, 0)

    place_rows(anchors, [(row.astype(I32), corner[:n, :])], begun, after)

    def finish(d, carry):
        copy(d).wait()
        return carry

    lax.fori_loop(0, served.shape[0], finish, 0)


def scores_kernel(need, column, anchors, fetched, weights, stats, partners, sem):
    load = pltpu.make_async_copy(fetched, partners, sem)
    load.start()
    blocks = weights.shape[0]
    load.wait()

    def body(i, carry):
        for j in range(4):
            b = i * 4 + j
            q = anchors[pl.ds(pl.multiple_of(b * BR, BR), BR), :]
            total = jnp.zeros((1, BR), F32)
            positive = jnp.zeros((1, BR), F32)
            want = column[pl.ds(b, 1), :]
            for k in range(PAIRS_REP):
                logits = dot(partners[need[b * PAIRS_REP + k]], q, 1, 1) / logit_sharpness
                hit = iota((BR, BR), 0) + k * BR == want
                w = jnp.where(hit, 0.0, jnp.exp(logits - 1.0 / logit_sharpness))
                weights[b, k * BR : (k + 1) * BR, :] = w.astype(BF)
                total += jnp.sum(w, axis=0, keepdims=True)
                positive += jnp.sum(jnp.where(hit, logits, 0.0), axis=0, keepdims=True)
            stats[pl.ds(b, 1), :] = total
            stats[pl.ds(blocks + b, 1), :] = positive
        return carry

    lax.fori_loop(0, blocks // 4, body, 0)


def mix_kernel(need, column, weights, partners, pulled, partner):
    blocks = weights.shape[0]

    def body(i, carry):
        for j in range(4):
            b = i * 4 + j
            w = weights[b]
            hit = hot(iota(w.shape, 0) == column[pl.ds(b, 1), :])
            pair = [partners[need[b * PAIRS_REP + k]] for k in range(PAIRS_REP)]
            both = dot(jnp.concatenate([w, hit], axis=1), jnp.concatenate(pair, axis=0), 0, 0)
            at = pl.ds(pl.multiple_of(b * BR, BR), BR)
            pulled[at, :] = both[:BR, :].astype(BF)
            partner[at, :] = both[BR:, :].astype(BF)
        return carry

    lax.fori_loop(0, blocks // 4, body, 0)


def pick_rows(out, rows, ids):
    step = 256
    for h in range(out.shape[0] // step):
        pick = hot(iota((step, rows.shape[0]), 1) == ids[h * step : (h + 1) * step, :])
        out[h * step : (h + 1) * step, :] = dot(pick, rows[...]).astype(BF)


def shares_kernel(factor, s0, s1, s2, s3, pulled, partner, slots, share, out):
    blocks = s0.shape[0] // 2
    stats = (s0[...] + s3[...]) + (s1[...] + s2[...])
    rest, matching = stats[:blocks, :], stats[blocks:, :]
    total = rest + jnp.exp(matching - 1.0 / logit_sharpness)
    scale = jnp.concatenate([factor / total, factor * (rest / total)], axis=0)
    scale = jnp.concatenate([scale] * (BR // (2 * blocks)), axis=0).T
    for b in range(blocks):
        at = slice(b * BR, (b + 1) * BR)
        grad = pulled[at, :].astype(F32) * scale[:, b : b + 1]
        grad -= partner[at, :].astype(F32) * scale[:, blocks + b : blocks + b + 1]
        share[at, :] = grad.astype(BF)
    pick_rows(out, share, column_of(slots[...]))


def pick_kernel(share, slots, out):
    pick_rows(out, share, column_of(slots[...]))


def back_kernel(a, b, c, place, back):
    total = a[...].astype(F32) + b[...].astype(F32) + c[...].astype(F32)
    rows = a.shape[0]
    pos = column_of(place[...])
    back[...] = dot(hot(iota((back.shape[0], rows), 1) == pos), total.astype(BF)).astype(BF)


def unit_grad_kernel(got, place, unit, norm, out, kept, sem):
    fetch = pltpu.make_async_copy(unit, kept, sem)
    fetch.start()
    n = norm.shape[0]
    grad = dot(hot(iota((n, got.shape[0]), 1) == column_of(place[...])), got[...])
    fetch.wait()
    rows = kept[...]
    radial = jnp.sum(rows * grad, axis=1, keepdims=True)
    out[...] = ((grad - rows * radial) / norm[:, 0:1]).astype(BF)


def head_begun_kernel(mine, grad, out):
    step = 256
    for i in range(out.shape[0] // step):
        at = slice(i * step, (i + 1) * step)
        out[at, :] = dot(mine[at, :], grad[...])


def head_grad_kernel(begun, theirs, partner, out):
    step = 256
    for i in range(out.shape[0] // step):
        at = slice(i * step, (i + 1) * step)
        out[at, :] = (begun[at, :] + dot(theirs[at, :], partner[...])).astype(BF)


def sum_kernel(parts, out):
    out[...] = jnp.sum(parts[...].astype(F32), axis=0)


def swap(x, axes=("core",)):
    size = 2 ** len(axes)
    return lax.ppermute(x, axes, [(i, size - 1 - i) for i in range(size)])


def exchange(x, axes):
    return lax.all_to_all(x, axes, 0, 0, tiled=True)


def shards(features, head_weight, slot_of_image, candidates, positives):
    sizes = {axis: lax.axis_size(axis) for axis in AXES}
    dp = sizes["z"] * sizes["x"] * 2
    slab = lax.axis_index("yhi")
    me = (lax.axis_index("z") * sizes["x"] + lax.axis_index("x")) * 2
    me = me + (lax.axis_index("ylo") ^ slab)
    core = lax.axis_index("core")
    member = core * 2 + slab
    home = core == (me & 1)
    n, width = features.shape
    e = head_weight.shape[1]
    devices = dp * REPS
    owner_slots = n * REPS
    blocks = owner_slots // BR
    cap = 2 * n // devices
    count = devices * cap
    factor = objective_factor / (logit_sharpness * math.sqrt(n * devices))
    vmem = pl.BlockSpec(memory_space=pltpu.VMEM)
    smem = pl.BlockSpec(memory_space=pltpu.SMEM)
    far_away = pl.BlockSpec(memory_space=pl.ANY)

    def call(kernel, name, shapes, args, **more):
        return pl.pallas_call(
            kernel, out_shape=shapes, compiler_params=params(), name=name, **more
        )(*args)

    send, unit, norm, place = call(
        lambda *r: project_kernel(owner_slots, sizes, cap, *r),
        "project",
        (sds((count, e + BR), BF), pltpu.HBM((n, e), F32), sds((n, BR), F32), sds((8, n), F32)),
        (
            slot_of_image.reshape(1, n),
            pltpu.with_memory_space_constraint(features, pltpu.HBM),
            pltpu.with_memory_space_constraint(head_weight, pltpu.HBM),
        ),
        in_specs=[vmem, far_away, far_away],
        out_specs=(vmem, far_away, vmem, vmem),
        scratch_shapes=[
            pltpu.VMEM((n, width), BF),
            pltpu.VMEM((width, e), BF),
            pltpu.VMEM((n, e), F32),
            pltpu.SemaphoreType.DMA((9,)),
        ],
    )
    send, late_features = lax.optimization_barrier((send, features))
    mine, other = call(
        lambda *r: stripes_kernel(sizes, *r),
        "stripes",
        (sds((width // 2, n), BF),) * 2,
        (core.reshape(1), late_features),
        in_specs=[smem, vmem],
    )
    got = exchange(send.reshape(devices, cap, e + BR), DISPATCH).reshape(count, e + BR)
    theirs = swap(other)

    table = candidates.reshape(dp, blocks, REPS, PAIRS_REP)
    table = lax.dynamic_index_in_dim(table, member, axis=2, keepdims=False)
    table = table.reshape(dp, blocks * PAIRS_REP)
    owner = table // blocks
    numbers = jnp.arange(dp, dtype=I32)
    wanted = jnp.sum(jnp.where(owner == me, table - owner * blocks, 0), axis=1)

    def fetch_place(number):
        column = number // 2
        z = column // sizes["x"]
        x = column - z * sizes["x"]
        return position(FETCH, sizes, dict(z=z, x=x, ylo=(number & 1) ^ slab))

    serve = jnp.sum(
        jnp.where(fetch_place(numbers)[None, :] == numbers[:, None], wanted[None, :], 0), axis=1
    )
    need = fetch_place(lax.dynamic_index_in_dim(owner, me, axis=0, keepdims=False))
    keys = serve * dp + numbers
    place_of = jnp.sum((keys[None, :] < keys[:, None]).astype(I32), axis=1)
    order = jnp.sum(jnp.where(place_of[None, :] == numbers[:, None], numbers[None, :], 0), axis=1)
    bounds = 2 * jnp.arange(blocks // 2 + 1, dtype=I32)
    ready = jnp.sum((serve[None, :] < bounds[:, None]).astype(I32), axis=1)

    got, serve, order, ready, need, mine, theirs = lax.optimization_barrier(
        (got, serve, order, ready, need, mine, theirs)
    )
    packed, back_place = call(
        compact_kernel, "compact", (sds((n + 16, e), BF), sds((8, count), F32)), (got, positives.reshape(4, e))
    )
    beside = swap(packed)
    across = swap(packed, ("yhi", "ylo"))

    whole = sds((owner_slots, e), BF)
    ids_shape = sds((8, n), F32)
    partial, slots, other_positives = call(
        near_kernel,
        "near",
        (whole, sds((2, 8, n), F32), sds((blocks, BR), I32)),
        (packed, beside),
        cost_estimate=cost(4),
    )
    column = jnp.where(home, positives.reshape(blocks, BR), other_positives)
    column = column - member * (PAIRS_REP * BR)
    partial, across, column = lax.optimization_barrier((partial, across, column))
    corner = swap(across)
    partial, slots_across = call(middle_kernel, "middle", (whole, ids_shape), (partial, across))
    anchors, served, slots_corner = call(
        far_kernel,
        "far",
        (whole, pltpu.HBM((dp, BR, e), BF), ids_shape),
        (serve, order, ready, partial, corner),
        in_specs=[smem] * 3 + [vmem] * 2,
        out_specs=(vmem, pl.BlockSpec(memory_space=pltpu.HBM), vmem),
        scratch_shapes=[pltpu.SemaphoreType.DMA((dp,))],
    )
    fetched = exchange(served, FETCH)
    weights, stats, partners = call(
        scores_kernel,
        "scores",
        (
            sds((blocks, PAIRS_REP * BR, BR), BF),
            sds((2 * blocks, BR), F32),
            sds((dp, BR, e), BF),
        ),
        (need, column, anchors, fetched),
        in_specs=[smem, vmem, vmem, far_away],
        scratch_shapes=[pltpu.SemaphoreType.DMA],
    )
    spread = (stats, swap(stats), swap(stats, ("yhi", "ylo")), swap(stats, ("core", "yhi", "ylo")))
    pulled, partner = call(
        mix_kernel,
        "mix",
        (sds((owner_slots, e), BF),) * 2,
        (need, column, weights, partners),
        in_specs=[smem] + [vmem] * 3,
    )
    share, for_corner = call(
        lambda *r: shares_kernel(factor, *r),
        "shares",
        (whole, sds((n, e), BF)),
        (*spread, pulled, partner, slots_corner),
    )

    def pick(name, rows, ids):
        return call(
            pick_kernel, name, sds((n, e), BF), (rows, ids), cost_estimate=cost(0.01)
        )

    for_across = pick("across", share, slots_across).astype(F32) + swap(for_corner).astype(F32)
    from_across = swap(for_across.astype(BF), ("yhi", "ylo"))
    own = pick("own", share, slots[0])
    from_beside = swap(pick("beside", share, slots[1]))
    both = (spread[0] + spread[3]) + (spread[1] + spread[2])
    rest, matching = both[:blocks], both[blocks:]
    total = rest + jnp.exp(matching - 1.0 / logit_sharpness)
    loss = (jnp.log(total) + 1.0 / logit_sharpness - matching).reshape(owner_slots)
    anchor_row_loss = jnp.where(home, loss, swap(loss, ("ylo",)))
    own, from_beside, anchor_row_loss = lax.optimization_barrier(
        (own, from_beside, anchor_row_loss)
    )
    back = call(
        back_kernel,
        "back",
        pltpu.HBM((count, e), BF),
        (own, from_beside, from_across, back_place),
    )
    returned = exchange(back.reshape(devices, cap, e), DISPATCH).reshape(count, e)

    grad = call(
        unit_grad_kernel,
        "unit_grad",
        sds((n, e), BF),
        (returned, place, pltpu.with_memory_space_constraint(unit, pltpu.HBM), norm),
        in_specs=[vmem, vmem, far_away, vmem],
        scratch_shapes=[pltpu.VMEM((n, e), F32), pltpu.SemaphoreType.DMA],
    )
    begun = call(head_begun_kernel, "head_begun", sds((width // 2, e), F32), (mine, grad))
    partial = call(
        head_grad_kernel,
        "head_grad",
        pltpu.HBM((width // 2, e), BF),
        (begun, theirs, swap(grad)),
    )
    parts = exchange(partial.reshape(devices // 2, width // devices, e), REDUCE)
    weight_grad = call(sum_kernel, "add", sds((width // devices, e), F32), (parts,))
    return (anchor_row_loss, weight_grad)


def solution(mesh):
    dp, rep = mesh.devices.shape
    z = x = math.isqrt(dp // 2)
    split = jax.sharding.Mesh(mesh.devices.reshape(z, x, 2, rep // 2, 2), AXES)
    owners = ("z", "x", "core")
    placed = (P(AXES, None), P(), P(AXES), P(), P(owners))
    return jax.shard_map(
        shards,
        mesh=split,
        in_specs=placed,
        out_specs=(P(owners), P(AXES, None)),
        check_vma=False,
    )
```

```python
import math

import jax
import jax.numpy as jnp
from jax import lax
from jax.experimental import pallas as pl
from jax.experimental.pallas import tpu as pltpu
from jax.sharding import PartitionSpec as P

BR = 128
PAIRS_REP = 2
REPS = 4

logit_sharpness = 0.05
objective_factor = 32.0
norm_eps = 1e-06

BF = jnp.bfloat16
F32 = jnp.float32
I32 = jnp.int32
VMEM_BYTES = 24 * 1024 * 1024


AXES = ("z", "x", "core", "yhi", "ylo")
DISPATCH = ("core", "x", "yhi", "ylo", "z")
FETCH = ("ylo", "x", "z")
REDUCE = ("x", "yhi", "ylo", "z")


def position(order, sizes, place):
    at = 0
    for axis in order:
        at = at * sizes[axis] + place[axis]
    return at


def params():
    return pltpu.CompilerParams(vmem_limit_bytes=VMEM_BYTES)


def cost(us):
    return pl.CostEstimate(flops=int(us * 1e9), bytes_accessed=int(us * 1e6), transcendentals=0)


def iota(shape, dim):
    return lax.broadcasted_iota(I32, shape, dim)


def hot(mask):
    return jnp.where(mask, 1.0, 0.0).astype(BF)


def dot(a, b, ca=1, cb=0):
    return lax.dot_general(a, b, (((ca,), (cb,)), ((), ())), preferred_element_type=F32)


def sds(shape, dtype):
    return jax.ShapeDtypeStruct(shape, dtype)


def column_of(rows):
    return float_column_of(rows).astype(I32)


def float_column_of(rows):
    wide = jnp.concatenate([rows] * (BR // rows.shape[0]), axis=0)
    return wide.T[:, 0:1]


def project_kernel(
    owner_slots, sizes, cap, slot, feat_in, head_in, sent, unit, place, feat, head, kept, send, sems
):
    n = feat.shape[0]
    width, e = head.shape
    parts = 4
    depth = width // parts
    copies = []
    for k in range(parts):
        at = pl.ds(k * depth, depth)
        copies.append(pltpu.make_async_copy(head_in.at[at, :], head.at[at, :], sems.at[k]))
        copies.append(pltpu.make_async_copy(feat_in.at[:, at], feat.at[:, at], sems.at[parts + k]))
    for c in copies:
        c.start()
    s = slot[...]
    owner = s // owner_slots
    local = s - owner * owner_slots
    owners = sizes["z"] * sizes["x"] * 2
    mine = iota((owners, n), 0) == owner
    before = dot(hot(mine), hot(iota((n, n), 0) < iota((n, n), 1)))
    rank = jnp.sum(jnp.where(mine, before, 0.0), axis=0, keepdims=True).astype(I32)
    member = rank & (REPS - 1)
    slab = member & 1
    column = owner // 2
    z = column // sizes["x"]
    place_of = dict(
        z=z, x=column - z * sizes["x"], core=member // 2, yhi=slab, ylo=(owner & 1) ^ slab
    )
    device = position(DISPATCH, sizes, place_of)
    p = device * cap + rank // REPS
    place[:8, :] = jnp.broadcast_to(p.astype(F32), (8, n))
    scatter = hot(iota((send.shape[0], n), 0) == p)
    high = local // BR
    low = local - high * BR
    row = iota((BR, n), 0)
    tags = jnp.where(row == 0, high, jnp.where(row == 1, low, jnp.where(row == 2, 1, 0)))
    send[:, e:] = dot(scatter, tags.astype(F32).astype(BF), 1, 1).astype(BF)
    projected = jnp.zeros((n, e), F32)
    for k in range(parts):
        copies[2 * k].wait()
        copies[2 * k + 1].wait()
        at = slice(k * depth, (k + 1) * depth)
        projected += dot(feat[:, at], head[at, :])
    length = jnp.sqrt(jnp.sum(projected * projected, axis=1, keepdims=True) + norm_eps)
    rows = projected / length
    kept[...] = rows
    keep = pltpu.make_async_copy(kept, unit, sems.at[2 * parts])
    keep.start()
    place[8:, :] = jnp.broadcast_to(length, (n, BR)).T[:8, :]
    descriptor = rows.astype(BF)
    step = send.shape[0] // parts
    leave = []
    for k in range(parts):
        at = slice(k * step, (k + 1) * step)
        send[at, :e] = dot(scatter[at, :], descriptor).astype(BF)
        at = pl.ds(k * step, step)
        leave.append(
            pltpu.make_async_copy(send.at[at, :], sent.at[at, :], sems.at[2 * parts + 1 + k])
        )
        leave[-1].start()
    keep.wait()
    for c in leave:
        c.wait()


def stripes_kernel(sizes, core, feat, mine, other):
    first = core[0] == 0
    half = BR // 2
    rows = half // REPS
    for column in range(feat.shape[1] // BR):
        t = feat[:, column * BR : (column + 1) * BR].astype(F32).T
        a, b = t[:half, :], t[half:, :]
        here, there = jnp.where(first, a, b).astype(BF), jnp.where(first, b, a).astype(BF)
        z, x = divmod(column, sizes["x"])
        for y in range(REPS):
            at = position(REDUCE, sizes, dict(z=z, x=x, yhi=y // 2, ylo=y % 2)) * rows
            mine[at : at + rows, :] = here[y * rows : (y + 1) * rows, :]
            other[at : at + rows, :] = there[y * rows : (y + 1) * rows, :]


def compact_kernel(got, positives, packed, place):
    count = got.shape[0]
    e = packed.shape[1]
    rows = packed.shape[0] - 16
    tags = got[:, e:].astype(F32).T
    valid = tags[2:3, :]
    upper = hot(iota((count, count), 0) < iota((count, count), 1))
    before = dot(jnp.broadcast_to(valid, (16, count)).astype(BF), upper)[0:1, :]
    pos = jnp.where(valid > 0.5, before, -1.0)
    place[...] = jnp.broadcast_to(pos, place.shape)
    pick = hot(iota((rows, count), 0) == pos.astype(I32))
    packed[:rows, :] = dot(pick, got[:, :e]).astype(BF)
    slot = dot(tags[:16, :].astype(BF), pick, 1, 1)
    high = positives[...] // BR
    low = positives[...] - high * BR
    spare = [slot[:4, :], high.astype(F32), low.astype(F32), jnp.zeros((4, e), F32)]
    packed[rows:, :] = jnp.concatenate(spare, axis=0).astype(BF)


def slot_row(tag):
    tag = tag.astype(F32)
    return tag[0:1, :] * BR + tag[1:2, :]


def place_rows(out, pieces, start, after=None):
    step = 2 * BR

    def body(i, carry):
        base = pl.multiple_of(i * step, step)
        total = None if start is None else start[pl.ds(base, step), :].astype(F32)
        for ids, rows in pieces:
            at = iota((step, rows.shape[0]), 0) + base
            part = dot(hot(at == ids), rows)
            total = part if total is None else total + part
        out[pl.ds(base, step), :] = total.astype(BF)
        if after is not None:
            after(i)
        return carry

    lax.fori_loop(0, out.shape[0] // step, body, 0)


def near_kernel(own, beside, partial, slots, positives):
    n = own.shape[0] - 16
    pieces = []
    for k, ref in enumerate((own, beside)):
        row = slot_row(ref[n:, :])
        slots[k, :, :] = jnp.broadcast_to(row, slots.shape[1:])
        pieces.append((row.astype(I32), ref[:n, :]))
    place_rows(partial, pieces, None)
    spare = beside[n:, :].astype(F32)
    digits = (spare[4:8, :] * BR + spare[8:12, :]).astype(I32)
    lanes = digits.shape[1] // BR
    for i in range(positives.shape[0]):
        at = slice((i % lanes) * BR, (i % lanes + 1) * BR)
        positives[i : i + 1, :] = digits[i // lanes : i // lanes + 1, at]


def middle_kernel(begun, across, partial, slots):
    n = across.shape[0] - 16
    row = slot_row(across[n:, :])
    slots[...] = jnp.broadcast_to(row, slots.shape)
    place_rows(partial, [(row.astype(I32), across[:n, :])], begun)


def far_kernel(serve, order, ready, begun, corner, anchors, served, slots, sems):
    n = corner.shape[0] - 16
    row = slot_row(corner[n:, :])
    slots[...] = jnp.broadcast_to(row, slots.shape)

    def copy(d):
        start = pl.multiple_of(serve[d] * BR, BR)
        return pltpu.make_async_copy(anchors.at[pl.ds(start, BR), :], served.at[d], sems.at[d])

    def begin(j, carry):
        copy(order[j]).start()
        return carry

    def after(i):
        lax.fori_loop(ready[i], ready[i + 1], begin, 0)

    place_rows(anchors, [(row.astype(I32), corner[:n, :])], begun, after)

    def finish(d, carry):
        copy(d).wait()
        return carry

    lax.fori_loop(0, served.shape[0], finish, 0)


def scores_kernel(need, column, anchors, partners, weights, stats):
    blocks = weights.shape[0]

    def body(i, carry):
        for j in range(4):
            b = i * 4 + j
            q = anchors[pl.ds(pl.multiple_of(b * BR, BR), BR), :]
            total = jnp.zeros((1, BR), F32)
            positive = jnp.zeros((1, BR), F32)
            want = column[pl.ds(b, 1), :]
            for k in range(PAIRS_REP):
                logits = dot(partners[need[b * PAIRS_REP + k]], q, 1, 1) / logit_sharpness
                hit = iota((BR, BR), 0) + k * BR == want
                w = jnp.where(hit, 0.0, jnp.exp(logits - 1.0 / logit_sharpness))
                weights[b, k * BR : (k + 1) * BR, :] = w.astype(BF)
                total += jnp.sum(w, axis=0, keepdims=True)
                positive += jnp.sum(jnp.where(hit, logits, 0.0), axis=0, keepdims=True)
            stats[pl.ds(b, 1), :] = total
            stats[pl.ds(blocks + b, 1), :] = positive
        return carry

    lax.fori_loop(0, blocks // 4, body, 0)


def mix_kernel(need, column, weights, partners, pulled, partner):
    blocks = weights.shape[0]

    def body(i, carry):
        for j in range(4):
            b = i * 4 + j
            w = weights[b]
            hit = hot(iota(w.shape, 0) == column[pl.ds(b, 1), :])
            pair = [partners[need[b * PAIRS_REP + k]] for k in range(PAIRS_REP)]
            both = dot(jnp.concatenate([w, hit], axis=1), jnp.concatenate(pair, axis=0), 0, 0)
            at = pl.ds(pl.multiple_of(b * BR, BR), BR)
            pulled[at, :] = both[:BR, :].astype(BF)
            partner[at, :] = both[BR:, :].astype(BF)
        return carry

    lax.fori_loop(0, blocks // 4, body, 0)


def pick_rows(out, rows, ids):
    step = 256
    for h in range(out.shape[0] // step):
        pick = hot(iota((step, rows.shape[0]), 1) == ids[h * step : (h + 1) * step, :])
        out[h * step : (h + 1) * step, :] = dot(pick, rows[...]).astype(BF)


def shares_kernel(factor, s0, s1, s2, s3, pulled, partner, slots, share, out):
    blocks = s0.shape[0] // 2
    stats = (s0[...] + s3[...]) + (s1[...] + s2[...])
    rest, matching = stats[:blocks, :], stats[blocks:, :]
    total = rest + jnp.exp(matching - 1.0 / logit_sharpness)
    scale = jnp.concatenate([factor / total, factor * (rest / total)], axis=0)
    scale = jnp.concatenate([scale] * (BR // (2 * blocks)), axis=0).T
    for b in range(blocks):
        at = slice(b * BR, (b + 1) * BR)
        grad = pulled[at, :].astype(F32) * scale[:, b : b + 1]
        grad -= partner[at, :].astype(F32) * scale[:, blocks + b : blocks + b + 1]
        share[at, :] = grad.astype(BF)
    pick_rows(out, share, column_of(slots[...]))


def pick_kernel(share, slots, out):
    pick_rows(out, share, column_of(slots[...]))


def chip_kernel(own, beside, place, total, pick):
    total[...] = own[...].astype(F32) + beside[...].astype(F32)
    pick[...] = hot(iota(pick.shape, 1) == column_of(place[...]))


def back_kernel(chip, across, pick, back):
    total = chip[...] + across[...].astype(F32)
    back[...] = dot(pick[...], total.astype(BF)).astype(BF)


def unit_grad_kernel(got, place, unit, out, kept, sem):
    fetch = pltpu.make_async_copy(unit, kept, sem)
    fetch.start()
    n = out.shape[0]
    grad = dot(hot(iota((n, got.shape[0]), 1) == column_of(place[:8, :])), got[...])
    fetch.wait()
    rows = kept[...]
    radial = jnp.sum(rows * grad, axis=1, keepdims=True)
    out[...] = ((grad - rows * radial) / float_column_of(place[8:, :])).astype(BF)


def head_begun_kernel(mine, grad, out):
    step = 256
    for i in range(out.shape[0] // step):
        at = slice(i * step, (i + 1) * step)
        out[at, :] = dot(mine[at, :], grad[...])


def head_grad_kernel(begun, theirs, partner, out):
    step = 256
    for i in range(out.shape[0] // step):
        at = slice(i * step, (i + 1) * step)
        out[at, :] = (begun[at, :] + dot(theirs[at, :], partner[...])).astype(BF)


def sum_kernel(parts, out):
    out[...] = jnp.sum(parts[...].astype(F32), axis=0)


def swap(x, axes=("core",)):
    size = 2 ** len(axes)
    return lax.ppermute(x, axes, [(i, size - 1 - i) for i in range(size)])


def exchange(x, axes):
    return lax.all_to_all(x, axes, 0, 0, tiled=True)


def shards(features, head_weight, slot_of_image, candidates, positives):
    sizes = {axis: lax.axis_size(axis) for axis in AXES}
    dp = sizes["z"] * sizes["x"] * 2
    slab = lax.axis_index("yhi")
    me = (lax.axis_index("z") * sizes["x"] + lax.axis_index("x")) * 2
    me = me + (lax.axis_index("ylo") ^ slab)
    core = lax.axis_index("core")
    member = core * 2 + slab
    home = core == (me & 1)
    n, width = features.shape
    e = head_weight.shape[1]
    devices = dp * REPS
    owner_slots = n * REPS
    blocks = owner_slots // BR
    cap = 2 * n // devices
    count = devices * cap
    factor = objective_factor / (logit_sharpness * math.sqrt(n * devices))
    vmem = pl.BlockSpec(memory_space=pltpu.VMEM)
    smem = pl.BlockSpec(memory_space=pltpu.SMEM)
    far_away = pl.BlockSpec(memory_space=pl.ANY)

    def call(kernel, name, shapes, args, **more):
        return pl.pallas_call(
            kernel, out_shape=shapes, compiler_params=params(), name=name, **more
        )(*args)

    send, unit, place = call(
        lambda *r: project_kernel(owner_slots, sizes, cap, *r),
        "project",
        (pltpu.HBM((count, e + BR), BF), pltpu.HBM((n, e), F32), pltpu.HBM((16, n), F32)),
        (
            slot_of_image.reshape(1, n),
            pltpu.with_memory_space_constraint(features, pltpu.HBM),
            pltpu.with_memory_space_constraint(head_weight, pltpu.HBM),
        ),
        in_specs=[vmem, far_away, far_away],
        out_specs=(far_away, far_away, vmem),
        scratch_shapes=[
            pltpu.VMEM((n, width), BF),
            pltpu.VMEM((width, e), BF),
            pltpu.VMEM((n, e), F32),
            pltpu.VMEM((count, e + BR), BF),
            pltpu.SemaphoreType.DMA((13,)),
        ],
    )
    send, late_features = lax.optimization_barrier((send, features))
    mine, other = call(
        lambda *r: stripes_kernel(sizes, *r),
        "stripes",
        (sds((width // 2, n), BF),) * 2,
        (core.reshape(1), late_features),
        in_specs=[smem, vmem],
    )
    got = exchange(send.reshape(devices, cap, e + BR), DISPATCH).reshape(count, e + BR)
    theirs = swap(other)

    table = candidates.reshape(dp, blocks, REPS, PAIRS_REP)
    table = lax.dynamic_index_in_dim(table, member, axis=2, keepdims=False)
    table = table.reshape(dp, blocks * PAIRS_REP)
    owner = table // blocks
    numbers = jnp.arange(dp, dtype=I32)
    wanted = jnp.sum(jnp.where(owner == me, table - owner * blocks, 0), axis=1)

    def fetch_place(number):
        column = number // 2
        z = column // sizes["x"]
        x = column - z * sizes["x"]
        return position(FETCH, sizes, dict(z=z, x=x, ylo=(number & 1) ^ slab))

    serve = jnp.sum(
        jnp.where(fetch_place(numbers)[None, :] == numbers[:, None], wanted[None, :], 0), axis=1
    )
    need = fetch_place(lax.dynamic_index_in_dim(owner, me, axis=0, keepdims=False))
    keys = serve * dp + numbers
    place_of = jnp.sum((keys[None, :] < keys[:, None]).astype(I32), axis=1)
    order = jnp.sum(jnp.where(place_of[None, :] == numbers[:, None], numbers[None, :], 0), axis=1)
    bounds = 2 * jnp.arange(blocks // 2 + 1, dtype=I32)
    ready = jnp.sum((serve[None, :] < bounds[:, None]).astype(I32), axis=1)

    got, serve, order, ready, need, mine, theirs = lax.optimization_barrier(
        (got, serve, order, ready, need, mine, theirs)
    )
    packed, back_place = call(
        compact_kernel, "compact", (sds((n + 16, e), BF), sds((8, count), F32)), (got, positives.reshape(4, e))
    )
    beside = swap(packed)
    across = swap(packed, ("yhi", "ylo"))

    whole = sds((owner_slots, e), BF)
    ids_shape = sds((8, n), F32)
    partial, slots, other_positives = call(
        near_kernel,
        "near",
        (whole, sds((2, 8, n), F32), sds((blocks, BR), I32)),
        (packed, beside),
        cost_estimate=cost(4),
    )
    column = jnp.where(home, positives.reshape(blocks, BR), other_positives)
    column = column - member * (PAIRS_REP * BR)
    partial, across, column = lax.optimization_barrier((partial, across, column))
    corner = swap(across)
    partial, slots_across = call(middle_kernel, "middle", (whole, ids_shape), (partial, across))
    anchors, served, slots_corner = call(
        far_kernel,
        "far",
        (whole, pltpu.HBM((dp, BR, e), BF), ids_shape),
        (serve, order, ready, partial, corner),
        in_specs=[smem] * 3 + [vmem] * 2,
        out_specs=(vmem, pl.BlockSpec(memory_space=pltpu.HBM), vmem),
        scratch_shapes=[pltpu.SemaphoreType.DMA((dp,))],
    )
    fetched = exchange(served, FETCH)
    weights, stats = call(
        scores_kernel,
        "scores",
        (
            sds((blocks, PAIRS_REP * BR, BR), BF),
            sds((2 * blocks, BR), F32),
        ),
        (need, column, anchors, fetched),
        in_specs=[smem] + [vmem] * 3,
    )
    spread = (stats, swap(stats), swap(stats, ("yhi", "ylo")), swap(stats, ("core", "yhi", "ylo")))
    pulled, partner = call(
        mix_kernel,
        "mix",
        (sds((owner_slots, e), BF),) * 2,
        (need, column, weights, fetched),
        in_specs=[smem] + [vmem] * 3,
    )
    share, for_corner = call(
        lambda *r: shares_kernel(factor, *r),
        "shares",
        (whole, sds((n, e), BF)),
        (*spread, pulled, partner, slots_corner),
    )

    def pick(name, rows, ids):
        return call(
            pick_kernel, name, sds((n, e), BF), (rows, ids), cost_estimate=cost(0.01)
        )

    for_across = pick("across", share, slots_across).astype(F32) + swap(for_corner).astype(F32)
    from_across = swap(for_across.astype(BF), ("yhi", "ylo"))
    own = pick("own", share, slots[0])
    from_beside = swap(pick("beside", share, slots[1]))
    both = (spread[0] + spread[3]) + (spread[1] + spread[2])
    rest, matching = both[:blocks], both[blocks:]
    total = rest + jnp.exp(matching - 1.0 / logit_sharpness)
    loss = (jnp.log(total) + 1.0 / logit_sharpness - matching).reshape(owner_slots)
    anchor_row_loss = jnp.where(home, loss, swap(loss, ("ylo",)))
    chip, back_pick = call(
        chip_kernel, "chip", (sds((n, e), F32), sds((count, n), BF)), (own, from_beside, back_place)
    )
    chip, back_pick, anchor_row_loss = lax.optimization_barrier((chip, back_pick, anchor_row_loss))
    back = call(
        back_kernel,
        "back",
        pltpu.HBM((count, e), BF),
        (chip, from_across, back_pick),
    )
    returned = exchange(back.reshape(devices, cap, e), DISPATCH).reshape(count, e)

    grad = call(
        unit_grad_kernel,
        "unit_grad",
        sds((n, e), BF),
        (returned, place, pltpu.with_memory_space_constraint(unit, pltpu.HBM)),
        in_specs=[vmem, vmem, far_away],
        scratch_shapes=[pltpu.VMEM((n, e), F32), pltpu.SemaphoreType.DMA],
    )
    begun = call(head_begun_kernel, "head_begun", sds((width // 2, e), F32), (mine, grad))
    partial = call(
        head_grad_kernel,
        "head_grad",
        pltpu.HBM((width // 2, e), BF),
        (begun, theirs, swap(grad)),
    )
    parts = exchange(partial.reshape(devices // 2, width // devices, e), REDUCE)
    weight_grad = call(sum_kernel, "add", sds((width // devices, e), F32), (parts,))
    return (anchor_row_loss, weight_grad)


def solution(mesh):
    dp, rep = mesh.devices.shape
    z = x = math.isqrt(dp // 2)
    split = jax.sharding.Mesh(mesh.devices.reshape(z, x, 2, rep // 2, 2), AXES)
    owners = ("z", "x", "core")
    placed = (P(AXES, None), P(), P(AXES), P(), P(owners))
    return jax.shard_map(
        shards,
        mesh=split,
        in_specs=placed,
        out_specs=(P(owners), P(AXES, None)),
        check_vma=False,
    )
```

```python
import math

import jax
import jax.numpy as jnp
from jax import lax
from jax.experimental import pallas as pl
from jax.experimental.pallas import tpu as pltpu
from jax.sharding import PartitionSpec as P

BR = 128
PAIRS_REP = 2
REPS = 4

logit_sharpness = 0.05
objective_factor = 32.0
norm_eps = 1e-06

BF = jnp.bfloat16
F32 = jnp.float32
I32 = jnp.int32
VMEM_BYTES = 24 * 1024 * 1024


AXES = ("z", "x", "core", "yhi", "ylo")
DISPATCH = ("core", "x", "yhi", "ylo", "z")
FETCH = ("ylo", "x", "z")
REDUCE = ("x", "yhi", "ylo", "z")


def position(order, sizes, place):
    at = 0
    for axis in order:
        at = at * sizes[axis] + place[axis]
    return at


def params():
    return pltpu.CompilerParams(vmem_limit_bytes=VMEM_BYTES)


def cost(us):
    return pl.CostEstimate(flops=int(us * 1e9), bytes_accessed=int(us * 1e6), transcendentals=0)


def iota(shape, dim):
    return lax.broadcasted_iota(I32, shape, dim)


def hot(mask):
    return jnp.where(mask, 1.0, 0.0).astype(BF)


def dot(a, b, ca=1, cb=0):
    return lax.dot_general(a, b, (((ca,), (cb,)), ((), ())), preferred_element_type=F32)


def sds(shape, dtype):
    return jax.ShapeDtypeStruct(shape, dtype)


def column_of(rows):
    return float_column_of(rows).astype(I32)


def float_column_of(rows):
    wide = jnp.concatenate([rows] * (BR // rows.shape[0]), axis=0)
    return wide.T[:, 0:1]


def project_kernel(
    owner_slots, sizes, cap, slot, feat_in, head_in, sent, unit, place, feat, head, kept, send, sems
):
    n = feat.shape[0]
    width, e = head.shape
    parts = 4
    depth = width // parts
    copies = []
    for k in range(parts):
        at = pl.ds(k * depth, depth)
        copies.append(pltpu.make_async_copy(head_in.at[at, :], head.at[at, :], sems.at[k]))
        copies.append(pltpu.make_async_copy(feat_in.at[:, at], feat.at[:, at], sems.at[parts + k]))
    for c in copies:
        c.start()
    s = slot[...]
    owner = s // owner_slots
    local = s - owner * owner_slots
    owners = sizes["z"] * sizes["x"] * 2
    mine = iota((owners, n), 0) == owner
    before = dot(hot(mine), hot(iota((n, n), 0) < iota((n, n), 1)))
    rank = jnp.sum(jnp.where(mine, before, 0.0), axis=0, keepdims=True).astype(I32)
    member = rank & (REPS - 1)
    slab = member & 1
    column = owner // 2
    z = column // sizes["x"]
    place_of = dict(
        z=z, x=column - z * sizes["x"], core=member // 2, yhi=slab, ylo=(owner & 1) ^ slab
    )
    device = position(DISPATCH, sizes, place_of)
    p = device * cap + rank // REPS
    place[:8, :] = jnp.broadcast_to(p.astype(F32), (8, n))
    scatter = hot(iota((send.shape[0], n), 0) == p)
    high = local // BR
    low = local - high * BR
    row = iota((BR, n), 0)
    tags = jnp.where(row == 0, high, jnp.where(row == 1, low, jnp.where(row == 2, 1, 0)))
    send[:, e:] = dot(scatter, tags.astype(F32).astype(BF), 1, 1).astype(BF)
    projected = jnp.zeros((n, e), F32)
    for k in range(parts):
        copies[2 * k].wait()
        copies[2 * k + 1].wait()
        at = slice(k * depth, (k + 1) * depth)
        projected += dot(feat[:, at], head[at, :])
    length = jnp.sqrt(jnp.sum(projected * projected, axis=1, keepdims=True) + norm_eps)
    rows = projected / length
    kept[...] = rows
    keep = pltpu.make_async_copy(kept, unit, sems.at[2 * parts])
    keep.start()
    place[8:, :] = jnp.broadcast_to(length, (n, BR)).T[:8, :]
    descriptor = rows.astype(BF)
    step = send.shape[0] // parts
    leave = []
    for k in range(parts):
        at = slice(k * step, (k + 1) * step)
        send[at, :e] = dot(scatter[at, :], descriptor).astype(BF)
        at = pl.ds(k * step, step)
        leave.append(
            pltpu.make_async_copy(send.at[at, :], sent.at[at, :], sems.at[2 * parts + 1 + k])
        )
        leave[-1].start()
    keep.wait()
    for c in leave:
        c.wait()


def stripes_kernel(sizes, core, feat, mine, other):
    first = core[0] == 0
    half = BR // 2
    rows = half // REPS
    for column in range(feat.shape[1] // BR):
        t = feat[:, column * BR : (column + 1) * BR].astype(F32).T
        a, b = t[:half, :], t[half:, :]
        here, there = jnp.where(first, a, b).astype(BF), jnp.where(first, b, a).astype(BF)
        z, x = divmod(column, sizes["x"])
        for y in range(REPS):
            at = position(REDUCE, sizes, dict(z=z, x=x, yhi=y // 2, ylo=y % 2)) * rows
            mine[at : at + rows, :] = here[y * rows : (y + 1) * rows, :]
            other[at : at + rows, :] = there[y * rows : (y + 1) * rows, :]


def compact_kernel(got, positives, packed, place):
    count = got.shape[0]
    e = packed.shape[1]
    rows = packed.shape[0] - 16
    tags = got[:, e:].astype(F32).T
    valid = tags[2:3, :]
    upper = hot(iota((count, count), 0) < iota((count, count), 1))
    before = dot(jnp.broadcast_to(valid, (16, count)).astype(BF), upper)[0:1, :]
    pos = jnp.where(valid > 0.5, before, -1.0)
    place[...] = jnp.broadcast_to(pos, place.shape)
    pick = hot(iota((rows, count), 0) == pos.astype(I32))
    packed[:rows, :] = dot(pick, got[:, :e]).astype(BF)
    slot = dot(tags[:16, :].astype(BF), pick, 1, 1)
    high = positives[...] // BR
    low = positives[...] - high * BR
    spare = [slot[:4, :], high.astype(F32), low.astype(F32), jnp.zeros((4, e), F32)]
    packed[rows:, :] = jnp.concatenate(spare, axis=0).astype(BF)


def slot_row(tag):
    tag = tag.astype(F32)
    return tag[0:1, :] * BR + tag[1:2, :]


def place_rows(out, pieces, start, after=None):
    step = 2 * BR

    def body(i, carry):
        base = pl.multiple_of(i * step, step)
        total = None if start is None else start[pl.ds(base, step), :].astype(F32)
        for ids, rows in pieces:
            at = iota((step, rows.shape[0]), 0) + base
            part = dot(hot(at == ids), rows)
            total = part if total is None else total + part
        out[pl.ds(base, step), :] = total.astype(BF)
        if after is not None:
            after(i)
        return carry

    lax.fori_loop(0, out.shape[0] // step, body, 0)


def near_kernel(own, beside, partial, slots, positives):
    n = own.shape[0] - 16
    pieces = []
    for k, ref in enumerate((own, beside)):
        row = slot_row(ref[n:, :])
        slots[k, :, :] = jnp.broadcast_to(row, slots.shape[1:])
        pieces.append((row.astype(I32), ref[:n, :]))
    place_rows(partial, pieces, None)
    spare = beside[n:, :].astype(F32)
    digits = (spare[4:8, :] * BR + spare[8:12, :]).astype(I32)
    lanes = digits.shape[1] // BR
    for i in range(positives.shape[0]):
        at = slice((i % lanes) * BR, (i % lanes + 1) * BR)
        positives[i : i + 1, :] = digits[i // lanes : i // lanes + 1, at]


def middle_kernel(begun, across, partial, slots):
    n = across.shape[0] - 16
    row = slot_row(across[n:, :])
    slots[...] = jnp.broadcast_to(row, slots.shape)
    place_rows(partial, [(row.astype(I32), across[:n, :])], begun)


def far_kernel(serve, order, ready, begun, corner, anchors, served, slots):
    n = corner.shape[0] - 16
    row = slot_row(corner[n:, :])
    slots[...] = jnp.broadcast_to(row, slots.shape)

    def begin(j, carry):
        d = order[j]
        served[d] = anchors[pl.ds(pl.multiple_of(serve[d] * BR, BR), BR), :]
        return carry

    def after(i):
        lax.fori_loop(ready[i], ready[i + 1], begin, 0)

    place_rows(anchors, [(row.astype(I32), corner[:n, :])], begun, after)


def scores_kernel(need, column, anchors, partners, weights, stats):
    blocks = weights.shape[0]

    def body(i, carry):
        for j in range(4):
            b = i * 4 + j
            q = anchors[pl.ds(pl.multiple_of(b * BR, BR), BR), :]
            total = jnp.zeros((1, BR), F32)
            positive = jnp.zeros((1, BR), F32)
            want = column[pl.ds(b, 1), :]
            for k in range(PAIRS_REP):
                logits = dot(partners[need[b * PAIRS_REP + k]], q, 1, 1) / logit_sharpness
                hit = iota((BR, BR), 0) + k * BR == want
                w = jnp.where(hit, 0.0, jnp.exp(logits - 1.0 / logit_sharpness))
                weights[b, k * BR : (k + 1) * BR, :] = w.astype(BF)
                total += jnp.sum(w, axis=0, keepdims=True)
                positive += jnp.sum(jnp.where(hit, logits, 0.0), axis=0, keepdims=True)
            stats[pl.ds(b, 1), :] = total
            stats[pl.ds(blocks + b, 1), :] = positive
        return carry

    lax.fori_loop(0, blocks // 4, body, 0)


def mix_kernel(need, column, weights, partners, pulled, partner):
    blocks = weights.shape[0]

    def body(i, carry):
        for j in range(4):
            b = i * 4 + j
            w = weights[b]
            hit = hot(iota(w.shape, 0) == column[pl.ds(b, 1), :])
            pair = [partners[need[b * PAIRS_REP + k]] for k in range(PAIRS_REP)]
            both = dot(jnp.concatenate([w, hit], axis=1), jnp.concatenate(pair, axis=0), 0, 0)
            at = pl.ds(pl.multiple_of(b * BR, BR), BR)
            pulled[at, :] = both[:BR, :].astype(BF)
            partner[at, :] = both[BR:, :].astype(BF)
        return carry

    lax.fori_loop(0, blocks // 4, body, 0)


def pick_rows(out, rows, ids):
    step = 256
    for h in range(out.shape[0] // step):
        pick = hot(iota((step, rows.shape[0]), 1) == ids[h * step : (h + 1) * step, :])
        out[h * step : (h + 1) * step, :] = dot(pick, rows[...]).astype(BF)


def shares_kernel(factor, s0, s1, s2, s3, pulled, partner, slots, share, out):
    blocks = s0.shape[0] // 2
    stats = (s0[...] + s3[...]) + (s1[...] + s2[...])
    rest, matching = stats[:blocks, :], stats[blocks:, :]
    total = rest + jnp.exp(matching - 1.0 / logit_sharpness)
    scale = jnp.concatenate([factor / total, factor * (rest / total)], axis=0)
    scale = jnp.concatenate([scale] * (BR // (2 * blocks)), axis=0).T
    for b in range(blocks):
        at = slice(b * BR, (b + 1) * BR)
        grad = pulled[at, :].astype(F32) * scale[:, b : b + 1]
        grad -= partner[at, :].astype(F32) * scale[:, blocks + b : blocks + b + 1]
        share[at, :] = grad.astype(BF)
    pick_rows(out, share, column_of(slots[...]))


def pick_kernel(share, slots, out):
    pick_rows(out, share, column_of(slots[...]))


def chip_kernel(own, beside, place, total, pick):
    total[...] = own[...].astype(F32) + beside[...].astype(F32)
    pick[...] = hot(iota(pick.shape, 1) == column_of(place[...]))


def back_kernel(chip, across, pick, back):
    total = chip[...] + across[...].astype(F32)
    back[...] = dot(pick[...], total.astype(BF)).astype(BF)


def unit_grad_kernel(got, place, unit, out, kept, sem):
    fetch = pltpu.make_async_copy(unit, kept, sem)
    fetch.start()
    n = out.shape[0]
    grad = dot(hot(iota((n, got.shape[0]), 1) == column_of(place[:8, :])), got[...])
    fetch.wait()
    rows = kept[...]
    radial = jnp.sum(rows * grad, axis=1, keepdims=True)
    out[...] = ((grad - rows * radial) / float_column_of(place[8:, :])).astype(BF)


def head_begun_kernel(mine, grad, out):
    step = 256
    for i in range(out.shape[0] // step):
        at = slice(i * step, (i + 1) * step)
        out[at, :] = dot(mine[at, :], grad[...])


def head_grad_kernel(begun, theirs, partner, out):
    step = 256
    for i in range(out.shape[0] // step):
        at = slice(i * step, (i + 1) * step)
        out[at, :] = (begun[at, :] + dot(theirs[at, :], partner[...])).astype(BF)


def sum_kernel(parts, out):
    out[...] = jnp.sum(parts[...].astype(F32), axis=0)


def swap(x, axes=("core",)):
    size = 2 ** len(axes)
    return lax.ppermute(x, axes, [(i, size - 1 - i) for i in range(size)])


def exchange(x, axes):
    return lax.all_to_all(x, axes, 0, 0, tiled=True)


def shards(features, head_weight, slot_of_image, candidates, positives):
    sizes = {axis: lax.axis_size(axis) for axis in AXES}
    dp = sizes["z"] * sizes["x"] * 2
    slab = lax.axis_index("yhi")
    me = (lax.axis_index("z") * sizes["x"] + lax.axis_index("x")) * 2
    me = me + (lax.axis_index("ylo") ^ slab)
    core = lax.axis_index("core")
    member = core * 2 + slab
    home = core == (me & 1)
    n, width = features.shape
    e = head_weight.shape[1]
    devices = dp * REPS
    owner_slots = n * REPS
    blocks = owner_slots // BR
    cap = 2 * n // devices
    count = devices * cap
    factor = objective_factor / (logit_sharpness * math.sqrt(n * devices))
    vmem = pl.BlockSpec(memory_space=pltpu.VMEM)
    smem = pl.BlockSpec(memory_space=pltpu.SMEM)
    far_away = pl.BlockSpec(memory_space=pl.ANY)

    def call(kernel, name, shapes, args, **more):
        return pl.pallas_call(
            kernel, out_shape=shapes, compiler_params=params(), name=name, **more
        )(*args)

    send, unit, place = call(
        lambda *r: project_kernel(owner_slots, sizes, cap, *r),
        "project",
        (pltpu.HBM((count, e + BR), BF), pltpu.HBM((n, e), F32), pltpu.HBM((16, n), F32)),
        (
            slot_of_image.reshape(1, n),
            pltpu.with_memory_space_constraint(features, pltpu.HBM),
            pltpu.with_memory_space_constraint(head_weight, pltpu.HBM),
        ),
        in_specs=[vmem, far_away, far_away],
        out_specs=(far_away, far_away, vmem),
        scratch_shapes=[
            pltpu.VMEM((n, width), BF),
            pltpu.VMEM((width, e), BF),
            pltpu.VMEM((n, e), F32),
            pltpu.VMEM((count, e + BR), BF),
            pltpu.SemaphoreType.DMA((13,)),
        ],
    )
    send, late_features = lax.optimization_barrier((send, features))
    mine, other = call(
        lambda *r: stripes_kernel(sizes, *r),
        "stripes",
        (sds((width // 2, n), BF),) * 2,
        (core.reshape(1), late_features),
        in_specs=[smem, vmem],
    )
    got = exchange(send.reshape(devices, cap, e + BR), DISPATCH).reshape(count, e + BR)
    theirs = swap(other)

    table = candidates.reshape(dp, blocks, REPS, PAIRS_REP)
    table = lax.dynamic_index_in_dim(table, member, axis=2, keepdims=False)
    table = table.reshape(dp, blocks * PAIRS_REP)
    owner = table // blocks
    numbers = jnp.arange(dp, dtype=I32)
    wanted = jnp.sum(jnp.where(owner == me, table - owner * blocks, 0), axis=1)

    def fetch_place(number):
        column = number // 2
        z = column // sizes["x"]
        x = column - z * sizes["x"]
        return position(FETCH, sizes, dict(z=z, x=x, ylo=(number & 1) ^ slab))

    serve = jnp.sum(
        jnp.where(fetch_place(numbers)[None, :] == numbers[:, None], wanted[None, :], 0), axis=1
    )
    need = fetch_place(lax.dynamic_index_in_dim(owner, me, axis=0, keepdims=False))
    keys = serve * dp + numbers
    place_of = jnp.sum((keys[None, :] < keys[:, None]).astype(I32), axis=1)
    order = jnp.sum(jnp.where(place_of[None, :] == numbers[:, None], numbers[None, :], 0), axis=1)
    bounds = 2 * jnp.arange(blocks // 2 + 1, dtype=I32)
    ready = jnp.sum((serve[None, :] < bounds[:, None]).astype(I32), axis=1)

    got, serve, order, ready, need, mine, theirs = lax.optimization_barrier(
        (got, serve, order, ready, need, mine, theirs)
    )
    packed, back_place = call(
        compact_kernel, "compact", (sds((n + 16, e), BF), sds((8, count), F32)), (got, positives.reshape(4, e))
    )
    beside = swap(packed)
    across = swap(packed, ("yhi", "ylo"))

    whole = sds((owner_slots, e), BF)
    ids_shape = sds((8, n), F32)
    partial, slots, other_positives = call(
        near_kernel,
        "near",
        (whole, sds((2, 8, n), F32), sds((blocks, BR), I32)),
        (packed, beside),
        cost_estimate=cost(4),
    )
    column = jnp.where(home, positives.reshape(blocks, BR), other_positives)
    column = column - member * (PAIRS_REP * BR)
    partial, across, column = lax.optimization_barrier((partial, across, column))
    corner = swap(across)
    partial, slots_across = call(middle_kernel, "middle", (whole, ids_shape), (partial, across))
    anchors, served, slots_corner = call(
        far_kernel,
        "far",
        (whole, sds((dp, BR, e), BF), ids_shape),
        (serve, order, ready, partial, corner),
        in_specs=[smem] * 3 + [vmem] * 2,
    )
    fetched = exchange(served, FETCH)
    weights, stats = call(
        scores_kernel,
        "scores",
        (
            sds((blocks, PAIRS_REP * BR, BR), BF),
            sds((2 * blocks, BR), F32),
        ),
        (need, column, anchors, fetched),
        in_specs=[smem] + [vmem] * 3,
    )
    spread = (stats, swap(stats), swap(stats, ("yhi", "ylo")), swap(stats, ("core", "yhi", "ylo")))
    pulled, partner = call(
        mix_kernel,
        "mix",
        (sds((owner_slots, e), BF),) * 2,
        (need, column, weights, fetched),
        in_specs=[smem] + [vmem] * 3,
    )
    share, for_corner = call(
        lambda *r: shares_kernel(factor, *r),
        "shares",
        (whole, sds((n, e), BF)),
        (*spread, pulled, partner, slots_corner),
    )

    def pick(name, rows, ids):
        return call(
            pick_kernel, name, sds((n, e), BF), (rows, ids), cost_estimate=cost(0.01)
        )

    for_across = pick("across", share, slots_across).astype(F32) + swap(for_corner).astype(F32)
    from_across = swap(for_across.astype(BF), ("yhi", "ylo"))
    own = pick("own", share, slots[0])
    from_beside = swap(pick("beside", share, slots[1]))
    both = (spread[0] + spread[3]) + (spread[1] + spread[2])
    rest, matching = both[:blocks], both[blocks:]
    total = rest + jnp.exp(matching - 1.0 / logit_sharpness)
    loss = (jnp.log(total) + 1.0 / logit_sharpness - matching).reshape(owner_slots)
    anchor_row_loss = jnp.where(home, loss, swap(loss, ("ylo",)))
    chip, back_pick = call(
        chip_kernel, "chip", (sds((n, e), F32), sds((count, n), BF)), (own, from_beside, back_place)
    )
    chip, back_pick, anchor_row_loss = lax.optimization_barrier((chip, back_pick, anchor_row_loss))
    back = call(
        back_kernel,
        "back",
        sds((count, e), BF),
        (chip, from_across, back_pick),
    )
    returned = exchange(back.reshape(devices, cap, e), DISPATCH).reshape(count, e)

    grad = call(
        unit_grad_kernel,
        "unit_grad",
        sds((n, e), BF),
        (returned, place, pltpu.with_memory_space_constraint(unit, pltpu.HBM)),
        in_specs=[vmem, vmem, far_away],
        scratch_shapes=[pltpu.VMEM((n, e), F32), pltpu.SemaphoreType.DMA],
    )
    begun = call(head_begun_kernel, "head_begun", sds((width // 2, e), F32), (mine, grad))
    partial = call(
        head_grad_kernel,
        "head_grad",
        sds((width // 2, e), BF),
        (begun, theirs, swap(grad)),
    )
    parts = exchange(partial.reshape(devices // 2, width // devices, e), REDUCE)
    weight_grad = call(sum_kernel, "add", sds((width // devices, e), F32), (parts,))
    return (anchor_row_loss, weight_grad)


def solution(mesh):
    dp, rep = mesh.devices.shape
    z = x = math.isqrt(dp // 2)
    split = jax.sharding.Mesh(mesh.devices.reshape(z, x, 2, rep // 2, 2), AXES)
    owners = ("z", "x", "core")
    placed = (P(AXES, None), P(), P(AXES), P(), P(owners))
    return jax.shard_map(
        shards,
        mesh=split,
        in_specs=placed,
        out_specs=(P(owners), P(AXES, None)),
        check_vma=False,
    )
```

```python
import math

import jax
import jax.numpy as jnp
from jax import lax
from jax.experimental import pallas as pl
from jax.experimental.pallas import tpu as pltpu
from jax.sharding import PartitionSpec as P

BR = 128
PAIRS_REP = 2
REPS = 4

logit_sharpness = 0.05
objective_factor = 32.0
norm_eps = 1e-06

BF = jnp.bfloat16
F32 = jnp.float32
I32 = jnp.int32
VMEM_BYTES = 24 * 1024 * 1024


AXES = ("z", "x", "core", "yhi", "ylo")
DISPATCH = ("core", "x", "yhi", "ylo", "z")
FETCH = ("ylo", "x", "z")
REDUCE = ("x", "yhi", "ylo", "z")


def position(order, sizes, place):
    at = 0
    for axis in order:
        at = at * sizes[axis] + place[axis]
    return at


def params():
    return pltpu.CompilerParams(vmem_limit_bytes=VMEM_BYTES)


def cost(us):
    return pl.CostEstimate(flops=int(us * 1e9), bytes_accessed=int(us * 1e6), transcendentals=0)


def iota(shape, dim):
    return lax.broadcasted_iota(I32, shape, dim)


def hot(mask):
    return jnp.where(mask, 1.0, 0.0).astype(BF)


def dot(a, b, ca=1, cb=0):
    return lax.dot_general(a, b, (((ca,), (cb,)), ((), ())), preferred_element_type=F32)


def sds(shape, dtype):
    return jax.ShapeDtypeStruct(shape, dtype)


def column_of(rows):
    return float_column_of(rows).astype(I32)


def float_column_of(rows):
    wide = jnp.concatenate([rows] * (BR // rows.shape[0]), axis=0)
    return wide.T[:, 0:1]


def project_kernel(
    owner_slots, sizes, cap, slot, feat_in, head_in, send, unit, place, feat, head, kept, sems
):
    n = feat.shape[0]
    width, e = head.shape
    parts = 4
    depth = width // parts
    copies = []
    for k in range(parts):
        at = pl.ds(k * depth, depth)
        copies.append(pltpu.make_async_copy(head_in.at[at, :], head.at[at, :], sems.at[k]))
        copies.append(pltpu.make_async_copy(feat_in.at[:, at], feat.at[:, at], sems.at[parts + k]))
    for c in copies:
        c.start()
    s = slot[...]
    owner = s // owner_slots
    local = s - owner * owner_slots
    owners = sizes["z"] * sizes["x"] * 2
    mine = iota((owners, n), 0) == owner
    before = dot(hot(mine), hot(iota((n, n), 0) < iota((n, n), 1)))
    rank = jnp.sum(jnp.where(mine, before, 0.0), axis=0, keepdims=True).astype(I32)
    member = rank & (REPS - 1)
    slab = member & 1
    column = owner // 2
    z = column // sizes["x"]
    place_of = dict(
        z=z, x=column - z * sizes["x"], core=member // 2, yhi=slab, ylo=(owner & 1) ^ slab
    )
    device = position(DISPATCH, sizes, place_of)
    p = device * cap + rank // REPS
    place[:8, :] = jnp.broadcast_to(p.astype(F32), (8, n))
    scatter = hot(iota((send.shape[0], n), 0) == p)
    high = local // BR
    low = local - high * BR
    row = iota((BR, n), 0)
    tags = jnp.where(row == 0, high, jnp.where(row == 1, low, jnp.where(row == 2, 1, 0)))
    send[:, e:] = dot(scatter, tags.astype(F32).astype(BF), 1, 1).astype(BF)
    projected = jnp.zeros((n, e), F32)
    for k in range(parts):
        copies[2 * k].wait()
        copies[2 * k + 1].wait()
        at = slice(k * depth, (k + 1) * depth)
        projected += dot(feat[:, at], head[at, :])
    length = jnp.sqrt(jnp.sum(projected * projected, axis=1, keepdims=True) + norm_eps)
    rows = projected / length
    kept[...] = rows
    keep = pltpu.make_async_copy(kept, unit, sems.at[2 * parts])
    keep.start()
    place[8:, :] = jnp.broadcast_to(length, (n, BR)).T[:8, :]
    send[:, :e] = dot(scatter, rows.astype(BF)).astype(BF)
    keep.wait()


def stripes_kernel(sizes, core, feat, mine, other):
    first = core[0] == 0
    half = BR // 2
    rows = half // REPS
    for column in range(feat.shape[1] // BR):
        t = feat[:, column * BR : (column + 1) * BR].astype(F32).T
        a, b = t[:half, :], t[half:, :]
        here, there = jnp.where(first, a, b).astype(BF), jnp.where(first, b, a).astype(BF)
        z, x = divmod(column, sizes["x"])
        for y in range(REPS):
            at = position(REDUCE, sizes, dict(z=z, x=x, yhi=y // 2, ylo=y % 2)) * rows
            mine[at : at + rows, :] = here[y * rows : (y + 1) * rows, :]
            other[at : at + rows, :] = there[y * rows : (y + 1) * rows, :]


def compact_kernel(got, positives, packed, place):
    count = got.shape[0]
    e = packed.shape[1]
    rows = packed.shape[0] - 16
    tags = got[:, e:].astype(F32).T
    valid = tags[2:3, :]
    upper = hot(iota((count, count), 0) < iota((count, count), 1))
    before = dot(jnp.broadcast_to(valid, (16, count)).astype(BF), upper)[0:1, :]
    pos = jnp.where(valid > 0.5, before, -1.0)
    place[...] = jnp.broadcast_to(pos, place.shape)
    pick = hot(iota((rows, count), 0) == pos.astype(I32))
    packed[:rows, :] = dot(pick, got[:, :e]).astype(BF)
    slot = dot(tags[:16, :].astype(BF), pick, 1, 1)
    high = positives[...] // BR
    low = positives[...] - high * BR
    spare = [slot[:4, :], high.astype(F32), low.astype(F32), jnp.zeros((4, e), F32)]
    packed[rows:, :] = jnp.concatenate(spare, axis=0).astype(BF)


def slot_row(tag):
    tag = tag.astype(F32)
    return tag[0:1, :] * BR + tag[1:2, :]


def place_rows(out, pieces, start, after=None):
    step = 2 * BR

    def body(i, carry):
        base = pl.multiple_of(i * step, step)
        total = None if start is None else start[pl.ds(base, step), :].astype(F32)
        for ids, rows in pieces:
            at = iota((step, rows.shape[0]), 0) + base
            part = dot(hot(at == ids), rows)
            total = part if total is None else total + part
        out[pl.ds(base, step), :] = total.astype(BF)
        if after is not None:
            after(i)
        return carry

    lax.fori_loop(0, out.shape[0] // step, body, 0)


def near_kernel(own, beside, partial, slots, positives):
    n = own.shape[0] - 16
    pieces = []
    for k, ref in enumerate((own, beside)):
        row = slot_row(ref[n:, :])
        slots[k, :, :] = jnp.broadcast_to(row, slots.shape[1:])
        pieces.append((row.astype(I32), ref[:n, :]))
    place_rows(partial, pieces, None)
    spare = beside[n:, :].astype(F32)
    digits = (spare[4:8, :] * BR + spare[8:12, :]).astype(I32)
    lanes = digits.shape[1] // BR
    for i in range(positives.shape[0]):
        at = slice((i % lanes) * BR, (i % lanes + 1) * BR)
        positives[i : i + 1, :] = digits[i // lanes : i // lanes + 1, at]


def middle_kernel(begun, across, partial, slots):
    n = across.shape[0] - 16
    row = slot_row(across[n:, :])
    slots[...] = jnp.broadcast_to(row, slots.shape)
    place_rows(partial, [(row.astype(I32), across[:n, :])], begun)


def far_kernel(serve, order, ready, begun, corner, anchors, served, slots):
    n = corner.shape[0] - 16
    row = slot_row(corner[n:, :])
    slots[...] = jnp.broadcast_to(row, slots.shape)

    def begin(j, carry):
        d = order[j]
        served[d] = anchors[pl.ds(pl.multiple_of(serve[d] * BR, BR), BR), :]
        return carry

    def after(i):
        lax.fori_loop(ready[i], ready[i + 1], begin, 0)

    place_rows(anchors, [(row.astype(I32), corner[:n, :])], begun, after)


def scores_kernel(need, column, anchors, partners, weights, stats):
    blocks = weights.shape[0]

    def body(i, carry):
        for j in range(4):
            b = i * 4 + j
            q = anchors[pl.ds(pl.multiple_of(b * BR, BR), BR), :]
            total = jnp.zeros((1, BR), F32)
            positive = jnp.zeros((1, BR), F32)
            want = column[pl.ds(b, 1), :]
            for k in range(PAIRS_REP):
                logits = dot(partners[need[b * PAIRS_REP + k]], q, 1, 1) / logit_sharpness
                hit = iota((BR, BR), 0) + k * BR == want
                w = jnp.where(hit, 0.0, jnp.exp(logits - 1.0 / logit_sharpness))
                weights[b, k * BR : (k + 1) * BR, :] = w.astype(BF)
                total += jnp.sum(w, axis=0, keepdims=True)
                positive += jnp.sum(jnp.where(hit, logits, 0.0), axis=0, keepdims=True)
            stats[pl.ds(b, 1), :] = total
            stats[pl.ds(blocks + b, 1), :] = positive
        return carry

    lax.fori_loop(0, blocks // 4, body, 0)


def mix_kernel(need, column, weights, partners, pulled, partner):
    blocks = weights.shape[0]

    def body(i, carry):
        for j in range(4):
            b = i * 4 + j
            w = weights[b]
            hit = hot(iota(w.shape, 0) == column[pl.ds(b, 1), :])
            pair = [partners[need[b * PAIRS_REP + k]] for k in range(PAIRS_REP)]
            both = dot(jnp.concatenate([w, hit], axis=1), jnp.concatenate(pair, axis=0), 0, 0)
            at = pl.ds(pl.multiple_of(b * BR, BR), BR)
            pulled[at, :] = both[:BR, :].astype(BF)
            partner[at, :] = both[BR:, :].astype(BF)
        return carry

    lax.fori_loop(0, blocks // 4, body, 0)


def pick_rows(out, rows, ids):
    step = 256
    for h in range(out.shape[0] // step):
        pick = hot(iota((step, rows.shape[0]), 1) == ids[h * step : (h + 1) * step, :])
        out[h * step : (h + 1) * step, :] = dot(pick, rows[...]).astype(BF)


def shares_kernel(factor, s0, s1, s2, s3, pulled, partner, slots, share, out):
    blocks = s0.shape[0] // 2
    stats = (s0[...] + s3[...]) + (s1[...] + s2[...])
    rest, matching = stats[:blocks, :], stats[blocks:, :]
    total = rest + jnp.exp(matching - 1.0 / logit_sharpness)
    scale = jnp.concatenate([factor / total, factor * (rest / total)], axis=0)
    scale = jnp.concatenate([scale] * (BR // (2 * blocks)), axis=0).T
    for b in range(blocks):
        at = slice(b * BR, (b + 1) * BR)
        grad = pulled[at, :].astype(F32) * scale[:, b : b + 1]
        grad -= partner[at, :].astype(F32) * scale[:, blocks + b : blocks + b + 1]
        share[at, :] = grad.astype(BF)
    pick_rows(out, share, column_of(slots[...]))


def pick_kernel(share, slots, out):
    pick_rows(out, share, column_of(slots[...]))


def chip_kernel(own, beside, place, total, pick):
    total[...] = own[...].astype(F32) + beside[...].astype(F32)
    pick[...] = hot(iota(pick.shape, 1) == column_of(place[...]))


def back_kernel(chip, across, pick, back):
    total = chip[...] + across[...].astype(F32)
    back[...] = dot(pick[...], total.astype(BF)).astype(BF)


def unit_grad_kernel(got, place, unit, out, kept, sem):
    fetch = pltpu.make_async_copy(unit, kept, sem)
    fetch.start()
    n = out.shape[0]
    grad = dot(hot(iota((n, got.shape[0]), 1) == column_of(place[:8, :])), got[...])
    fetch.wait()
    rows = kept[...]
    radial = jnp.sum(rows * grad, axis=1, keepdims=True)
    out[...] = ((grad - rows * radial) / float_column_of(place[8:, :])).astype(BF)


def head_begun_kernel(mine, grad, out):
    step = 256
    for i in range(out.shape[0] // step):
        at = slice(i * step, (i + 1) * step)
        out[at, :] = dot(mine[at, :], grad[...])


def head_grad_kernel(begun, theirs, partner, out):
    step = 256
    for i in range(out.shape[0] // step):
        at = slice(i * step, (i + 1) * step)
        out[at, :] = (begun[at, :] + dot(theirs[at, :], partner[...])).astype(BF)


def sum_kernel(parts, out):
    out[...] = jnp.sum(parts[...].astype(F32), axis=0)


def swap(x, axes=("core",)):
    size = 2 ** len(axes)
    return lax.ppermute(x, axes, [(i, size - 1 - i) for i in range(size)])


def exchange(x, axes):
    return lax.all_to_all(x, axes, 0, 0, tiled=True)


def shards(features, head_weight, slot_of_image, candidates, positives):
    sizes = {axis: lax.axis_size(axis) for axis in AXES}
    dp = sizes["z"] * sizes["x"] * 2
    slab = lax.axis_index("yhi")
    me = (lax.axis_index("z") * sizes["x"] + lax.axis_index("x")) * 2
    me = me + (lax.axis_index("ylo") ^ slab)
    core = lax.axis_index("core")
    member = core * 2 + slab
    home = core == (me & 1)
    n, width = features.shape
    e = head_weight.shape[1]
    devices = dp * REPS
    owner_slots = n * REPS
    blocks = owner_slots // BR
    cap = 2 * n // devices
    count = devices * cap
    factor = objective_factor / (logit_sharpness * math.sqrt(n * devices))
    vmem = pl.BlockSpec(memory_space=pltpu.VMEM)
    smem = pl.BlockSpec(memory_space=pltpu.SMEM)
    far_away = pl.BlockSpec(memory_space=pl.ANY)

    def call(kernel, name, shapes, args, **more):
        return pl.pallas_call(
            kernel, out_shape=shapes, compiler_params=params(), name=name, **more
        )(*args)

    send, unit, place = call(
        lambda *r: project_kernel(owner_slots, sizes, cap, *r),
        "project",
        (sds((count, e + BR), BF), pltpu.HBM((n, e), F32), pltpu.HBM((16, n), F32)),
        (
            slot_of_image.reshape(1, n),
            pltpu.with_memory_space_constraint(features, pltpu.HBM),
            pltpu.with_memory_space_constraint(head_weight, pltpu.HBM),
        ),
        in_specs=[vmem, far_away, far_away],
        out_specs=(vmem, far_away, vmem),
        scratch_shapes=[
            pltpu.VMEM((n, width), BF),
            pltpu.VMEM((width, e), BF),
            pltpu.VMEM((n, e), F32),
            pltpu.SemaphoreType.DMA((9,)),
        ],
    )
    send, own_positives = lax.optimization_barrier((send, positives.reshape(4, e)))
    got = exchange(send.reshape(devices, cap, e + BR), DISPATCH).reshape(count, e + BR)
    packed, back_place = call(
        compact_kernel, "compact", (sds((n + 16, e), BF), sds((8, count), F32)), (got, own_positives)
    )
    beside = swap(packed)
    across = swap(packed, ("yhi", "ylo"))

    whole = sds((owner_slots, e), BF)
    ids_shape = sds((8, n), F32)
    partial, slots, other_positives = call(
        near_kernel,
        "near",
        (whole, sds((2, 8, n), F32), sds((blocks, BR), I32)),
        (packed, beside),
        cost_estimate=cost(4),
    )
    partial, late_features, late_candidates = lax.optimization_barrier(
        (partial, features, candidates)
    )
    mine, other = call(
        lambda *r: stripes_kernel(sizes, *r),
        "stripes",
        (sds((width // 2, n), BF),) * 2,
        (core.reshape(1), late_features),
        in_specs=[smem, vmem],
    )
    theirs = swap(other)
    table = late_candidates.reshape(dp, blocks, REPS, PAIRS_REP)
    table = lax.dynamic_index_in_dim(table, member, axis=2, keepdims=False)
    table = table.reshape(dp, blocks * PAIRS_REP)
    owner = table // blocks
    numbers = jnp.arange(dp, dtype=I32)
    wanted = jnp.sum(jnp.where(owner == me, table - owner * blocks, 0), axis=1)

    def fetch_place(number):
        column = number // 2
        z = column // sizes["x"]
        x = column - z * sizes["x"]
        return position(FETCH, sizes, dict(z=z, x=x, ylo=(number & 1) ^ slab))

    serve = jnp.sum(
        jnp.where(fetch_place(numbers)[None, :] == numbers[:, None], wanted[None, :], 0), axis=1
    )
    need = fetch_place(lax.dynamic_index_in_dim(owner, me, axis=0, keepdims=False))
    keys = serve * dp + numbers
    place_of = jnp.sum((keys[None, :] < keys[:, None]).astype(I32), axis=1)
    order = jnp.sum(jnp.where(place_of[None, :] == numbers[:, None], numbers[None, :], 0), axis=1)
    bounds = 2 * jnp.arange(blocks // 2 + 1, dtype=I32)
    ready = jnp.sum((serve[None, :] < bounds[:, None]).astype(I32), axis=1)

    column = jnp.where(home, positives.reshape(blocks, BR), other_positives)
    column = column - member * (PAIRS_REP * BR)
    partial, across, column, mine, theirs, serve, order, ready, need = lax.optimization_barrier(
        (partial, across, column, mine, theirs, serve, order, ready, need)
    )
    corner = swap(across)
    partial, slots_across = call(middle_kernel, "middle", (whole, ids_shape), (partial, across))
    anchors, served, slots_corner = call(
        far_kernel,
        "far",
        (whole, sds((dp, BR, e), BF), ids_shape),
        (serve, order, ready, partial, corner),
        in_specs=[smem] * 3 + [vmem] * 2,
    )
    fetched = exchange(served, FETCH)
    weights, stats = call(
        scores_kernel,
        "scores",
        (
            sds((blocks, PAIRS_REP * BR, BR), BF),
            sds((2 * blocks, BR), F32),
        ),
        (need, column, anchors, fetched),
        in_specs=[smem] + [vmem] * 3,
    )
    spread = (stats, swap(stats), swap(stats, ("yhi", "ylo")), swap(stats, ("core", "yhi", "ylo")))
    pulled, partner = call(
        mix_kernel,
        "mix",
        (sds((owner_slots, e), BF),) * 2,
        (need, column, weights, fetched),
        in_specs=[smem] + [vmem] * 3,
    )
    share, for_corner = call(
        lambda *r: shares_kernel(factor, *r),
        "shares",
        (whole, sds((n, e), BF)),
        (*spread, pulled, partner, slots_corner),
    )

    def pick(name, rows, ids):
        return call(
            pick_kernel, name, sds((n, e), BF), (rows, ids), cost_estimate=cost(0.01)
        )

    for_across = pick("across", share, slots_across).astype(F32) + swap(for_corner).astype(F32)
    from_across = swap(for_across.astype(BF), ("yhi", "ylo"))
    own = pick("own", share, slots[0])
    from_beside = swap(pick("beside", share, slots[1]))
    both = (spread[0] + spread[3]) + (spread[1] + spread[2])
    rest, matching = both[:blocks], both[blocks:]
    total = rest + jnp.exp(matching - 1.0 / logit_sharpness)
    loss = (jnp.log(total) + 1.0 / logit_sharpness - matching).reshape(owner_slots)
    anchor_row_loss = jnp.where(home, loss, swap(loss, ("ylo",)))
    chip, back_pick = call(
        chip_kernel, "chip", (sds((n, e), F32), sds((count, n), BF)), (own, from_beside, back_place)
    )
    chip, back_pick, anchor_row_loss = lax.optimization_barrier((chip, back_pick, anchor_row_loss))
    back = call(
        back_kernel,
        "back",
        sds((count, e), BF),
        (chip, from_across, back_pick),
    )
    returned = exchange(back.reshape(devices, cap, e), DISPATCH).reshape(count, e)

    grad = call(
        unit_grad_kernel,
        "unit_grad",
        sds((n, e), BF),
        (returned, place, pltpu.with_memory_space_constraint(unit, pltpu.HBM)),
        in_specs=[vmem, vmem, far_away],
        scratch_shapes=[pltpu.VMEM((n, e), F32), pltpu.SemaphoreType.DMA],
    )
    begun = call(head_begun_kernel, "head_begun", sds((width // 2, e), F32), (mine, grad))
    partial = call(
        head_grad_kernel,
        "head_grad",
        sds((width // 2, e), BF),
        (begun, theirs, swap(grad)),
    )
    parts = exchange(partial.reshape(devices // 2, width // devices, e), REDUCE)
    weight_grad = call(sum_kernel, "add", sds((width // devices, e), F32), (parts,))
    return (anchor_row_loss, weight_grad)


def solution(mesh):
    dp, rep = mesh.devices.shape
    z = x = math.isqrt(dp // 2)
    split = jax.sharding.Mesh(mesh.devices.reshape(z, x, 2, rep // 2, 2), AXES)
    owners = ("z", "x", "core")
    placed = (P(AXES, None), P(), P(AXES), P(), P(owners))
    return jax.shard_map(
        shards,
        mesh=split,
        in_specs=placed,
        out_specs=(P(owners), P(AXES, None)),
        check_vma=False,
    )
```

```python
import math

import jax
import jax.numpy as jnp
from jax import lax
from jax.experimental import pallas as pl
from jax.experimental.pallas import tpu as pltpu
from jax.sharding import PartitionSpec as P

BR = 128
PAIRS_REP = 2
REPS = 4

logit_sharpness = 0.05
objective_factor = 32.0
norm_eps = 1e-06

BF = jnp.bfloat16
F32 = jnp.float32
I32 = jnp.int32
VMEM_BYTES = 24 * 1024 * 1024


AXES = ("z", "x", "core", "yhi", "ylo")
DISPATCH = ("core", "x", "yhi", "ylo", "z")
FETCH = ("ylo", "x", "z")
REDUCE = ("x", "yhi", "ylo", "z")


def position(order, sizes, place):
    at = 0
    for axis in order:
        at = at * sizes[axis] + place[axis]
    return at


def params():
    return pltpu.CompilerParams(vmem_limit_bytes=VMEM_BYTES)


def cost(us):
    return pl.CostEstimate(flops=int(us * 1e9), bytes_accessed=int(us * 1e6), transcendentals=0)


def iota(shape, dim):
    return lax.broadcasted_iota(I32, shape, dim)


def hot(mask):
    return jnp.where(mask, 1.0, 0.0).astype(BF)


def dot(a, b, ca=1, cb=0):
    return lax.dot_general(a, b, (((ca,), (cb,)), ((), ())), preferred_element_type=F32)


def sds(shape, dtype):
    return jax.ShapeDtypeStruct(shape, dtype)


def column_of(rows):
    return float_column_of(rows).astype(I32)


def float_column_of(rows):
    wide = jnp.concatenate([rows] * (BR // rows.shape[0]), axis=0)
    return wide.T[:, 0:1]


def project_kernel(
    owner_slots, sizes, cap, slot, feat_in, head_in, send, unit, place, feat, head, kept, sems
):
    n = feat.shape[0]
    width, e = head.shape
    parts = 4
    depth = width // parts
    copies = []
    for k in range(parts):
        at = pl.ds(k * depth, depth)
        copies.append(pltpu.make_async_copy(head_in.at[at, :], head.at[at, :], sems.at[k]))
        copies.append(pltpu.make_async_copy(feat_in.at[:, at], feat.at[:, at], sems.at[parts + k]))
    for c in copies:
        c.start()
    s = slot[...]
    owner = s // owner_slots
    local = s - owner * owner_slots
    owners = sizes["z"] * sizes["x"] * 2
    mine = iota((owners, n), 0) == owner
    before = dot(hot(mine), hot(iota((n, n), 0) < iota((n, n), 1)))
    rank = jnp.sum(jnp.where(mine, before, 0.0), axis=0, keepdims=True).astype(I32)
    member = rank & (REPS - 1)
    slab = member & 1
    column = owner // 2
    z = column // sizes["x"]
    place_of = dict(
        z=z, x=column - z * sizes["x"], core=member // 2, yhi=slab, ylo=(owner & 1) ^ slab
    )
    device = position(DISPATCH, sizes, place_of)
    p = device * cap + rank // REPS
    place[:8, :] = jnp.broadcast_to(p.astype(F32), (8, n))
    scatter = hot(iota((send.shape[0], n), 0) == p)
    high = local // BR
    low = local - high * BR
    row = iota((BR, n), 0)
    tags = jnp.where(row == 0, high, jnp.where(row == 1, low, jnp.where(row == 2, 1, 0)))
    send[:, e:] = dot(scatter, tags.astype(F32).astype(BF), 1, 1).astype(BF)
    projected = jnp.zeros((n, e), F32)
    for k in range(parts):
        copies[2 * k].wait()
        copies[2 * k + 1].wait()
        at = slice(k * depth, (k + 1) * depth)
        projected += dot(feat[:, at], head[at, :])
    length = jnp.sqrt(jnp.sum(projected * projected, axis=1, keepdims=True) + norm_eps)
    rows = projected / length
    kept[...] = rows
    keep = pltpu.make_async_copy(kept, unit, sems.at[2 * parts])
    keep.start()
    place[8:, :] = jnp.broadcast_to(length, (n, BR)).T[:8, :]
    send[:, :e] = dot(scatter, rows.astype(BF)).astype(BF)
    keep.wait()


def stripes_kernel(sizes, core, feat, mine, other):
    first = core[0] == 0
    half = BR // 2
    rows = half // REPS
    for column in range(feat.shape[1] // BR):
        t = feat[:, column * BR : (column + 1) * BR].astype(F32).T
        a, b = t[:half, :], t[half:, :]
        here, there = jnp.where(first, a, b).astype(BF), jnp.where(first, b, a).astype(BF)
        z, x = divmod(column, sizes["x"])
        for y in range(REPS):
            at = position(REDUCE, sizes, dict(z=z, x=x, yhi=y // 2, ylo=y % 2)) * rows
            mine[at : at + rows, :] = here[y * rows : (y + 1) * rows, :]
            other[at : at + rows, :] = there[y * rows : (y + 1) * rows, :]


def compact_kernel(got, positives, packed, place):
    count = got.shape[0]
    e = packed.shape[1]
    rows = packed.shape[0] - 16
    tags = got[:, e:].astype(F32).T
    valid = tags[2:3, :]
    upper = hot(iota((count, count), 0) < iota((count, count), 1))
    before = dot(jnp.broadcast_to(valid, (16, count)).astype(BF), upper)[0:1, :]
    pos = jnp.where(valid > 0.5, before, -1.0)
    place[...] = jnp.broadcast_to(pos, place.shape)
    pick = hot(iota((rows, count), 0) == pos.astype(I32))
    packed[:rows, :] = dot(pick, got[:, :e]).astype(BF)
    slot = dot(tags[:16, :].astype(BF), pick, 1, 1)
    high = positives[...] // BR
    low = positives[...] - high * BR
    spare = [slot[:4, :], high.astype(F32), low.astype(F32), jnp.zeros((4, e), F32)]
    packed[rows:, :] = jnp.concatenate(spare, axis=0).astype(BF)


def slot_row(tag):
    tag = tag.astype(F32)
    return tag[0:1, :] * BR + tag[1:2, :]


def place_rows(out, pieces, start, after=None):
    step = 2 * BR

    def body(i, carry):
        base = pl.multiple_of(i * step, step)
        total = None if start is None else start[pl.ds(base, step), :].astype(F32)
        for ids, rows in pieces:
            at = iota((step, rows.shape[0]), 0) + base
            part = dot(hot(at == ids), rows)
            total = part if total is None else total + part
        out[pl.ds(base, step), :] = total.astype(BF)
        if after is not None:
            after(i)
        return carry

    lax.fori_loop(0, out.shape[0] // step, body, 0)


def near_kernel(own, beside, partial, slots, positives):
    n = own.shape[0] - 16
    pieces = []
    for k, ref in enumerate((own, beside)):
        row = slot_row(ref[n:, :])
        slots[k, :, :] = jnp.broadcast_to(row, slots.shape[1:])
        pieces.append((row.astype(I32), ref[:n, :]))
    place_rows(partial, pieces, None)
    spare = beside[n:, :].astype(F32)
    digits = (spare[4:8, :] * BR + spare[8:12, :]).astype(I32)
    lanes = digits.shape[1] // BR
    for i in range(positives.shape[0]):
        at = slice((i % lanes) * BR, (i % lanes + 1) * BR)
        positives[i : i + 1, :] = digits[i // lanes : i // lanes + 1, at]


def middle_kernel(begun, across, partial, slots):
    n = across.shape[0] - 16
    row = slot_row(across[n:, :])
    slots[...] = jnp.broadcast_to(row, slots.shape)
    place_rows(partial, [(row.astype(I32), across[:n, :])], begun)


def far_kernel(serve, order, ready, begun, corner, anchors, served, slots):
    n = corner.shape[0] - 16
    row = slot_row(corner[n:, :])
    slots[...] = jnp.broadcast_to(row, slots.shape)

    def begin(j, carry):
        d = order[j]
        served[d] = anchors[pl.ds(pl.multiple_of(serve[d] * BR, BR), BR), :]
        return carry

    def after(i):
        lax.fori_loop(ready[i], ready[i + 1], begin, 0)

    place_rows(anchors, [(row.astype(I32), corner[:n, :])], begun, after)


def scores_kernel(need, column, anchors, partners, weights, stats):
    blocks = weights.shape[0]

    def body(i, carry):
        for j in range(4):
            b = i * 4 + j
            q = anchors[pl.ds(pl.multiple_of(b * BR, BR), BR), :]
            total = jnp.zeros((1, BR), F32)
            positive = jnp.zeros((1, BR), F32)
            want = column[pl.ds(b, 1), :]
            for k in range(PAIRS_REP):
                logits = dot(partners[need[b * PAIRS_REP + k]], q, 1, 1) / logit_sharpness
                hit = iota((BR, BR), 0) + k * BR == want
                w = jnp.where(hit, 0.0, jnp.exp(logits - 1.0 / logit_sharpness))
                weights[b, k * BR : (k + 1) * BR, :] = w.astype(BF)
                total += jnp.sum(w, axis=0, keepdims=True)
                positive += jnp.sum(jnp.where(hit, logits, 0.0), axis=0, keepdims=True)
            stats[pl.ds(b, 1), :] = total
            stats[pl.ds(blocks + b, 1), :] = positive
        return carry

    lax.fori_loop(0, blocks // 4, body, 0)


def mix_kernel(need, column, weights, partners, pulled, partner):
    blocks = weights.shape[0]

    def body(i, carry):
        for j in range(4):
            b = i * 4 + j
            w = weights[b]
            hit = hot(iota(w.shape, 0) == column[pl.ds(b, 1), :])
            pair = [partners[need[b * PAIRS_REP + k]] for k in range(PAIRS_REP)]
            both = dot(jnp.concatenate([w, hit], axis=1), jnp.concatenate(pair, axis=0), 0, 0)
            at = pl.ds(pl.multiple_of(b * BR, BR), BR)
            pulled[at, :] = both[:BR, :].astype(BF)
            partner[at, :] = both[BR:, :].astype(BF)
        return carry

    lax.fori_loop(0, blocks // 4, body, 0)


def pick_rows(out, rows, ids):
    step = 256
    for h in range(out.shape[0] // step):
        pick = hot(iota((step, rows.shape[0]), 1) == ids[h * step : (h + 1) * step, :])
        out[h * step : (h + 1) * step, :] = dot(pick, rows[...]).astype(BF)


def shares_kernel(factor, s0, s1, s2, s3, pulled, partner, slots, share, out):
    blocks = s0.shape[0] // 2
    stats = (s0[...] + s3[...]) + (s1[...] + s2[...])
    rest, matching = stats[:blocks, :], stats[blocks:, :]
    total = rest + jnp.exp(matching - 1.0 / logit_sharpness)
    scale = jnp.concatenate([factor / total, factor * (rest / total)], axis=0)
    scale = jnp.concatenate([scale] * (BR // (2 * blocks)), axis=0).T
    for b in range(blocks):
        at = slice(b * BR, (b + 1) * BR)
        grad = pulled[at, :].astype(F32) * scale[:, b : b + 1]
        grad -= partner[at, :].astype(F32) * scale[:, blocks + b : blocks + b + 1]
        share[at, :] = grad.astype(BF)
    pick_rows(out, share, column_of(slots[...]))


def pick_kernel(share, slots, out):
    pick_rows(out, share, column_of(slots[...]))


def chip_kernel(own, beside, place, total, pick):
    total[...] = own[...].astype(F32) + beside[...].astype(F32)
    pick[...] = hot(iota(pick.shape, 1) == column_of(place[...]))


def back_kernel(chip, across, pick, back):
    total = chip[...] + across[...].astype(F32)
    back[...] = dot(pick[...], total.astype(BF)).astype(BF)


def unit_grad_kernel(got, place, unit, out, kept, sem):
    fetch = pltpu.make_async_copy(unit, kept, sem)
    fetch.start()
    n = out.shape[0]
    grad = dot(hot(iota((n, got.shape[0]), 1) == column_of(place[:8, :])), got[...])
    fetch.wait()
    rows = kept[...]
    radial = jnp.sum(rows * grad, axis=1, keepdims=True)
    out[...] = ((grad - rows * radial) / float_column_of(place[8:, :])).astype(BF)


def head_begun_kernel(mine, grad, out):
    step = 256
    for i in range(out.shape[0] // step):
        at = slice(i * step, (i + 1) * step)
        out[at, :] = dot(mine[at, :], grad[...])


def head_grad_kernel(begun, theirs, partner, out):
    step = 256
    for i in range(out.shape[0] // step):
        at = slice(i * step, (i + 1) * step)
        out[at, :] = (begun[at, :] + dot(theirs[at, :], partner[...])).astype(BF)


def sum_kernel(parts, out):
    out[...] = jnp.sum(parts[...].astype(F32), axis=0)


def swap(x, axes=("core",)):
    size = 2 ** len(axes)
    return lax.ppermute(x, axes, [(i, size - 1 - i) for i in range(size)])


def exchange(x, axes):
    return lax.all_to_all(x, axes, 0, 0, tiled=True)


def shards(features, head_weight, slot_of_image, candidates, positives):
    sizes = {axis: lax.axis_size(axis) for axis in AXES}
    dp = sizes["z"] * sizes["x"] * 2
    slab = lax.axis_index("yhi")
    me = (lax.axis_index("z") * sizes["x"] + lax.axis_index("x")) * 2
    me = me + (lax.axis_index("ylo") ^ slab)
    core = lax.axis_index("core")
    member = core * 2 + slab
    home = core == (me & 1)
    n, width = features.shape
    e = head_weight.shape[1]
    devices = dp * REPS
    owner_slots = n * REPS
    blocks = owner_slots // BR
    cap = 2 * n // devices
    count = devices * cap
    factor = objective_factor / (logit_sharpness * math.sqrt(n * devices))
    vmem = pl.BlockSpec(memory_space=pltpu.VMEM)
    smem = pl.BlockSpec(memory_space=pltpu.SMEM)
    far_away = pl.BlockSpec(memory_space=pl.ANY)

    def call(kernel, name, shapes, args, **more):
        return pl.pallas_call(
            kernel, out_shape=shapes, compiler_params=params(), name=name, **more
        )(*args)

    send, unit, place = call(
        lambda *r: project_kernel(owner_slots, sizes, cap, *r),
        "project",
        (sds((count, e + BR), BF), pltpu.HBM((n, e), F32), pltpu.HBM((16, n), F32)),
        (
            slot_of_image.reshape(1, n),
            pltpu.with_memory_space_constraint(features, pltpu.HBM),
            pltpu.with_memory_space_constraint(head_weight, pltpu.HBM),
        ),
        in_specs=[vmem, far_away, far_away],
        out_specs=(vmem, far_away, vmem),
        scratch_shapes=[
            pltpu.VMEM((n, width), BF),
            pltpu.VMEM((width, e), BF),
            pltpu.VMEM((n, e), F32),
            pltpu.SemaphoreType.DMA((9,)),
        ],
    )
    send, own_positives = lax.optimization_barrier((send, positives.reshape(4, e)))
    got = exchange(send.reshape(devices, cap, e + BR), DISPATCH).reshape(count, e + BR)
    packed, back_place = call(
        compact_kernel, "compact", (sds((n + 16, e), BF), sds((8, count), F32)), (got, own_positives)
    )
    beside = swap(packed)
    across = swap(packed, ("yhi", "ylo"))

    whole = sds((owner_slots, e), BF)
    ids_shape = sds((8, n), F32)
    partial, slots, other_positives = call(
        near_kernel,
        "near",
        (whole, sds((2, 8, n), F32), sds((blocks, BR), I32)),
        (packed, beside),
        cost_estimate=cost(4),
    )
    partial, late_features, late_candidates, slab, me = lax.optimization_barrier(
        (partial, features, candidates, slab, me)
    )
    mine, other = call(
        lambda *r: stripes_kernel(sizes, *r),
        "stripes",
        (sds((width // 2, n), BF),) * 2,
        (core.reshape(1), late_features),
        in_specs=[smem, vmem],
    )
    theirs = swap(other)
    table = late_candidates.reshape(dp, blocks, REPS, PAIRS_REP)
    table = lax.dynamic_index_in_dim(table, member, axis=2, keepdims=False)
    table = table.reshape(dp, blocks * PAIRS_REP)
    owner = table // blocks
    numbers = jnp.arange(dp, dtype=I32)
    wanted = jnp.sum(jnp.where(owner == me, table - owner * blocks, 0), axis=1)

    def fetch_place(number):
        column = number // 2
        z = column // sizes["x"]
        x = column - z * sizes["x"]
        return position(FETCH, sizes, dict(z=z, x=x, ylo=(number & 1) ^ slab))

    serve = jnp.sum(
        jnp.where(fetch_place(numbers)[None, :] == numbers[:, None], wanted[None, :], 0), axis=1
    )
    need = fetch_place(lax.dynamic_index_in_dim(owner, me, axis=0, keepdims=False))
    keys = serve * dp + numbers
    place_of = jnp.sum((keys[None, :] < keys[:, None]).astype(I32), axis=1)
    order = jnp.sum(jnp.where(place_of[None, :] == numbers[:, None], numbers[None, :], 0), axis=1)
    bounds = 2 * jnp.arange(blocks // 2 + 1, dtype=I32)
    ready = jnp.sum((serve[None, :] < bounds[:, None]).astype(I32), axis=1)

    column = jnp.where(home, positives.reshape(blocks, BR), other_positives)
    column = column - member * (PAIRS_REP * BR)
    partial, across, column, mine, theirs, serve, order, ready, need = lax.optimization_barrier(
        (partial, across, column, mine, theirs, serve, order, ready, need)
    )
    corner = swap(across)
    partial, slots_across = call(middle_kernel, "middle", (whole, ids_shape), (partial, across))
    anchors, served, slots_corner = call(
        far_kernel,
        "far",
        (whole, sds((dp, BR, e), BF), ids_shape),
        (serve, order, ready, partial, corner),
        in_specs=[smem] * 3 + [vmem] * 2,
    )
    fetched = exchange(served, FETCH)
    weights, stats = call(
        scores_kernel,
        "scores",
        (
            sds((blocks, PAIRS_REP * BR, BR), BF),
            sds((2 * blocks, BR), F32),
        ),
        (need, column, anchors, fetched),
        in_specs=[smem] + [vmem] * 3,
    )
    spread = (stats, swap(stats), swap(stats, ("yhi", "ylo")), swap(stats, ("core", "yhi", "ylo")))
    pulled, partner = call(
        mix_kernel,
        "mix",
        (sds((owner_slots, e), BF),) * 2,
        (need, column, weights, fetched),
        in_specs=[smem] + [vmem] * 3,
    )
    share, for_corner = call(
        lambda *r: shares_kernel(factor, *r),
        "shares",
        (whole, sds((n, e), BF)),
        (*spread, pulled, partner, slots_corner),
    )

    def pick(name, rows, ids):
        return call(
            pick_kernel, name, sds((n, e), BF), (rows, ids), cost_estimate=cost(0.01)
        )

    for_across = pick("across", share, slots_across).astype(F32) + swap(for_corner).astype(F32)
    from_across = swap(for_across.astype(BF), ("yhi", "ylo"))
    own = pick("own", share, slots[0])
    from_beside = swap(pick("beside", share, slots[1]))
    both = (spread[0] + spread[3]) + (spread[1] + spread[2])
    rest, matching = both[:blocks], both[blocks:]
    total = rest + jnp.exp(matching - 1.0 / logit_sharpness)
    loss = (jnp.log(total) + 1.0 / logit_sharpness - matching).reshape(owner_slots)
    anchor_row_loss = jnp.where(home, loss, swap(loss, ("ylo",)))
    chip, back_pick = call(
        chip_kernel, "chip", (sds((n, e), F32), sds((count, n), BF)), (own, from_beside, back_place)
    )
    chip, back_pick, anchor_row_loss = lax.optimization_barrier((chip, back_pick, anchor_row_loss))
    back = call(
        back_kernel,
        "back",
        sds((count, e), BF),
        (chip, from_across, back_pick),
    )
    returned = exchange(back.reshape(devices, cap, e), DISPATCH).reshape(count, e)

    grad = call(
        unit_grad_kernel,
        "unit_grad",
        sds((n, e), BF),
        (returned, place, pltpu.with_memory_space_constraint(unit, pltpu.HBM)),
        in_specs=[vmem, vmem, far_away],
        scratch_shapes=[pltpu.VMEM((n, e), F32), pltpu.SemaphoreType.DMA],
    )
    begun = call(head_begun_kernel, "head_begun", sds((width // 2, e), F32), (mine, grad))
    partial = call(
        head_grad_kernel,
        "head_grad",
        sds((width // 2, e), BF),
        (begun, theirs, swap(grad)),
    )
    parts = exchange(partial.reshape(devices // 2, width // devices, e), REDUCE)
    weight_grad = call(sum_kernel, "add", sds((width // devices, e), F32), (parts,))
    return (anchor_row_loss, weight_grad)


def solution(mesh):
    dp, rep = mesh.devices.shape
    z = x = math.isqrt(dp // 2)
    split = jax.sharding.Mesh(mesh.devices.reshape(z, x, 2, rep // 2, 2), AXES)
    owners = ("z", "x", "core")
    placed = (P(AXES, None), P(), P(AXES), P(), P(owners))
    return jax.shard_map(
        shards,
        mesh=split,
        in_specs=placed,
        out_specs=(P(owners), P(AXES, None)),
        check_vma=False,
    )
```
